256 devices in a mesh: seq: 32 (over y, z), store: 8 (over x, core).
Axes of the slice: x: 4, y: 4, z: 8, core: 2. Of those that a mesh axis runs over, the one named last changes fastest.
Arguments:
- hidden: bfloat16 [24576, 4096], P('seq', 'store'), may hold values from -6 to 6
- nbr_shard: int32 [384, 2], P('seq'), may hold values from 0 to 31, all different within a row; in each aligned block of 12 rows (0 to 11, 12 to 23, ...) at most 2 rows name the same one
- nbr_block: int32 [384, 2], P('seq'), may hold values from 0 to 7
- seq_lengths: int32 [24], replicated, may hold values from 1 to 128, 384 in all
- kv_store: bfloat16 [256, 128, 2, 4096], P('seq', None, None, 'store'), may hold values from -250 to 250
- w_query: bfloat16 [4096, 4096], P(None, 'store'), may hold values from -0.09375 to 0.09375
- w_out: bfloat16 [4096, 4096], P('store'), may hold values from -0.125 to 0.125
Outputs:
- output: bfloat16 [24576, 4096], P('seq', 'store')
The draws below stay inside these ranges and needn't reach their ends.
Inputs may be any that keep to these rules, and one draw needn't show every extreme that they name: `nbr_shard`: among the spans of one device, no store shard is named by more than 2 neighbour entries; the 2 neighbours of a span lie on different shards. `seq_lengths`: the lengths sum to 384; the longest is 128.
All inputs are finite; a program needn't handle non-finite values.
Results may differ from the reference program's by a relative error of at most 0.025.
Values may be sent and summed in bfloat16 or wider, within the bound.
No kernel may reach another device: no remote copies, remote signals or barrier semaphores. Data moves between devices by JAX's collectives and lax.ppermute only.
A program may use at most 128 MiB of HBM per device.

```python
import math
import jax
import jax.numpy as jnp
import numpy as np
from jax import lax

HEAD_DIM = 128
D = 4096
SPAN = 64
NBR = 2
NBR_LEN = 128
CH_DEV = 12
SHARDS = 32
SPANS = 384
TOKENS = 24576
CAP = 2
BLK_DEV = 8
BLOCKS = 256
SEQS = 24
SEQ_MOST = 128
N_STORE = 8


def draw_kv_store(key, part):
    key = jax.random.fold_in(key, 11)
    fifth_key = jax.random.fold_in(key, 4)
    full_shape = (BLOCKS, NBR_LEN, 2, D)
    component = lax.broadcasted_iota(jnp.int32, full_shape, 2)
    factor = jnp.where(component == 0, 1.5, 3.0).astype(jnp.float32)
    base = jax.random.normal(fifth_key, full_shape, jnp.float32)
    drawn = jnp.clip(base, -6.0, 6.0) * factor
    return drawn.astype(jnp.bfloat16)


def plant(values, own_key, least, high):
    extent = values.shape
    place = [jax.random.randint(jax.random.fold_in(own_key, axis), (), 0, extent[axis]) for axis in range(len(extent))]
    values = values.at[tuple(place)].set(least)
    longest = extent.index(max(extent))
    place[longest] = (place[longest] + 1) % extent[longest]
    return values.at[tuple(place)].set(high)


def raised(entries, own_key, source, target, parts, factor):
    def block_of(axis_at):
        return (jnp.arange(entries.shape[axis_at]) // (entries.shape[axis_at] // parts)).reshape((-1,) + (1,) * (entries.ndim - 1 - axis_at))

    one_side = jax.random.permutation(own_key, parts)[block_of(target)]
    other_side = (block_of(target) + parts // 2) % parts
    return jnp.where((block_of(source) == one_side) | (block_of(source) == other_side), factor * entries, entries)


def block_levels(stream_key, dims, cuts, low, high):
    def one(dim, parts):
        draws = jax.random.uniform(jax.random.fold_in(jax.random.fold_in(stream_key, 6), dim), (parts,), jnp.float32, low / len(cuts), high / len(cuts))
        return jnp.repeat(jnp.exp(draws), dims[dim] // parts).reshape((-1,) + (1,) * (len(dims) - dim - 1))

    level = one(*cuts[0])
    for cut in cuts[1:]:
        level = level * one(*cut)
    return level


def split_up(number_of, total, most, skew):
    portions = [(1 << 20) // math.isqrt(standing ** skew) + 1 for standing in range(2, number_of + 1)]
    spare, holding = total - most - (number_of - 1), [1] * (number_of - 1)
    while spare > 0:
        movable = [i for i in range(number_of - 1) if holding[i] < most]
        mass, budget = sum([portions[i] for i in movable]), spare
        for i in movable:
            addition = min(most - holding[i], max(1, budget * portions[i] // mass), spare)
            holding[i] = holding[i] + addition
            spare = spare - addition
    return np.array([most] + holding)


def uneven(rng, amount, total, limit, lean):
    if amount == 2:
        one = jax.random.randint(rng, (), max(1, total - limit), min(limit, total - 1) + 1)
        return jnp.stack([one, total - one])
    tallies = jnp.asarray(split_up(amount, total, limit, lean), jnp.int32)
    couples = (amount - 1) // 2
    source_of, receiver = tallies[1:1 + 2 * couples:2], tallies[2:2 + 2 * couples:2]
    margin = jnp.minimum(source_of - 1, limit - receiver)
    moved = jax.random.randint(jax.random.fold_in(rng, 1), (couples,), 0, 1 << 20) % (margin + 1)
    tallies = tallies.at[1:1 + 2 * couples:2].set(source_of - moved).at[2:2 + 2 * couples:2].set(receiver + moved)
    return tallies[jax.random.permutation(jax.random.fold_in(rng, 2), amount)]


def routed_block(key, own, number, rows, amount, top, bound, lean):
    sequence = jax.random.permutation(key, amount)
    packed, ordinary = load_shares(amount, rows * top, bound, lean, True), load_shares(amount, rows * top, bound, lean, False)
    places = jnp.arange(amount)

    def named(sizes, rotation):
        used = int((sizes > 0).sum())
        fixed = max(1, used // 4)
        passed = fixed + (places - fixed + rotation * (used - fixed)) % max(1, amount - fixed)
        return jnp.zeros((amount,), jnp.int32).at[sequence[jnp.where(places < fixed, places, passed)]].set(jnp.asarray(sizes, jnp.int32))

    sizes = jnp.where(number % 4 == 0, named(packed, number // 4), named(ordinary, number - number // 4 - 1))
    mixed = jax.random.permutation(jax.random.fold_in(own, 3), amount)
    giver, sink = mixed[0:amount // 2 * 2:2], mixed[1:amount // 2 * 2:2]
    slack = jnp.minimum(sizes[giver] - 1, bound - sizes[sink]) // 2
    slack = jnp.where((giver == sequence[0]) | (sink == sequence[0]) | (sizes[sink] == 0), 0, jnp.maximum(slack, 0))
    passed = jax.random.randint(jax.random.fold_in(own, 4), (amount // 2,), 0, 1 << 20) % (slack + 1)
    sizes = sizes.at[giver].add(-passed).at[sink].add(passed)
    items = jnp.searchsorted(jnp.cumsum(sizes), jnp.arange(rows * top), side="right").astype(jnp.int32)
    table = items.reshape(top, rows).T
    table = table[jax.random.permutation(jax.random.fold_in(own, 1), rows)]
    rotation = jax.random.randint(jax.random.fold_in(own, 2), (rows, 1), 0, top)
    return jnp.take_along_axis(table, (jnp.arange(top)[None, :] + rotation) % top, axis=1)


def load_shares(amount, total, limit, lean, full):
    weights = [(1 << 20) // math.isqrt(standing ** lean) + 1 for standing in range(1, amount + 1)]
    largest = limit if full else min(limit, max(-(-total // amount), total * weights[0] // sum(weights)))
    least = 1 if total - largest >= amount - 1 else 0
    given, rest = [largest] + [least] * (amount - 1), total - largest - least * (amount - 1)
    while rest > 0:
        candidates = [i for i in range(1, amount) if given[i] < largest] or [i for i in range(1, amount) if given[i] < limit]
        mass, remaining = sum([weights[i] for i in candidates]), rest
        for i in candidates:
            more = min(limit - given[i], max(1, remaining * weights[i] // mass), rest)
            given[i] = given[i] + more
            rest = rest - more
    return np.array(given)


def noise(key, shape, scale, most, cuts=(), kind=jnp.bfloat16):
    gain = block_levels(key, shape, cuts, -0.22, 0.18) if cuts else 1.0
    result = jax.random.normal(key, shape, jnp.float32) * scale * gain
    return jnp.minimum(jnp.maximum(result, -most), most).astype(kind)


def noise_with(rng, dims, scale, most, cuts, heavy, kind=jnp.bfloat16):
    array = scale * jax.random.normal(rng, dims, jnp.float32)
    if cuts:
        array = array * block_levels(rng, dims, cuts, -0.22, 0.18)
    return jnp.clip(raised(array, jax.random.fold_in(rng, 3), *heavy), -most, most).astype(kind)


def setup_inputs(seed: int = 0) -> dict:
    arg_keys = jax.random.split(jax.random.key(seed), 8)
    hidden = noise(arg_keys[0], (TOKENS, D), 1.0, 6.0, ((0, 32), (1, 8)))
    nbr_shard_keys = jax.random.split(jax.random.fold_in(arg_keys[1], 1), SPANS // CH_DEV)
    nbr_shard_turns = jax.random.permutation(jax.random.fold_in(arg_keys[1], 3), SPANS // CH_DEV)
    nbr_shard = jax.vmap(lambda own, number: routed_block(jax.random.fold_in(arg_keys[1], 2), own, number, CH_DEV, SHARDS, NBR, CAP, 2))(nbr_shard_keys, nbr_shard_turns).reshape((SPANS, NBR))
    nbr_block = plant(jax.random.randint(arg_keys[2], (SPANS, NBR), 0, BLK_DEV), jax.random.fold_in(arg_keys[2], 1), 0, BLK_DEV - 1).astype(jnp.int32)
    seq_lengths = uneven(arg_keys[3], SEQS, SPANS, SEQ_MOST, 2).astype(jnp.int32)
    kv_store = draw_kv_store(jax.random.fold_in(arg_keys[7], 71), 0)
    w_query = noise(arg_keys[5], (D, D), D ** -0.5, 0.09375, ((1, 8),))
    w_out = noise_with(arg_keys[6], (D, D), D ** -0.5, 0.125, ((0, 8),), (0, 1, 8, 2.0))
    return dict(hidden=hidden, nbr_shard=nbr_shard, nbr_block=nbr_block, seq_lengths=seq_lengths, kv_store=kv_store, w_query=w_query, w_out=w_out)


def partial_attention(queries, blocks):
    width = queries.shape[-1]
    head_count = width // HEAD_DIM
    query_heads = queries.reshape(queries.shape[:-1] + (head_count, HEAD_DIM)).astype(jnp.float32)
    key_heads = blocks[..., :width].reshape(blocks.shape[:-1] + (head_count, HEAD_DIM)).astype(jnp.float32)
    value_heads = blocks[..., width:].reshape(blocks.shape[:-1] + (head_count, HEAD_DIM)).astype(jnp.float32)
    scores = jnp.einsum('...qhd,...khd->...hqk', query_heads, key_heads) * HEAD_DIM ** (-0.5)
    peaks = lax.optimization_barrier(jnp.max(scores, axis=-1))
    weights = jnp.exp(scores - peaks[..., None])
    totals = lax.optimization_barrier(jnp.sum(weights, axis=-1))
    rounded = weights.astype(jnp.bfloat16)
    mixed = jnp.einsum('...hqk,...khd->...hqd', rounded.astype(jnp.float32), value_heads).astype(jnp.bfloat16)
    return (mixed, peaks, totals)

def combine(mixed, peaks, totals, axis_pos):
    best = lax.optimization_barrier(jnp.max(peaks, axis=axis_pos, keepdims=True))
    factors = jnp.exp(peaks - best)
    numer = lax.optimization_barrier(jnp.sum(factors[..., None] * mixed.astype(jnp.float32), axis=axis_pos))
    denom = lax.optimization_barrier(jnp.sum(factors * totals, axis=axis_pos))
    return numer / denom[..., None]

def reference(hidden, nbr_shard, nbr_block, seq_lengths, kv_store, w_query, w_out):
    values = hidden.astype(jnp.float32)
    normed = (values * lax.rsqrt(lax.optimization_barrier(jnp.mean(values * values, axis=-1, keepdims=True)) + 1e-05)).astype(jnp.bfloat16)
    queries = jnp.dot(normed, w_query, preferred_element_type=jnp.float32).astype(jnp.bfloat16)
    attending = jnp.concatenate([queries[SPAN - 1:], jnp.zeros((SPAN - 1, D), jnp.bfloat16)], axis=0)
    attending = attending.reshape(SPANS, SPAN, D)
    block_ids = (nbr_shard * BLK_DEV + nbr_block).astype(jnp.int32)
    store = kv_store.reshape(BLOCKS, NBR_LEN, 2 * D)

    def one_span(pair):
        span_queries, chosen = pair
        blocks = store[chosen]
        spread = jnp.broadcast_to(span_queries, (NBR,) + span_queries.shape)
        mixed, peaks, totals = partial_attention(spread, blocks)
        merged = combine(mixed, peaks, totals, 0)
        return jnp.transpose(merged, (1, 0, 2)).reshape(SPAN, D)
    attended = lax.map(one_span, (attending, block_ids))
    span_index = jnp.arange(SPANS, dtype=jnp.int32)
    seq_ends = jnp.cumsum(seq_lengths).astype(jnp.int32)
    boundary = jnp.any(seq_ends[None, :] == span_index[:, None] + 1, axis=1)
    first_row = jnp.arange(SPAN, dtype=jnp.int32) == 0
    keep_mask = first_row[None, :] | jnp.logical_not(boundary)[:, None]
    masked = jnp.where(keep_mask[..., None], attended, 0.0).astype(jnp.bfloat16).reshape(TOKENS, D)
    att_rows = jnp.concatenate([jnp.zeros((SPAN - 1, D), jnp.bfloat16), masked[:TOKENS - (SPAN - 1)]], axis=0)
    group_width = D // N_STORE
    projected = jnp.zeros((TOKENS, D), jnp.float32)
    for group in range(N_STORE):
        lower = group * group_width
        upper = lower + group_width
        partial_term = jnp.dot(att_rows[:, lower:upper], w_out[lower:upper], preferred_element_type=jnp.float32).astype(jnp.bfloat16)
        partial_term = lax.optimization_barrier(partial_term)
        projected = projected + partial_term.astype(jnp.float32)
    return (values + projected).astype(jnp.bfloat16)
```

```python
import functools
import jax
import jax.numpy as jnp
from jax import lax
from jax.experimental import pallas as pl
from jax.experimental.pallas import tpu as pltpu
from jax.sharding import Mesh, PartitionSpec as P

HEAD_DIM = 128
SPAN = 64
NBR = 2
NBR_LEN = 128
HEADS = 4
WIDTH = HEADS * HEAD_DIM
BLK_DEV = 8
NY, NZ, NX, NC = 4, 8, 4, 2
SPANS_DEV = 12
CHUNKS = ((6, 12), (0, 6))
STAT_ROWS = 16
FAR = -1e30
LANES = 128


def ring(array, axis, size, by):
    return lax.ppermute(array, axis, [(i, (i + by) % size) for i in range(size)])


def lane_rows(rows):
    return -(-rows // LANES) * LANES


def load_state(state_ref, out_ref, stat_ref, first, rows):
    out_ref[pl.ds(first, rows), :] = state_ref[pl.ds(0, rows), :]
    wide = lane_rows(rows)
    packed = state_ref[pl.ds(rows, STAT_ROWS), pl.ds(0, wide)].astype(jnp.float32)
    parts = jnp.concatenate([packed, jnp.zeros((LANES - STAT_ROWS, wide), jnp.float32)], axis=0).T
    total = parts + pltpu.roll(parts, LANES - HEADS, 1) + pltpu.roll(parts, LANES - 2 * HEADS, 1)
    stat_ref[pl.ds(first, rows), :] = total[:rows]


def store_stats(stat_ref, out_ref, rows):
    wide = lane_rows(rows)
    lse = stat_ref[pl.ds(0, rows), :]
    if wide != rows:
        lse = jnp.concatenate([lse, jnp.zeros((wide - rows, LANES), jnp.float32)], axis=0)
    high = lse.astype(jnp.bfloat16).astype(jnp.float32)
    rest = lse - high
    middle = rest.astype(jnp.bfloat16).astype(jnp.float32)
    low = rest - middle
    lane = lax.broadcasted_iota(jnp.int32, lse.shape, 1)
    packed = jnp.where(
        lane < HEADS,
        high,
        jnp.where(lane < 2 * HEADS, pltpu.roll(middle, HEADS, 1), pltpu.roll(low, 2 * HEADS, 1)),
    )
    packed = jnp.where(lane < 3 * HEADS, packed, 0.0).T
    out_ref[pl.ds(rows, STAT_ROWS), pl.ds(0, wide)] = packed[:STAT_ROWS].astype(jnp.bfloat16)
    if wide < WIDTH:
        out_ref[pl.ds(rows, STAT_ROWS), pl.ds(wide, WIDTH - wide)] = jnp.zeros(
            (STAT_ROWS, WIDTH - wide), jnp.bfloat16
        )


def merge(old, old_lse, new, new_lse):
    best = jnp.maximum(old_lse, new_lse)
    old_part = jnp.exp(old_lse - best)
    new_part = jnp.exp(new_lse - best)
    both = old_part + new_part
    scale = 1.0 / both
    return old * (old_part * scale) + new * (new_part * scale), best + jnp.log(both)


def attend(q_ref, q_row, block, out_ref, stat_ref, row):
    stats = stat_ref[pl.ds(row, SPAN), :]
    lane = lax.broadcasted_iota(jnp.int32, (SPAN, LANES), 1)
    for head in range(HEADS):
        cols = slice(head * HEAD_DIM, (head + 1) * HEAD_DIM)
        queries = q_ref[pl.ds(q_row, SPAN), cols]
        keys = block[:, cols]
        values = block[:, WIDTH + head * HEAD_DIM : WIDTH + (head + 1) * HEAD_DIM]
        scores = (
            lax.dot_general(
                queries, keys, (((1,), (1,)), ((), ())), preferred_element_type=jnp.float32
            )
            * HEAD_DIM**-0.5
        )
        peaks = jnp.max(scores, axis=-1, keepdims=True)
        weights = jnp.exp(scores - peaks)
        totals = jnp.sum(weights, axis=-1, keepdims=True)
        mixed = jnp.dot(weights.astype(jnp.bfloat16), values, preferred_element_type=jnp.float32)
        old = out_ref[pl.ds(row, SPAN), cols].astype(jnp.float32)
        out, lse = merge(
            old, stats[:, head : head + 1], mixed / totals, peaks + jnp.log(totals)
        )
        out_ref[pl.ds(row, SPAN), cols] = out.astype(jnp.bfloat16)
        stats = jnp.where(lane == head, lse, stats)
    stat_ref[pl.ds(row, SPAN), :] = stats


def kv_copy(kv_ref, buf_ref, sems, block, slot):
    return pltpu.make_async_copy(kv_ref.at[block], buf_ref.at[slot], sems.at[slot])


def start_blocks(ids_ref, base, spans, kv_ref, buf_ref, sems, slot0):
    def one(i, carry):
        block = ids_ref[base + i]

        @pl.when(block >= 0)
        def _():
            kv_copy(kv_ref, buf_ref, sems, block, slot0 + i).start()

        return carry

    lax.fori_loop(0, spans * NBR, one, 0)


def attend_blocks(ids_ref, base, spans, q_ref, kv_ref, buf_ref, sems, slot0, out_ref, stat_ref):
    def one(i, carry):
        block = ids_ref[base + i]

        @pl.when(block >= 0)
        def _():
            kv_copy(kv_ref, buf_ref, sems, block, slot0 + i).wait()
            row = pl.multiple_of((i // NBR) * SPAN, SPAN)
            attend(q_ref, row, buf_ref.at[slot0 + i], out_ref, stat_ref, row)

        return carry

    lax.fori_loop(0, spans * NBR, one, 0)


def relay_kernel(ways, *refs):
    ids_ref, kv_ref = refs[:2]
    refs = refs[2:]
    plan = []
    for base, spans, begin, held in ways:
        q_ref, refs = refs[0], refs[1:]
        state_ref = None
        if held:
            state_ref, refs = refs[0], refs[1:]
        plan.append([base, spans, begin, held, q_ref, state_ref])
    outs, refs = refs[: len(ways)], refs[len(ways) :]
    buf_ref, sems = refs[:2]
    stats = refs[2:]
    slot0 = 0
    for base, spans, *_ in plan:
        start_blocks(ids_ref, base, spans, kv_ref, buf_ref, sems, slot0)
        slot0 += spans * NBR
    slot0 = 0
    for (base, spans, begin, held, q_ref, state_ref), out_ref, stat_ref in zip(plan, outs, stats):
        rows = spans * SPAN
        if held != spans:
            out_ref[pl.ds(0, rows), :] = jnp.zeros((rows, WIDTH), jnp.bfloat16)
            stat_ref[...] = jnp.full((rows, LANES), FAR, jnp.float32)
        if held:
            load_state(state_ref, out_ref, stat_ref, begin * SPAN, held * SPAN)
        attend_blocks(
            ids_ref, base, spans, q_ref, kv_ref, buf_ref, sems, slot0, out_ref, stat_ref
        )
        store_stats(stat_ref, out_ref, rows)
        slot0 += spans * NBR


def final_kernel(base, spans, mask_base, ids_ref, edge_ref, kv_ref, q_ref, fwd_ref, bwd_ref, out_ref, buf_ref, sems, stat_ref, other_ref, other_stat):
    rows = spans * SPAN
    start_blocks(ids_ref, base, spans, kv_ref, buf_ref, sems, 0)
    load_state(fwd_ref, out_ref, stat_ref, 0, rows)
    load_state(bwd_ref, other_ref, other_stat, 0, rows)
    lane = lax.broadcasted_iota(jnp.int32, (rows, LANES), 1)
    stats = stat_ref[...]
    for head in range(HEADS):
        cols = slice(head * HEAD_DIM, (head + 1) * HEAD_DIM)
        out, lse = merge(
            out_ref[:, cols].astype(jnp.float32),
            stat_ref[:, head : head + 1],
            other_ref[:, cols].astype(jnp.float32),
            other_stat[:, head : head + 1],
        )
        out_ref[:, cols] = out.astype(jnp.bfloat16)
        stats = jnp.where(lane == head, lse, stats)
    stat_ref[...] = stats
    attend_blocks(ids_ref, base, spans, q_ref, kv_ref, buf_ref, sems, 0, out_ref, stat_ref)

    def cut(i, carry):
        @pl.when(edge_ref[mask_base + i] > 0)
        def _():
            at = pl.ds(pl.multiple_of(i * SPAN, SPAN), SPAN)
            kept = lax.broadcasted_iota(jnp.int32, (SPAN, WIDTH), 0) == 0
            out_ref[at, :] = jnp.where(kept, out_ref[at, :], jnp.zeros((SPAN, WIDTH), jnp.bfloat16))

        return carry

    lax.fori_loop(0, spans, cut, 0)


SMEM = pl.BlockSpec(memory_space=pltpu.SMEM)
VMEM = pl.BlockSpec(memory_space=pltpu.VMEM)
ANY = pl.BlockSpec(memory_space=pl.ANY)


def cost(pairs, rows):
    return pl.CostEstimate(
        flops=pairs * HEADS * 4 * SPAN * HEAD_DIM * NBR_LEN,
        bytes_accessed=pairs * NBR_LEN * 4 * WIDTH + rows * WIDTH * 8,
        transcendentals=pairs * HEADS * SPAN * NBR_LEN,
    )


def relay(ids, kv, ways):
    specs = [w[:4] for w in ways]
    operands = [ids, kv]
    for base, spans, begin, held, queries, state in ways:
        operands.append(queries)
        if held:
            operands.append(state)
    total = sum(spans for _, spans, _, _ in specs)
    return pl.pallas_call(
        functools.partial(relay_kernel, specs),
        out_shape=[
            jax.ShapeDtypeStruct((spans * SPAN + STAT_ROWS, WIDTH), jnp.bfloat16)
            for _, spans, _, _ in specs
        ],
        in_specs=[SMEM, ANY] + [VMEM] * (len(operands) - 2),
        out_specs=[VMEM] * len(specs),
        scratch_shapes=[
            pltpu.VMEM((total * NBR, NBR_LEN, 2 * WIDTH), jnp.bfloat16),
            pltpu.SemaphoreType.DMA((total * NBR,)),
        ]
        + [pltpu.VMEM((spans * SPAN, LANES), jnp.float32) for _, spans, _, _ in specs],
        compiler_params=pltpu.CompilerParams(vmem_limit_bytes=24 * 1024 * 1024),
        cost_estimate=cost(6, total * SPAN),
    )(*operands)


def finish(ids, edges, kv, base, spans, mask_base, queries, fwd, bwd):
    rows = spans * SPAN
    return pl.pallas_call(
        functools.partial(final_kernel, base, spans, mask_base),
        out_shape=jax.ShapeDtypeStruct((rows, WIDTH), jnp.bfloat16),
        in_specs=[SMEM, SMEM, ANY] + [VMEM] * 3,
        out_specs=VMEM,
        scratch_shapes=[
            pltpu.VMEM((spans * NBR, NBR_LEN, 2 * WIDTH), jnp.bfloat16),
            pltpu.SemaphoreType.DMA((spans * NBR,)),
            pltpu.VMEM((rows, LANES), jnp.float32),
            pltpu.VMEM((rows, WIDTH), jnp.bfloat16),
            pltpu.VMEM((rows, LANES), jnp.float32),
        ],
        compiler_params=pltpu.CompilerParams(vmem_limit_bytes=24 * 1024 * 1024),
        cost_estimate=cost(3, rows),
    )(ids, edges, kv, queries, fwd, bwd)


def on_device(hidden, nbr_shard, nbr_block, seq_lengths, kv_store, w_query, w_out):
    rows = hidden.shape[0]
    my_y, my_z = lax.axis_index("y"), lax.axis_index("z")
    seq_at = my_y * NZ + my_z
    order = [(i, i - 1) for i in range(1, NY * NZ)]
    edge = lax.ppermute(hidden[: SPAN - 1], ("y", "z"), order)
    attending = jnp.concatenate([hidden[SPAN - 1 :], edge], axis=0)

    wanted = nbr_shard * BLK_DEV + nbr_block
    wanted = lax.all_gather(wanted, "z")
    shard, block = wanted // BLK_DEV, wanted % BLK_DEV
    local = jnp.where(
        shard % NZ == my_z, ((shard // NZ - my_y) % NY) * BLK_DEV + block, -1
    ).astype(jnp.int32)
    local = local[(my_z + jnp.arange(NZ)) % NZ].reshape(-1)
    span_index = seq_at * SPANS_DEV + jnp.arange(SPANS_DEV, dtype=jnp.int32)
    boundary = jnp.any(jnp.cumsum(seq_lengths)[None, :] == span_index[:, None] + 1, axis=1)
    boundary = boundary.astype(jnp.int32)

    own = kv_store.reshape(BLK_DEV, NBR_LEN, 2 * WIDTH)
    above = ring(own, "y", NY, -1)
    below = ring(own, "y", NY, 1)
    half = BLK_DEV // 2
    across = jnp.concatenate(
        [ring(above[:half], "y", NY, -1), ring(below[half:], "y", NY, 1)], axis=0
    )
    kv = jnp.concatenate([own, above, across, below], axis=0)

    gathered, queries = [], []
    for first, last in CHUNKS:
        part = lax.all_gather(attending[first * SPAN : last * SPAN], ("x", "core"), axis=1, tiled=True)
        gathered.append(part)
        values = part.astype(jnp.float32)
        scale = lax.rsqrt(jnp.mean(values * values, axis=-1, keepdims=True) + 1e-05)
        product = jnp.dot(part, w_query, preferred_element_type=jnp.float32)
        queries.append((product * scale).astype(jnp.bfloat16))
    w_out, _ = lax.optimization_barrier((w_out, gathered[-1]))
    w_cols = lax.all_to_all(w_out, ("x", "core"), split_axis=1, concat_axis=0, tiled=True)

    outs = []
    for (first, last), mine in zip(CHUNKS, queries):
        spans = last - first
        cut = (spans // 2) * SPAN
        fwd, bwd = [mine], [mine]
        for _ in range(3):
            fwd.append(ring(fwd[-1], "z", NZ, 1))
            bwd.append(ring(bwd[-1], "z", NZ, -1))
        far_top = ring(fwd[3][:cut], "z", NZ, 1)
        far_low = ring(bwd[3][cut:], "z", NZ, -1)

        def base(distance, start=0):
            return ((distance % NZ) * SPANS_DEV + first + start) * NBR

        split = spans // 2
        top, low = relay(
            local,
            kv,
            [
                (base(4), split, 0, 0, far_top, None),
                (base(4, split), spans - split, 0, 0, far_low, None),
            ],
        )
        top, low = ring(top, "z", NZ, 1), ring(low, "z", NZ, -1)
        starts, helds = (0, split), (split, spans - split)
        for s in (3, 2, 1):
            top, low = relay(
                local,
                kv,
                [
                    (base(s), spans, starts[0], helds[0], bwd[s], top),
                    (base(-s), spans, starts[1], helds[1], fwd[s], low),
                ],
            )
            top, low = ring(top, "z", NZ, 1), ring(low, "z", NZ, -1)
            starts, helds = (0, 0), (spans, spans)
        attended = finish(local, boundary, kv, base(0), spans, first, mine, top, low)
        whole = lax.all_gather(attended, ("x", "core"), axis=1, tiled=True)
        projected = jnp.dot(whole, w_cols, preferred_element_type=jnp.float32)
        residual = attending[first * SPAN : last * SPAN].astype(jnp.float32)
        outs.append((residual + projected).astype(jnp.bfloat16))

    result = jnp.concatenate([o for _, o in sorted(zip([c[0] for c in CHUNKS], outs), key=lambda p: p[0])], axis=0)
    order = [(i, i + 1) for i in range(NY * NZ - 1)]
    head = lax.ppermute(result[rows - (SPAN - 1) :], ("y", "z"), order)
    head = jnp.where(seq_at == 0, hidden[: SPAN - 1], head)
    return jnp.concatenate([head, result[: rows - (SPAN - 1)]], axis=0)


def solution(mesh):
    fine = Mesh(mesh.devices.reshape(NY, NZ, NX, NC), ("y", "z", "x", "core"))
    seq, store = ("y", "z"), ("x", "core")
    return jax.shard_map(
        on_device,
        mesh=fine,
        in_specs=(
            P(seq, store),
            P(seq, None),
            P(seq, None),
            P(),
            P(seq, None, None, store),
            P(None, store),
            P(store, None),
        ),
        out_specs=P(seq, store),
        check_vma=False,
    )
```

```python
import functools
import jax
import jax.numpy as jnp
from jax import lax
from jax.experimental import pallas as pl
from jax.experimental.pallas import tpu as pltpu
from jax.sharding import Mesh, PartitionSpec as P

HEAD_DIM = 128
SPAN = 64
NBR = 2
NBR_LEN = 128
HEADS = 4
WIDTH = HEADS * HEAD_DIM
BLK_DEV = 8
NY, NZ, NX, NC = 4, 8, 4, 2
SEQ, STORE = ("y", "z"), ("x", "core")
SPANS_DEV = 12
CHUNKS = ((6, 12), (0, 6))
STAT_ROWS = 16
FAR = -1e30
KV_PARTS = 5
ROW_TILE = 128
LANES = 128


def ring(array, axis, size, by):
    return lax.ppermute(array, axis, [(i, (i + by) % size) for i in range(size)])


def lane_rows(rows):
    return -(-rows // LANES) * LANES


def load_state(state_ref, out_ref, stat_ref, first, rows):
    out_ref[pl.ds(first, rows), :] = state_ref[pl.ds(0, rows), :]
    wide = lane_rows(rows)
    packed = state_ref[pl.ds(rows, STAT_ROWS), pl.ds(0, wide)].astype(jnp.float32)
    parts = jnp.concatenate([packed, jnp.zeros((LANES - STAT_ROWS, wide), jnp.float32)], axis=0).T
    total = parts + pltpu.roll(parts, LANES - HEADS, 1) + pltpu.roll(parts, LANES - 2 * HEADS, 1)
    stat_ref[pl.ds(first, rows), :] = total[:rows]


def store_stats(stat_ref, out_ref, rows):
    wide = lane_rows(rows)
    lse = stat_ref[pl.ds(0, rows), :]
    if wide != rows:
        lse = jnp.concatenate([lse, jnp.zeros((wide - rows, LANES), jnp.float32)], axis=0)
    high = lse.astype(jnp.bfloat16).astype(jnp.float32)
    rest = lse - high
    middle = rest.astype(jnp.bfloat16).astype(jnp.float32)
    low = rest - middle
    lane = lax.broadcasted_iota(jnp.int32, lse.shape, 1)
    packed = jnp.where(
        lane < HEADS,
        high,
        jnp.where(lane < 2 * HEADS, pltpu.roll(middle, HEADS, 1), pltpu.roll(low, 2 * HEADS, 1)),
    )
    packed = jnp.where(lane < 3 * HEADS, packed, 0.0).T
    out_ref[pl.ds(rows, STAT_ROWS), pl.ds(0, wide)] = packed[:STAT_ROWS].astype(jnp.bfloat16)
    if wide < WIDTH:
        out_ref[pl.ds(rows, STAT_ROWS), pl.ds(wide, WIDTH - wide)] = jnp.zeros(
            (STAT_ROWS, WIDTH - wide), jnp.bfloat16
        )


def merge(old, old_lse, new, new_lse):
    best = jnp.maximum(old_lse, new_lse)
    old_part = jnp.exp(old_lse - best)
    new_part = jnp.exp(new_lse - best)
    both = old_part + new_part
    scale = 1.0 / both
    return old * (old_part * scale) + new * (new_part * scale), best + jnp.log(both)


def attend(q_ref, q_row, block, out_ref, stat_ref, row):
    stats = stat_ref[pl.ds(row, SPAN), :]
    lane = lax.broadcasted_iota(jnp.int32, (SPAN, LANES), 1)
    for head in range(HEADS):
        cols = slice(head * HEAD_DIM, (head + 1) * HEAD_DIM)
        queries = q_ref[pl.ds(q_row, SPAN), cols]
        keys = block[:, cols]
        values = block[:, WIDTH + head * HEAD_DIM : WIDTH + (head + 1) * HEAD_DIM]
        scores = (
            lax.dot_general(
                queries, keys, (((1,), (1,)), ((), ())), preferred_element_type=jnp.float32
            )
            * HEAD_DIM**-0.5
        )
        peaks = jnp.max(scores, axis=-1, keepdims=True)
        weights = jnp.exp(scores - peaks)
        totals = jnp.sum(weights, axis=-1, keepdims=True)
        mixed = jnp.dot(weights.astype(jnp.bfloat16), values, preferred_element_type=jnp.float32)
        old = out_ref[pl.ds(row, SPAN), cols].astype(jnp.float32)
        out, lse = merge(
            old, stats[:, head : head + 1], mixed / totals, peaks + jnp.log(totals)
        )
        out_ref[pl.ds(row, SPAN), cols] = out.astype(jnp.bfloat16)
        stats = jnp.where(lane == head, lse, stats)
    stat_ref[pl.ds(row, SPAN), :] = stats


def start_blocks(ids_ref, base, spans, kv_refs, buf_ref, sems, slot0):
    def one(i, carry):
        block = ids_ref[base + i]
        first = 0
        for kv_ref in kv_refs:
            held = kv_ref.shape[0]

            @pl.when((block >= first) & (block < first + held))
            def _():
                pltpu.make_async_copy(
                    kv_ref.at[block - first], buf_ref.at[slot0 + i], sems.at[slot0 + i]
                ).start()

            first += held
        return carry

    lax.fori_loop(0, spans * NBR, one, 0)


def attend_blocks(ids_ref, base, spans, q_ref, kv_refs, buf_ref, sems, slot0, out_ref, stat_ref):
    def one(i, carry):
        block = ids_ref[base + i]

        @pl.when(block >= 0)
        def _():
            pltpu.make_async_copy(
                kv_refs[0].at[0], buf_ref.at[slot0 + i], sems.at[slot0 + i]
            ).wait()
            row = pl.multiple_of((i // NBR) * SPAN, SPAN)
            attend(q_ref, row, buf_ref.at[slot0 + i], out_ref, stat_ref, row)

        return carry

    lax.fori_loop(0, spans * NBR, one, 0)


def relay_kernel(ways, *refs):
    ids_ref, kv_refs = refs[0], refs[1 : 1 + KV_PARTS]
    refs = refs[1 + KV_PARTS :]
    plan = []
    for base, spans, begin, held in ways:
        q_ref, refs = refs[0], refs[1:]
        state_ref = None
        if held:
            state_ref, refs = refs[0], refs[1:]
        plan.append([base, spans, begin, held, q_ref, state_ref])
    outs, refs = refs[: len(ways)], refs[len(ways) :]
    buf_ref, sems = refs[:2]
    stats = refs[2:]
    slot0 = 0
    for base, spans, *_ in plan:
        start_blocks(ids_ref, base, spans, kv_refs, buf_ref, sems, slot0)
        slot0 += spans * NBR
    slot0 = 0
    for (base, spans, begin, held, q_ref, state_ref), out_ref, stat_ref in zip(plan, outs, stats):
        rows = spans * SPAN
        if held != spans:
            out_ref[pl.ds(0, rows), :] = jnp.zeros((rows, WIDTH), jnp.bfloat16)
            stat_ref[...] = jnp.full((rows, LANES), FAR, jnp.float32)
        if held:
            load_state(state_ref, out_ref, stat_ref, begin * SPAN, held * SPAN)
        attend_blocks(
            ids_ref, base, spans, q_ref, kv_refs, buf_ref, sems, slot0, out_ref, stat_ref
        )
        store_stats(stat_ref, out_ref, rows)
        slot0 += spans * NBR


def final_kernel(base, spans, mask_base, ids_ref, edge_ref, *refs):
    kv_refs, refs = refs[:KV_PARTS], refs[KV_PARTS:]
    q_ref, fwd_ref, bwd_ref, out_ref, buf_ref, sems, stat_ref, other_ref, other_stat = refs
    rows = spans * SPAN
    start_blocks(ids_ref, base, spans, kv_refs, buf_ref, sems, 0)
    load_state(fwd_ref, out_ref, stat_ref, 0, rows)
    load_state(bwd_ref, other_ref, other_stat, 0, rows)
    lane = lax.broadcasted_iota(jnp.int32, (rows, LANES), 1)
    stats = stat_ref[...]
    for head in range(HEADS):
        cols = slice(head * HEAD_DIM, (head + 1) * HEAD_DIM)
        out, lse = merge(
            out_ref[:, cols].astype(jnp.float32),
            stat_ref[:, head : head + 1],
            other_ref[:, cols].astype(jnp.float32),
            other_stat[:, head : head + 1],
        )
        out_ref[:, cols] = out.astype(jnp.bfloat16)
        stats = jnp.where(lane == head, lse, stats)
    stat_ref[...] = stats
    attend_blocks(ids_ref, base, spans, q_ref, kv_refs, buf_ref, sems, 0, out_ref, stat_ref)

    def cut(i, carry):
        @pl.when(edge_ref[mask_base + i] > 0)
        def _():
            at = pl.ds(pl.multiple_of(i * SPAN, SPAN), SPAN)
            kept = lax.broadcasted_iota(jnp.int32, (SPAN, WIDTH), 0) == 0
            out_ref[at, :] = jnp.where(kept, out_ref[at, :], jnp.zeros((SPAN, WIDTH), jnp.bfloat16))

        return carry

    lax.fori_loop(0, spans, cut, 0)


SMEM = pl.BlockSpec(memory_space=pltpu.SMEM)
VMEM = pl.BlockSpec(memory_space=pltpu.VMEM)
ANY = pl.BlockSpec(memory_space=pl.ANY)


def cost(pairs, rows):
    return pl.CostEstimate(
        flops=pairs * HEADS * 4 * SPAN * HEAD_DIM * NBR_LEN,
        bytes_accessed=pairs * NBR_LEN * 4 * WIDTH + rows * WIDTH * 8,
        transcendentals=pairs * HEADS * SPAN * NBR_LEN,
    )


def relay(ids, kv, ways):
    specs = [w[:4] for w in ways]
    operands = [ids, *kv]
    for base, spans, begin, held, queries, state in ways:
        operands.append(queries)
        if held:
            operands.append(state)
    total = sum(spans for _, spans, _, _ in specs)
    return pl.pallas_call(
        functools.partial(relay_kernel, specs),
        out_shape=[
            jax.ShapeDtypeStruct((spans * SPAN + STAT_ROWS, WIDTH), jnp.bfloat16)
            for _, spans, _, _ in specs
        ],
        in_specs=[SMEM] + [ANY] * KV_PARTS + [VMEM] * (len(operands) - 1 - KV_PARTS),
        out_specs=[VMEM] * len(specs),
        scratch_shapes=[
            pltpu.VMEM((total * NBR, NBR_LEN, 2 * WIDTH), jnp.bfloat16),
            pltpu.SemaphoreType.DMA((total * NBR,)),
        ]
        + [pltpu.VMEM((spans * SPAN, LANES), jnp.float32) for _, spans, _, _ in specs],
        compiler_params=pltpu.CompilerParams(vmem_limit_bytes=24 * 1024 * 1024),
        cost_estimate=cost(6, total * SPAN),
    )(*operands)


def finish(ids, edges, kv, base, spans, mask_base, queries, fwd, bwd):
    rows = spans * SPAN
    return pl.pallas_call(
        functools.partial(final_kernel, base, spans, mask_base),
        out_shape=jax.ShapeDtypeStruct((rows, WIDTH), jnp.bfloat16),
        in_specs=[SMEM, SMEM] + [ANY] * KV_PARTS + [VMEM] * 3,
        out_specs=VMEM,
        scratch_shapes=[
            pltpu.VMEM((spans * NBR, NBR_LEN, 2 * WIDTH), jnp.bfloat16),
            pltpu.SemaphoreType.DMA((spans * NBR,)),
            pltpu.VMEM((rows, LANES), jnp.float32),
            pltpu.VMEM((rows, WIDTH), jnp.bfloat16),
            pltpu.VMEM((rows, LANES), jnp.float32),
        ],
        compiler_params=pltpu.CompilerParams(vmem_limit_bytes=24 * 1024 * 1024),
        cost_estimate=cost(3, rows),
    )(ids, edges, *kv, queries, fwd, bwd)


def gathered_kernel(norm, place_ref, *refs):
    pieces, refs = refs[: NX * NC], refs[NX * NC :]
    weight_ref, refs = refs[0], refs[1:]
    out_ref = refs[-1]

    def one(tile, carry):
        at = pl.ds(pl.multiple_of(tile * ROW_TILE, ROW_TILE), ROW_TILE)
        total = jnp.zeros((ROW_TILE, WIDTH), jnp.float32)
        squares = jnp.zeros((ROW_TILE, 1), jnp.float32)
        for i, piece_ref in enumerate(pieces):
            piece = piece_ref[at, :]
            block = pl.ds(pl.multiple_of(place_ref[i] * WIDTH, WIDTH), WIDTH)
            total += jnp.dot(piece, weight_ref[block, :], preferred_element_type=jnp.float32)
            if norm:
                wide = piece.astype(jnp.float32)
                squares += jnp.sum(wide * wide, axis=-1, keepdims=True)
        if norm:
            total = total * lax.rsqrt(squares * (1.0 / (WIDTH * NX * NC)) + 1e-05)
        else:
            total = total + refs[0][at, :].astype(jnp.float32)
        out_ref[at, :] = total.astype(jnp.bfloat16)
        return carry

    lax.fori_loop(0, out_ref.shape[0] // ROW_TILE, one, 0)


def gathered_dot(place, pieces, weight, residual=None):
    rows = pieces[0].shape[0]
    extra = [] if residual is None else [residual]
    return pl.pallas_call(
        functools.partial(gathered_kernel, residual is None),
        out_shape=jax.ShapeDtypeStruct((rows, WIDTH), jnp.bfloat16),
        in_specs=[SMEM] + [VMEM] * (NX * NC + 1 + len(extra)),
        out_specs=VMEM,
        compiler_params=pltpu.CompilerParams(vmem_limit_bytes=24 * 1024 * 1024),
        cost_estimate=pl.CostEstimate(
            flops=2 * rows * WIDTH * WIDTH * NX * NC,
            bytes_accessed=2 * WIDTH * (rows + WIDTH) * NX * NC,
            transcendentals=0,
        ),
    )(place, *pieces, weight, *extra)


def gather_pieces(own):
    up = [(2 * x, 2 * ((x + 1) % NX)) for x in range(NX)]
    down = [(2 * x + 1, 2 * ((x - 1) % NX) + 1) for x in range(NX)]
    swap = [(i, i ^ 1) for i in range(NX * NC)]
    held = [own]
    for _ in range(NX - 1):
        held.append(lax.ppermute(held[-1], STORE, up + down))
    return held + [lax.ppermute(piece, STORE, swap) for piece in held]


def piece_places():
    x, core = lax.axis_index("x"), lax.axis_index("core")
    step = 1 - 2 * core
    away = jnp.arange(NX, dtype=jnp.int32) * step
    mine = ((x - away) % NX) * NC + core
    others = ((x + away) % NX) * NC + 1 - core
    return jnp.concatenate([mine, others]).astype(jnp.int32)


def tie(array, *after):
    return lax.optimization_barrier((array, *after))[0]


def tie_all(arrays, *after):
    return list(lax.optimization_barrier((*arrays, *after))[: len(arrays)])


def on_device(hidden, nbr_shard, nbr_block, seq_lengths, kv_store, w_query, w_out):
    rows = hidden.shape[0]
    my_y, my_z = lax.axis_index("y"), lax.axis_index("z")
    seq_at = my_y * NZ + my_z
    order = [(i, i - 1) for i in range(1, NY * NZ)]
    edge = lax.ppermute(hidden[: SPAN - 1], SEQ, order)
    attending = jnp.concatenate([hidden[SPAN - 1 :], edge], axis=0)
    place = piece_places()

    wanted = nbr_shard * BLK_DEV + nbr_block
    wanted = lax.all_gather(wanted, "z")
    shard, block = wanted // BLK_DEV, wanted % BLK_DEV
    local = jnp.where(
        shard % NZ == my_z, ((shard // NZ - my_y) % NY) * BLK_DEV + block, -1
    ).astype(jnp.int32)
    local = local[(my_z + jnp.arange(NZ)) % NZ].reshape(-1)
    span_index = seq_at * SPANS_DEV + jnp.arange(SPANS_DEV, dtype=jnp.int32)
    boundary = jnp.any(jnp.cumsum(seq_lengths)[None, :] == span_index[:, None] + 1, axis=1)
    boundary = boundary.astype(jnp.int32)

    own = kv_store.reshape(BLK_DEV, NBR_LEN, 2 * WIDTH)
    above = ring(own, "y", NY, -1)
    below = ring(own, "y", NY, 1)
    half = BLK_DEV // 2
    kv = [own, above, ring(above[:half], "y", NY, -1), ring(below[half:], "y", NY, 1), below]

    parts = [attending[first * SPAN : last * SPAN] for first, last in CHUNKS]
    queries = [gathered_dot(place, gather_pieces(part), w_query) for part in parts]
    w_cols = jnp.concatenate([w_out[:, k * WIDTH : (k + 1) * WIDTH] for k in range(NX * NC)], axis=0)
    w_cols = tie(w_cols, queries[1])
    w_ready = w_cols
    w_cols = lax.all_to_all(w_cols, STORE, split_axis=0, concat_axis=0, tiled=True)

    count = len(CHUNKS)
    fwd, bwd = [[q] for q in queries], [[q] for q in queries]
    for step in range(3):
        for c in range(count):
            if step == 1 and c == 0:
                fwd[c][-1] = tie(fwd[c][-1], w_ready)
            fwd[c].append(ring(fwd[c][-1], "z", NZ, 1))
            bwd[c].append(ring(bwd[c][-1], "z", NZ, -1))
    cuts = [(last - first) // 2 for first, last in CHUNKS]
    far = [
        (ring(fwd[c][3][: cuts[c] * SPAN], "z", NZ, 1), ring(bwd[c][3][cuts[c] * SPAN :], "z", NZ, -1))
        for c in range(count)
    ]

    state = [None] * count
    sent = None
    for s in (4, 3, 2, 1, 0):
        for c, (first, last) in enumerate(CHUNKS):
            spans, split = last - first, cuts[c]

            def base(distance, start=0):
                return ((distance % NZ) * SPANS_DEV + first + start) * NBR

            if s == 4:
                top, low = far[c]
                if sent is not None:
                    top, low = tie_all([top, low], *sent)
                ways = [
                    (base(4), split, 0, 0, top, None),
                    (base(4, split), spans - split, 0, 0, low, None),
                ]
            else:
                if s == 2 and c == 0:
                    sent = [*sent, w_cols]
                top, low = tie_all(state[c], *sent)
                starts, helds = ((0, split), (split, spans - split)) if s == 3 else ((0, 0), (spans, spans))
                ways = [
                    (base(s), spans, starts[0], helds[0], bwd[c][s], top),
                    (base(-s), spans, starts[1], helds[1], fwd[c][s], low),
                ]
            if s:
                sent = relay(local, kv, ways)
                state[c] = [ring(sent[0], "z", NZ, 1), ring(sent[1], "z", NZ, -1)]
            else:
                state[c] = finish(
                    local, boundary, kv, base(0), spans, first, queries[c], top, low
                )
                sent = [state[c]]

    outs = {}
    for c, (first, last) in enumerate(CHUNKS):
        outs[first] = gathered_dot(place, gather_pieces(state[c]), w_cols, parts[c])
    result = jnp.concatenate([outs[first] for first in sorted(outs)], axis=0)
    order = [(i, i + 1) for i in range(NY * NZ - 1)]
    head = lax.ppermute(result[rows - (SPAN - 1) :], SEQ, order)
    head = jnp.where(seq_at == 0, hidden[: SPAN - 1], head)
    return jnp.concatenate([head, result[: rows - (SPAN - 1)]], axis=0)


def solution(mesh):
    fine = Mesh(mesh.devices.reshape(NY, NZ, NX, NC), ("y", "z", "x", "core"))
    return jax.shard_map(
        on_device,
        mesh=fine,
        in_specs=(
            P(SEQ, STORE),
            P(SEQ, None),
            P(SEQ, None),
            P(),
            P(SEQ, None, None, STORE),
            P(None, STORE),
            P(STORE, None),
        ),
        out_specs=P(SEQ, STORE),
        check_vma=False,
    )
```

```python
import functools
import jax
import jax.numpy as jnp
from jax import lax
from jax.experimental import pallas as pl
from jax.experimental.pallas import tpu as pltpu
from jax.sharding import Mesh, PartitionSpec as P

HEAD_DIM = 128
SPAN = 64
NBR = 2
NBR_LEN = 128
HEADS = 4
WIDTH = HEADS * HEAD_DIM
BLK_DEV = 8
NY, NZ, NX, NC = 4, 8, 4, 2
SEQ, STORE = ("y", "z"), ("x", "core")
SPANS_DEV = 12
CHUNKS = ((6, 12), (0, 6))
STAT_ROWS = 16
FAR = -1e30
KV_PARTS = 5
ROW_TILE = 128
SCALE = HEAD_DIM**-0.5 * 1.4426950408889634
LANES = 128


def ring(array, axis, size, by):
    return lax.ppermute(array, axis, [(i, (i + by) % size) for i in range(size)])


def lane_rows(rows):
    return -(-rows // LANES) * LANES


def load_state(state_ref, out_ref, stat_ref, first, rows):
    out_ref[pl.ds(first, rows), :] = state_ref[pl.ds(0, rows), :]
    wide = lane_rows(rows)
    packed = state_ref[pl.ds(rows, STAT_ROWS), pl.ds(0, wide)].astype(jnp.float32)
    parts = jnp.concatenate([packed, jnp.zeros((LANES - STAT_ROWS, wide), jnp.float32)], axis=0).T
    total = parts + pltpu.roll(parts, LANES - HEADS, 1) + pltpu.roll(parts, LANES - 2 * HEADS, 1)
    stat_ref[pl.ds(first, rows), :] = total[:rows]


def store_stats(stat_ref, out_ref, rows):
    wide = lane_rows(rows)
    lse = stat_ref[pl.ds(0, rows), :]
    if wide != rows:
        lse = jnp.concatenate([lse, jnp.zeros((wide - rows, LANES), jnp.float32)], axis=0)
    high = lse.astype(jnp.bfloat16).astype(jnp.float32)
    rest = lse - high
    middle = rest.astype(jnp.bfloat16).astype(jnp.float32)
    low = rest - middle
    lane = lax.broadcasted_iota(jnp.int32, lse.shape, 1)
    packed = jnp.where(
        lane < HEADS,
        high,
        jnp.where(lane < 2 * HEADS, pltpu.roll(middle, HEADS, 1), pltpu.roll(low, 2 * HEADS, 1)),
    )
    packed = jnp.where(lane < 3 * HEADS, packed, 0.0).T
    out_ref[pl.ds(rows, STAT_ROWS), pl.ds(0, wide)] = packed[:STAT_ROWS].astype(jnp.bfloat16)
    if wide < WIDTH:
        out_ref[pl.ds(rows, STAT_ROWS), pl.ds(wide, WIDTH - wide)] = jnp.zeros(
            (STAT_ROWS, WIDTH - wide), jnp.bfloat16
        )


def merge(old, new):
    best = jnp.maximum(old, new)
    old_part = jnp.exp2(old - best)
    new_part = jnp.exp2(new - best)
    both = old_part + new_part
    scale = 1.0 / both
    return old_part * scale, new_part * scale, best + jnp.log2(both)


def attend(q_ref, q_row, block, out_ref, stat_ref, row):
    at = pl.ds(row, SPAN)
    lane = lax.broadcasted_iota(jnp.int32, (SPAN, LANES), 1)
    queries = q_ref[pl.ds(q_row, SPAN), :]
    old = out_ref[at, :].astype(jnp.float32)
    old_lse = stat_ref[at, :]
    heads = [slice(head * HEAD_DIM, (head + 1) * HEAD_DIM) for head in range(HEADS)]
    scores = [
        lax.dot_general(
            queries[:, cols], block[:, cols], (((1,), (1,)), ((), ())),
            preferred_element_type=jnp.float32,
        )
        for cols in heads
    ]
    peaks = [jnp.max(score, axis=-1, keepdims=True) for score in scores]
    weights = [jnp.exp2((score - peak) * SCALE) for score, peak in zip(scores, peaks)]
    totals = [jnp.sum(weight, axis=-1, keepdims=True) for weight in weights]
    mixed = [
        jnp.dot(
            weight.astype(jnp.bfloat16),
            block[:, WIDTH + cols.start : WIDTH + cols.stop],
            preferred_element_type=jnp.float32,
        )
        for weight, cols in zip(weights, heads)
    ]
    peak_tile = jnp.zeros((SPAN, LANES), jnp.float32)
    total_tile = jnp.ones((SPAN, LANES), jnp.float32)
    for head in range(HEADS):
        peak_tile = jnp.where(lane == head, peaks[head], peak_tile)
        total_tile = jnp.where(lane == head, totals[head], total_tile)
    old_weight, new_weight, lse = merge(old_lse, peak_tile * SCALE + jnp.log2(total_tile))
    new_weight = new_weight / total_tile
    outs = [
        old[:, cols] * old_weight[:, head : head + 1] + mixed[head] * new_weight[:, head : head + 1]
        for head, cols in enumerate(heads)
    ]
    stat_ref[at, :] = lse
    for cols, out in zip(heads, outs):
        out_ref[at, cols] = out.astype(jnp.bfloat16)


def start_blocks(ids_ref, base, spans, kv_refs, buf_ref, sems, slot0):
    def one(i, carry):
        block = ids_ref[base + i]
        first = 0
        for kv_ref in kv_refs:
            held = kv_ref.shape[0]

            @pl.when((block >= first) & (block < first + held))
            def _():
                pltpu.make_async_copy(
                    kv_ref.at[block - first], buf_ref.at[slot0 + i], sems.at[slot0 + i]
                ).start()

            first += held
        return carry

    lax.fori_loop(0, spans * NBR, one, 0)


def attend_blocks(ids_ref, base, spans, q_ref, kv_refs, buf_ref, sems, slot0, out_ref, stat_ref):
    def one(i, carry):
        block = ids_ref[base + i]

        @pl.when(block >= 0)
        def _():
            pltpu.make_async_copy(
                kv_refs[0].at[0], buf_ref.at[slot0 + i], sems.at[slot0 + i]
            ).wait()
            row = pl.multiple_of((i // NBR) * SPAN, SPAN)
            attend(q_ref, row, buf_ref.at[slot0 + i], out_ref, stat_ref, row)

        return carry

    lax.fori_loop(0, spans * NBR, one, 0)


def relay_kernel(ways, *refs):
    ids_ref, kv_refs = refs[0], refs[1 : 1 + KV_PARTS]
    refs = refs[1 + KV_PARTS :]
    plan = []
    for base, spans, begin, held in ways:
        q_ref, refs = refs[0], refs[1:]
        state_ref = None
        if held:
            state_ref, refs = refs[0], refs[1:]
        plan.append([base, spans, begin, held, q_ref, state_ref])
    outs, refs = refs[: len(ways)], refs[len(ways) :]
    buf_ref, sems = refs[:2]
    stats = refs[2:]
    slot0 = 0
    for base, spans, *_ in plan:
        start_blocks(ids_ref, base, spans, kv_refs, buf_ref, sems, slot0)
        slot0 += spans * NBR
    slot0 = 0
    for (base, spans, begin, held, q_ref, state_ref), out_ref, stat_ref in zip(plan, outs, stats):
        rows = spans * SPAN
        if held != spans:
            out_ref[pl.ds(0, rows), :] = jnp.zeros((rows, WIDTH), jnp.bfloat16)
            stat_ref[...] = jnp.full((rows, LANES), FAR, jnp.float32)
        if held:
            load_state(state_ref, out_ref, stat_ref, begin * SPAN, held * SPAN)
        attend_blocks(
            ids_ref, base, spans, q_ref, kv_refs, buf_ref, sems, slot0, out_ref, stat_ref
        )
        store_stats(stat_ref, out_ref, rows)
        slot0 += spans * NBR


def final_kernel(base, spans, mask_base, ids_ref, edge_ref, *refs):
    kv_refs, refs = refs[:KV_PARTS], refs[KV_PARTS:]
    q_ref, fwd_ref, bwd_ref, out_ref, buf_ref, sems, stat_ref, other_ref, other_stat = refs
    rows = spans * SPAN
    start_blocks(ids_ref, base, spans, kv_refs, buf_ref, sems, 0)
    load_state(fwd_ref, out_ref, stat_ref, 0, rows)
    load_state(bwd_ref, other_ref, other_stat, 0, rows)
    weight, other_weight, lse = merge(stat_ref[...], other_stat[...])
    stat_ref[...] = lse
    for head in range(HEADS):
        cols = slice(head * HEAD_DIM, (head + 1) * HEAD_DIM)
        out_ref[:, cols] = (
            out_ref[:, cols].astype(jnp.float32) * weight[:, head : head + 1]
            + other_ref[:, cols].astype(jnp.float32) * other_weight[:, head : head + 1]
        ).astype(jnp.bfloat16)
    attend_blocks(ids_ref, base, spans, q_ref, kv_refs, buf_ref, sems, 0, out_ref, stat_ref)

    def cut(i, carry):
        @pl.when(edge_ref[mask_base + i] > 0)
        def _():
            at = pl.ds(pl.multiple_of(i * SPAN, SPAN), SPAN)
            kept = lax.broadcasted_iota(jnp.int32, (SPAN, WIDTH), 0) == 0
            out_ref[at, :] = jnp.where(kept, out_ref[at, :], jnp.zeros((SPAN, WIDTH), jnp.bfloat16))

        return carry

    lax.fori_loop(0, spans, cut, 0)


SMEM = pl.BlockSpec(memory_space=pltpu.SMEM)
VMEM = pl.BlockSpec(memory_space=pltpu.VMEM)
ANY = pl.BlockSpec(memory_space=pl.ANY)


def cost(pairs, rows):
    return pl.CostEstimate(
        flops=pairs * HEADS * 4 * SPAN * HEAD_DIM * NBR_LEN,
        bytes_accessed=pairs * NBR_LEN * 4 * WIDTH + rows * WIDTH * 8,
        transcendentals=pairs * HEADS * SPAN * NBR_LEN,
    )


def relay(ids, kv, ways):
    specs = [w[:4] for w in ways]
    operands = [ids, *kv]
    for base, spans, begin, held, queries, state in ways:
        operands.append(queries)
        if held:
            operands.append(state)
    total = sum(spans for _, spans, _, _ in specs)
    return pl.pallas_call(
        functools.partial(relay_kernel, specs),
        out_shape=[
            jax.ShapeDtypeStruct((spans * SPAN + STAT_ROWS, WIDTH), jnp.bfloat16)
            for _, spans, _, _ in specs
        ],
        in_specs=[SMEM] + [ANY] * KV_PARTS + [VMEM] * (len(operands) - 1 - KV_PARTS),
        out_specs=[VMEM] * len(specs),
        scratch_shapes=[
            pltpu.VMEM((total * NBR, NBR_LEN, 2 * WIDTH), jnp.bfloat16),
            pltpu.SemaphoreType.DMA((total * NBR,)),
        ]
        + [pltpu.VMEM((spans * SPAN, LANES), jnp.float32) for _, spans, _, _ in specs],
        compiler_params=pltpu.CompilerParams(vmem_limit_bytes=16 * 1024 * 1024),
        cost_estimate=cost(6, total * SPAN),
    )(*operands)


def finish(ids, edges, kv, base, spans, mask_base, queries, fwd, bwd):
    rows = spans * SPAN
    return pl.pallas_call(
        functools.partial(final_kernel, base, spans, mask_base),
        out_shape=jax.ShapeDtypeStruct((rows, WIDTH), jnp.bfloat16),
        in_specs=[SMEM, SMEM] + [ANY] * KV_PARTS + [VMEM] * 3,
        out_specs=VMEM,
        scratch_shapes=[
            pltpu.VMEM((spans * NBR, NBR_LEN, 2 * WIDTH), jnp.bfloat16),
            pltpu.SemaphoreType.DMA((spans * NBR,)),
            pltpu.VMEM((rows, LANES), jnp.float32),
            pltpu.VMEM((rows, WIDTH), jnp.bfloat16),
            pltpu.VMEM((rows, LANES), jnp.float32),
        ],
        compiler_params=pltpu.CompilerParams(vmem_limit_bytes=16 * 1024 * 1024),
        cost_estimate=cost(3, rows),
    )(ids, edges, *kv, queries, fwd, bwd)


def gathered_kernel(norm, place_ref, *refs):
    pieces, refs = refs[: NX * NC], refs[NX * NC :]
    weight_ref, refs = refs[0], refs[1:]
    out_ref = refs[-1]

    def one(tile, carry):
        at = pl.ds(pl.multiple_of(tile * ROW_TILE, ROW_TILE), ROW_TILE)
        total = jnp.zeros((ROW_TILE, WIDTH), jnp.float32)
        squares = jnp.zeros((ROW_TILE, 1), jnp.float32)
        for i, piece_ref in enumerate(pieces):
            piece = piece_ref[at, :]
            block = pl.ds(pl.multiple_of(place_ref[i] * WIDTH, WIDTH), WIDTH)
            total += jnp.dot(piece, weight_ref[block, :], preferred_element_type=jnp.float32)
            if norm:
                wide = piece.astype(jnp.float32)
                squares += jnp.sum(wide * wide, axis=-1, keepdims=True)
        if norm:
            total = total * lax.rsqrt(squares * (1.0 / (WIDTH * NX * NC)) + 1e-05)
        else:
            total = total + refs[0][at, :].astype(jnp.float32)
        out_ref[at, :] = total.astype(jnp.bfloat16)
        return carry

    lax.fori_loop(0, out_ref.shape[0] // ROW_TILE, one, 0)


def gathered_dot(place, pieces, weight, residual=None):
    rows = pieces[0].shape[0]
    extra = [] if residual is None else [residual]
    return pl.pallas_call(
        functools.partial(gathered_kernel, residual is None),
        out_shape=jax.ShapeDtypeStruct((rows, WIDTH), jnp.bfloat16),
        in_specs=[SMEM] + [VMEM] * (NX * NC + 1 + len(extra)),
        out_specs=VMEM,
        compiler_params=pltpu.CompilerParams(vmem_limit_bytes=16 * 1024 * 1024),
        cost_estimate=pl.CostEstimate(
            flops=2 * rows * WIDTH * WIDTH * NX * NC,
            bytes_accessed=2 * WIDTH * (rows + WIDTH) * NX * NC,
            transcendentals=0,
        ),
    )(place, *pieces, weight, *extra)


def gather_pieces(own):
    up = [(2 * x, 2 * ((x + 1) % NX)) for x in range(NX)]
    down = [(2 * x + 1, 2 * ((x - 1) % NX) + 1) for x in range(NX)]
    swap = [(i, i ^ 1) for i in range(NX * NC)]
    held = [own]
    for _ in range(NX - 1):
        held.append(lax.ppermute(held[-1], STORE, up + down))
    return held + [lax.ppermute(piece, STORE, swap) for piece in held]


def piece_places():
    x, core = lax.axis_index("x"), lax.axis_index("core")
    step = 1 - 2 * core
    away = jnp.arange(NX, dtype=jnp.int32) * step
    mine = ((x - away) % NX) * NC + core
    others = ((x + away) % NX) * NC + 1 - core
    return jnp.concatenate([mine, others]).astype(jnp.int32)


def column_kernel(w_ref, out_ref, sems):
    copies = [
        pltpu.make_async_copy(
            w_ref.at[:, pl.ds(k * WIDTH, WIDTH)], out_ref.at[pl.ds(k * WIDTH, WIDTH), :], sems.at[k]
        )
        for k in range(NX * NC)
    ]
    for copy in copies:
        copy.start()
    for copy in copies:
        copy.wait()


def column_blocks(weight):
    return pl.pallas_call(
        column_kernel,
        out_shape=jax.ShapeDtypeStruct((NX * NC * WIDTH, WIDTH), weight.dtype),
        in_specs=[ANY],
        out_specs=ANY,
        scratch_shapes=[pltpu.SemaphoreType.DMA((NX * NC,))],
        cost_estimate=pl.CostEstimate(
            flops=0, bytes_accessed=4 * NX * NC * WIDTH * WIDTH, transcendentals=0
        ),
    )(weight)


def tie(array, *after):
    return lax.optimization_barrier((array, *after))[0]


def tie_all(arrays, *after):
    return list(lax.optimization_barrier((*arrays, *after))[: len(arrays)])


def on_device(hidden, nbr_shard, nbr_block, seq_lengths, kv_store, w_query, w_out):
    rows = hidden.shape[0]
    my_y, my_z = lax.axis_index("y"), lax.axis_index("z")
    seq_at = my_y * NZ + my_z
    order = [(i, i - 1) for i in range(1, NY * NZ)]
    edge = lax.ppermute(hidden[: SPAN - 1], SEQ, order)
    attending = jnp.concatenate([hidden[SPAN - 1 :], edge], axis=0)
    place = piece_places()

    wanted = (nbr_shard * BLK_DEV + nbr_block).reshape(-1)
    for by in (1, 2, 4):
        wanted = jnp.concatenate([wanted, ring(wanted, "z", NZ, -by)])
    shard, block = wanted // BLK_DEV, wanted % BLK_DEV
    local = jnp.where(
        shard % NZ == my_z, ((shard // NZ - my_y) % NY) * BLK_DEV + block, -1
    ).astype(jnp.int32)
    span_index = seq_at * SPANS_DEV + jnp.arange(SPANS_DEV, dtype=jnp.int32)
    upto = jnp.arange(seq_lengths.shape[0])
    seq_ends = jnp.sum(jnp.where(upto[None, :] <= upto[:, None], seq_lengths[None, :], 0), axis=1)
    boundary = jnp.any(seq_ends[None, :] == span_index[:, None] + 1, axis=1)
    boundary = boundary.astype(jnp.int32)

    own = kv_store.reshape(BLK_DEV, NBR_LEN, 2 * WIDTH)
    above = ring(own, "y", NY, -1)
    below = ring(own, "y", NY, 1)
    half = BLK_DEV // 2
    kv = [own, above, ring(above[:half], "y", NY, -1), ring(below[half:], "y", NY, 1), below]

    parts = [attending[first * SPAN : last * SPAN] for first, last in CHUNKS]
    queries = [gathered_dot(place, gather_pieces(part), w_query) for part in parts]
    w_cols = tie(column_blocks(w_out), *queries)
    w_ready = w_cols
    w_cols = lax.all_to_all(w_cols, STORE, split_axis=0, concat_axis=0, tiled=True)

    count = len(CHUNKS)
    fwd, bwd = [[q] for q in queries], [[q] for q in queries]
    for step in range(3):
        for c in range(count):
            if step == 1 and c == 0:
                fwd[c][-1] = tie(fwd[c][-1], above, below, local, boundary, w_ready)
            fwd[c].append(ring(fwd[c][-1], "z", NZ, 1))
            bwd[c].append(ring(bwd[c][-1], "z", NZ, -1))
    cuts = [(last - first) // 2 for first, last in CHUNKS]
    far = [
        (ring(fwd[c][3][: cuts[c] * SPAN], "z", NZ, 1), ring(bwd[c][3][cuts[c] * SPAN :], "z", NZ, -1))
        for c in range(count)
    ]

    state = [None] * count
    sent = None
    for s in (4, 3, 2, 1, 0):
        for c, (first, last) in enumerate(CHUNKS):
            spans, split = last - first, cuts[c]

            def base(distance, start=0):
                return ((distance % NZ) * SPANS_DEV + first + start) * NBR

            if s == 4:
                top, low = far[c]
                if sent is not None:
                    top, low = tie_all([top, low], *sent)
                ways = [
                    (base(4), split, 0, 0, top, None),
                    (base(4, split), spans - split, 0, 0, low, None),
                ]
            else:
                if s == 2 and c == 0:
                    sent = [*sent, w_cols]
                top, low = tie_all(state[c], *sent)
                starts, helds = ((0, split), (split, spans - split)) if s == 3 else ((0, 0), (spans, spans))
                ways = [
                    (base(s), spans, starts[0], helds[0], bwd[c][s], top),
                    (base(-s), spans, starts[1], helds[1], fwd[c][s], low),
                ]
            if s:
                sent = relay(local, kv, ways)
                state[c] = [ring(sent[0], "z", NZ, 1), ring(sent[1], "z", NZ, -1)]
            else:
                state[c] = finish(
                    local, boundary, kv, base(0), spans, first, queries[c], top, low
                )
                sent = [state[c]]

    outs = {}
    for c, (first, last) in enumerate(CHUNKS):
        outs[first] = gathered_dot(place, gather_pieces(state[c]), w_cols, parts[c])
    result = jnp.concatenate([outs[first] for first in sorted(outs)], axis=0)
    order = [(i, i + 1) for i in range(NY * NZ - 1)]
    head = lax.ppermute(result[rows - (SPAN - 1) :], SEQ, order)
    head = jnp.where(seq_at == 0, hidden[: SPAN - 1], head)
    return jnp.concatenate([head, result[: rows - (SPAN - 1)]], axis=0)


def solution(mesh):
    fine = Mesh(mesh.devices.reshape(NY, NZ, NX, NC), ("y", "z", "x", "core"))
    return jax.shard_map(
        on_device,
        mesh=fine,
        in_specs=(
            P(SEQ, STORE),
            P(SEQ, None),
            P(SEQ, None),
            P(),
            P(SEQ, None, None, STORE),
            P(None, STORE),
            P(STORE, None),
        ),
        out_specs=P(SEQ, STORE),
        check_vma=False,
    )
```

```python
import functools
import jax
import jax.numpy as jnp
from jax import lax
from jax.experimental import pallas as pl
from jax.experimental.pallas import tpu as pltpu
from jax.sharding import Mesh, PartitionSpec as P

HEAD_DIM = 128
SPAN = 64
NBR = 2
NBR_LEN = 128
HEADS = 4
WIDTH = HEADS * HEAD_DIM
BLK_DEV = 8
NY, NZ, NX, NC = 4, 8, 4, 2
SEQ, STORE = ("y", "z"), ("x", "core")
SPANS_DEV = 12
CHUNKS = ((6, 12), (0, 6))
STAT_ROWS = 16
FAR = -1e30
ROW_TILE = 384
SCALE = HEAD_DIM**-0.5 * 1.4426950408889634
LANES = 128


def ring(array, axis, size, by):
    return lax.ppermute(array, axis, [(i, (i + by) % size) for i in range(size)])


def lane_rows(rows):
    return -(-rows // LANES) * LANES


def load_state(state_ref, out_ref, stat_ref, first, rows):
    out_ref[pl.ds(first, rows), :] = state_ref[pl.ds(0, rows), :]
    wide = lane_rows(rows)
    packed = state_ref[pl.ds(rows, STAT_ROWS), pl.ds(0, wide)].astype(jnp.float32)
    parts = jnp.concatenate([packed, jnp.zeros((LANES - STAT_ROWS, wide), jnp.float32)], axis=0).T
    total = parts + pltpu.roll(parts, LANES - HEADS, 1) + pltpu.roll(parts, LANES - 2 * HEADS, 1)
    stat_ref[pl.ds(first, rows), :] = total[:rows]


def store_stats(stat_ref, out_ref, rows):
    wide = lane_rows(rows)
    lse = stat_ref[pl.ds(0, rows), :]
    if wide != rows:
        lse = jnp.concatenate([lse, jnp.zeros((wide - rows, LANES), jnp.float32)], axis=0)
    high = lse.astype(jnp.bfloat16).astype(jnp.float32)
    rest = lse - high
    middle = rest.astype(jnp.bfloat16).astype(jnp.float32)
    low = rest - middle
    lane = lax.broadcasted_iota(jnp.int32, lse.shape, 1)
    packed = jnp.where(
        lane < HEADS,
        high,
        jnp.where(lane < 2 * HEADS, pltpu.roll(middle, HEADS, 1), pltpu.roll(low, 2 * HEADS, 1)),
    )
    packed = jnp.where(lane < 3 * HEADS, packed, 0.0).T
    out_ref[pl.ds(rows, STAT_ROWS), pl.ds(0, wide)] = packed[:STAT_ROWS].astype(jnp.bfloat16)
    if wide < WIDTH:
        out_ref[pl.ds(rows, STAT_ROWS), pl.ds(wide, WIDTH - wide)] = jnp.zeros(
            (STAT_ROWS, WIDTH - wide), jnp.bfloat16
        )


def merge(old, new):
    best = jnp.maximum(old, new)
    old_part = jnp.exp2(old - best)
    new_part = jnp.exp2(new - best)
    both = old_part + new_part
    scale = 1.0 / both
    return old_part * scale, new_part * scale, best + jnp.log2(both)


def attend(q_ref, q_row, block, out_ref, stat_ref, row):
    at = pl.ds(row, SPAN)
    lane = lax.broadcasted_iota(jnp.int32, (SPAN, LANES), 1)
    queries = q_ref[pl.ds(q_row, SPAN), :]
    old = out_ref[at, :].astype(jnp.float32)
    old_lse = stat_ref[at, :]
    heads = [slice(head * HEAD_DIM, (head + 1) * HEAD_DIM) for head in range(HEADS)]
    scores = [
        lax.dot_general(
            queries[:, cols], block[:, cols], (((1,), (1,)), ((), ())),
            preferred_element_type=jnp.float32,
        )
        for cols in heads
    ]
    peaks = [jnp.max(score, axis=-1, keepdims=True) for score in scores]
    weights = [jnp.exp2((score - peak) * SCALE) for score, peak in zip(scores, peaks)]
    totals = [jnp.sum(weight, axis=-1, keepdims=True) for weight in weights]
    mixed = [
        jnp.dot(
            weight.astype(jnp.bfloat16),
            block[:, WIDTH + cols.start : WIDTH + cols.stop],
            preferred_element_type=jnp.float32,
        )
        for weight, cols in zip(weights, heads)
    ]
    peak_tile = jnp.zeros((SPAN, LANES), jnp.float32)
    total_tile = jnp.ones((SPAN, LANES), jnp.float32)
    for head in range(HEADS):
        peak_tile = jnp.where(lane == head, peaks[head], peak_tile)
        total_tile = jnp.where(lane == head, totals[head], total_tile)
    old_weight, new_weight, lse = merge(old_lse, peak_tile * SCALE + jnp.log2(total_tile))
    new_weight = new_weight / total_tile
    outs = [
        old[:, cols] * old_weight[:, head : head + 1] + mixed[head] * new_weight[:, head : head + 1]
        for head, cols in enumerate(heads)
    ]
    stat_ref[at, :] = lse
    for cols, out in zip(heads, outs):
        out_ref[at, cols] = out.astype(jnp.bfloat16)


def start_blocks(ids_ref, base, spans, kv_ref, buf_ref, sems, slot0):
    def one(i, carry):
        block = ids_ref[base + i]

        @pl.when(block >= 0)
        def _():
            pltpu.make_async_copy(
                kv_ref.at[block], buf_ref.at[slot0 + i], sems.at[slot0 + i]
            ).start()

        return carry

    lax.fori_loop(0, spans * NBR, one, 0)


def attend_blocks(ids_ref, base, spans, q_ref, kv_ref, buf_ref, sems, slot0, out_ref, stat_ref):
    def one(i, carry):
        block = ids_ref[base + i]

        @pl.when(block >= 0)
        def _():
            pltpu.make_async_copy(
                kv_ref.at[0], buf_ref.at[slot0 + i], sems.at[slot0 + i]
            ).wait()
            row = pl.multiple_of((i // NBR) * SPAN, SPAN)
            attend(q_ref, row, buf_ref.at[slot0 + i], out_ref, stat_ref, row)

        return carry

    lax.fori_loop(0, spans * NBR, one, 0)


def relay_kernel(ways, *refs):
    ids_ref, kv_ref = refs[:2]
    refs = refs[2:]
    plan = []
    for base, spans, begin, held in ways:
        q_ref, refs = refs[0], refs[1:]
        state_ref = None
        if held:
            state_ref, refs = refs[0], refs[1:]
        plan.append([base, spans, begin, held, q_ref, state_ref])
    outs, refs = refs[: len(ways)], refs[len(ways) :]
    buf_ref, sems = refs[:2]
    stats = refs[2:]
    slot0 = 0
    for base, spans, *_ in plan:
        start_blocks(ids_ref, base, spans, kv_ref, buf_ref, sems, slot0)
        slot0 += spans * NBR
    slot0 = 0
    for (base, spans, begin, held, q_ref, state_ref), out_ref, stat_ref in zip(plan, outs, stats):
        rows = spans * SPAN
        if held != spans:
            out_ref[pl.ds(0, rows), :] = jnp.zeros((rows, WIDTH), jnp.bfloat16)
            stat_ref[...] = jnp.full((rows, LANES), FAR, jnp.float32)
        if held:
            load_state(state_ref, out_ref, stat_ref, begin * SPAN, held * SPAN)
        attend_blocks(
            ids_ref, base, spans, q_ref, kv_ref, buf_ref, sems, slot0, out_ref, stat_ref
        )
        store_stats(stat_ref, out_ref, rows)
        slot0 += spans * NBR


def final_kernel(base, spans, mask_base, ids_ref, edge_ref, kv_ref, *refs):
    q_ref, fwd_ref, bwd_ref, out_ref, buf_ref, sems, stat_ref, other_ref, other_stat = refs
    rows = spans * SPAN
    start_blocks(ids_ref, base, spans, kv_ref, buf_ref, sems, 0)
    load_state(fwd_ref, out_ref, stat_ref, 0, rows)
    load_state(bwd_ref, other_ref, other_stat, 0, rows)
    weight, other_weight, lse = merge(stat_ref[...], other_stat[...])
    stat_ref[...] = lse
    for head in range(HEADS):
        cols = slice(head * HEAD_DIM, (head + 1) * HEAD_DIM)
        out_ref[:, cols] = (
            out_ref[:, cols].astype(jnp.float32) * weight[:, head : head + 1]
            + other_ref[:, cols].astype(jnp.float32) * other_weight[:, head : head + 1]
        ).astype(jnp.bfloat16)
    attend_blocks(ids_ref, base, spans, q_ref, kv_ref, buf_ref, sems, 0, out_ref, stat_ref)

    def cut(i, carry):
        @pl.when(edge_ref[mask_base + i] > 0)
        def _():
            at = pl.ds(pl.multiple_of(i * SPAN, SPAN), SPAN)
            kept = lax.broadcasted_iota(jnp.int32, (SPAN, WIDTH), 0) == 0
            out_ref[at, :] = jnp.where(kept, out_ref[at, :], jnp.zeros((SPAN, WIDTH), jnp.bfloat16))

        return carry

    lax.fori_loop(0, spans, cut, 0)


SMEM = pl.BlockSpec(memory_space=pltpu.SMEM)
VMEM = pl.BlockSpec(memory_space=pltpu.VMEM)
ANY = pl.BlockSpec(memory_space=pl.ANY)


def cost(pairs, rows):
    return pl.CostEstimate(
        flops=pairs * HEADS * 4 * SPAN * HEAD_DIM * NBR_LEN,
        bytes_accessed=pairs * NBR_LEN * 4 * WIDTH + rows * WIDTH * 8,
        transcendentals=pairs * HEADS * SPAN * NBR_LEN,
    )


def relay(ids, kv, ways):
    specs = [w[:4] for w in ways]
    operands = [ids, kv]
    for base, spans, begin, held, queries, state in ways:
        operands.append(queries)
        if held:
            operands.append(state)
    total = sum(spans for _, spans, _, _ in specs)
    return pl.pallas_call(
        functools.partial(relay_kernel, specs),
        out_shape=[
            jax.ShapeDtypeStruct((spans * SPAN + STAT_ROWS, WIDTH), jnp.bfloat16)
            for _, spans, _, _ in specs
        ],
        in_specs=[SMEM, ANY] + [VMEM] * (len(operands) - 2),
        out_specs=[VMEM] * len(specs),
        scratch_shapes=[
            pltpu.VMEM((total * NBR, NBR_LEN, 2 * WIDTH), jnp.bfloat16),
            pltpu.SemaphoreType.DMA((total * NBR,)),
        ]
        + [pltpu.VMEM((spans * SPAN, LANES), jnp.float32) for _, spans, _, _ in specs],
        compiler_params=pltpu.CompilerParams(vmem_limit_bytes=16 * 1024 * 1024),
        cost_estimate=cost(6, total * SPAN),
    )(*operands)


def finish(ids, edges, kv, base, spans, mask_base, queries, fwd, bwd):
    rows = spans * SPAN
    return pl.pallas_call(
        functools.partial(final_kernel, base, spans, mask_base),
        out_shape=jax.ShapeDtypeStruct((rows, WIDTH), jnp.bfloat16),
        in_specs=[SMEM, SMEM, ANY] + [VMEM] * 3,
        out_specs=VMEM,
        scratch_shapes=[
            pltpu.VMEM((spans * NBR, NBR_LEN, 2 * WIDTH), jnp.bfloat16),
            pltpu.SemaphoreType.DMA((spans * NBR,)),
            pltpu.VMEM((rows, LANES), jnp.float32),
            pltpu.VMEM((rows, WIDTH), jnp.bfloat16),
            pltpu.VMEM((rows, LANES), jnp.float32),
        ],
        compiler_params=pltpu.CompilerParams(vmem_limit_bytes=16 * 1024 * 1024),
        cost_estimate=cost(3, rows),
    )(ids, edges, kv, queries, fwd, bwd)


def gathered_kernel(norm, place_ref, *refs):
    pieces, refs = refs[: NX * NC], refs[NX * NC :]
    weight_ref, refs = refs[0], refs[1:]
    out_ref = refs[-1]

    def one(tile, carry):
        at = pl.ds(pl.multiple_of(tile * ROW_TILE, ROW_TILE), ROW_TILE)
        total = jnp.zeros((ROW_TILE, WIDTH), jnp.float32)
        squares = jnp.zeros((ROW_TILE, 1), jnp.float32)
        for i, piece_ref in enumerate(pieces):
            piece = piece_ref[at, :]
            block = pl.ds(pl.multiple_of(place_ref[i] * WIDTH, WIDTH), WIDTH)
            total += jnp.dot(piece, weight_ref[block, :], preferred_element_type=jnp.float32)
            if norm:
                wide = piece.astype(jnp.float32)
                squares += jnp.sum(wide * wide, axis=-1, keepdims=True)
        if norm:
            total = total * lax.rsqrt(squares * (1.0 / (WIDTH * NX * NC)) + 1e-05)
        else:
            total = total + refs[0][at, :].astype(jnp.float32)
        out_ref[at, :] = total.astype(jnp.bfloat16)
        return carry

    lax.fori_loop(0, out_ref.shape[0] // ROW_TILE, one, 0)


def gathered_dot(place, pieces, weight, residual=None):
    rows = pieces[0].shape[0]
    extra = [] if residual is None else [residual]
    return pl.pallas_call(
        functools.partial(gathered_kernel, residual is None),
        out_shape=jax.ShapeDtypeStruct((rows, WIDTH), jnp.bfloat16),
        in_specs=[SMEM] + [VMEM] * (NX * NC + 1 + len(extra)),
        out_specs=VMEM,
        compiler_params=pltpu.CompilerParams(vmem_limit_bytes=16 * 1024 * 1024),
        cost_estimate=pl.CostEstimate(
            flops=2 * rows * WIDTH * WIDTH * NX * NC,
            bytes_accessed=2 * WIDTH * (rows + WIDTH) * NX * NC,
            transcendentals=0,
        ),
    )(place, *pieces, weight, *extra)


def gather_pieces(own, before=()):
    up = [(2 * x, 2 * ((x + 1) % NX)) for x in range(NX)]
    down = [(2 * x + 1, 2 * ((x - 1) % NX) + 1) for x in range(NX)]
    swap = [(i, i ^ 1) for i in range(NX * NC)]
    held = [own]
    for step in range(NX - 1):
        if step < len(before):
            held[-1] = tie(held[-1], *before[step])
        held.append(lax.ppermute(held[-1], STORE, up + down))
    return held + [lax.ppermute(piece, STORE, swap) for piece in held]


def piece_places():
    x, core = lax.axis_index("x"), lax.axis_index("core")
    step = 1 - 2 * core
    away = jnp.arange(NX, dtype=jnp.int32) * step
    mine = ((x - away) % NX) * NC + core
    others = ((x + away) % NX) * NC + 1 - core
    return jnp.concatenate([mine, others]).astype(jnp.int32)


def column_kernel(w_ref, out_ref):
    out_ref[...] = w_ref[...]


def column_blocks(weight):
    return pl.pallas_call(
        column_kernel,
        out_shape=jax.ShapeDtypeStruct((NX * NC * WIDTH, WIDTH), weight.dtype),
        grid=(NX * NC,),
        in_specs=[pl.BlockSpec((WIDTH, WIDTH), lambda k: (0, k))],
        out_specs=pl.BlockSpec((WIDTH, WIDTH), lambda k: (k, 0)),
        cost_estimate=pl.CostEstimate(
            flops=0, bytes_accessed=4 * NX * NC * WIDTH * WIDTH, transcendentals=0
        ),
    )(weight)


def tie(array, *after):
    return lax.optimization_barrier((array, *after))[0]


def tie_all(arrays, *after):
    return list(lax.optimization_barrier((*arrays, *after))[: len(arrays)])


def on_device(hidden, nbr_shard, nbr_block, seq_lengths, kv_store, w_query, w_out):
    rows = hidden.shape[0]
    my_y, my_z = lax.axis_index("y"), lax.axis_index("z")
    seq_at = my_y * NZ + my_z
    order = [(i, i - 1) for i in range(1, NY * NZ)]
    edge = lax.ppermute(hidden[: SPAN - 1], SEQ, order)
    attending = jnp.concatenate([hidden[SPAN - 1 :], edge], axis=0)
    place = piece_places()

    wanted = (nbr_shard * BLK_DEV + nbr_block).reshape(-1)
    for by in (1, 2, 4):
        wanted = jnp.concatenate([wanted, ring(wanted, "z", NZ, -by)])
    shard, block = wanted // BLK_DEV, wanted % BLK_DEV
    local = jnp.where(shard % NZ == my_z, shard // NZ * BLK_DEV + block, -1).astype(jnp.int32)
    span_index = seq_at * SPANS_DEV + jnp.arange(SPANS_DEV, dtype=jnp.int32)
    upto = jnp.arange(seq_lengths.shape[0])
    seq_ends = jnp.sum(jnp.where(upto[None, :] <= upto[:, None], seq_lengths[None, :], 0), axis=1)
    boundary = jnp.any(seq_ends[None, :] == span_index[:, None] + 1, axis=1)
    boundary = boundary.astype(jnp.int32)

    own = kv_store.reshape(BLK_DEV, NBR_LEN, 2 * WIDTH)
    kv = lax.all_gather(own, "y", axis=0, tiled=True)

    parts = [attending[first * SPAN : last * SPAN] for first, last in CHUNKS]
    columns = column_blocks(w_out)
    before = [[(), (local, boundary), (columns,)], ()]
    queries = [
        gathered_dot(place, gather_pieces(part, when), w_query)
        for part, when in zip(parts, before)
    ]
    w_cols = tie(columns, *queries)
    w_cols = lax.all_to_all(w_cols, STORE, split_axis=0, concat_axis=0, tiled=True)

    count = len(CHUNKS)
    fwd, bwd = [[q] for q in queries], [[q] for q in queries]
    for _ in range(3):
        for c in range(count):
            fwd[c].append(ring(fwd[c][-1], "z", NZ, 1))
            bwd[c].append(ring(bwd[c][-1], "z", NZ, -1))
    cuts = [(last - first) // 2 for first, last in CHUNKS]
    far = [
        (ring(fwd[c][3][: cuts[c] * SPAN], "z", NZ, 1), ring(bwd[c][3][cuts[c] * SPAN :], "z", NZ, -1))
        for c in range(count)
    ]

    state = [None] * count
    sent = None
    for s in (4, 3, 2, 1, 0):
        for c, (first, last) in enumerate(CHUNKS):
            spans, split = last - first, cuts[c]

            def base(distance, start=0):
                return ((distance % NZ) * SPANS_DEV + first + start) * NBR

            if s == 4:
                top, low = far[c]
                if sent is not None:
                    top, low = tie_all([top, low], *sent)
                ways = [
                    (base(4), split, 0, 0, top, None),
                    (base(4, split), spans - split, 0, 0, low, None),
                ]
            else:
                if s == 2 and c == 0:
                    sent = [*sent, w_cols]
                top, low = tie_all(state[c], *sent)
                starts, helds = ((0, split), (split, spans - split)) if s == 3 else ((0, 0), (spans, spans))
                ways = [
                    (base(s), spans, starts[0], helds[0], bwd[c][s], top),
                    (base(-s), spans, starts[1], helds[1], fwd[c][s], low),
                ]
            if s:
                sent = relay(local, kv, ways)
                state[c] = [ring(sent[0], "z", NZ, 1), ring(sent[1], "z", NZ, -1)]
            else:
                state[c] = finish(
                    local, boundary, kv, base(0), spans, first, queries[c], top, low
                )
                sent = [state[c]]

    outs = {}
    for c, (first, last) in enumerate(CHUNKS):
        outs[first] = gathered_dot(place, gather_pieces(state[c]), w_cols, parts[c])
    result = jnp.concatenate([outs[first] for first in sorted(outs)], axis=0)
    order = [(i, i + 1) for i in range(NY * NZ - 1)]
    head = lax.ppermute(result[rows - (SPAN - 1) :], SEQ, order)
    head = jnp.where(seq_at == 0, hidden[: SPAN - 1], head)
    return jnp.concatenate([head, result[: rows - (SPAN - 1)]], axis=0)


def solution(mesh):
    fine = Mesh(mesh.devices.reshape(NY, NZ, NX, NC), ("y", "z", "x", "core"))
    return jax.shard_map(
        on_device,
        mesh=fine,
        in_specs=(
            P(SEQ, STORE),
            P(SEQ, None),
            P(SEQ, None),
            P(),
            P(SEQ, None, None, STORE),
            P(None, STORE),
            P(STORE, None),
        ),
        out_specs=P(SEQ, STORE),
        check_vma=False,
    )
```

```python
import functools
import jax
import jax.numpy as jnp
from jax import lax
from jax.experimental import pallas as pl
from jax.experimental.pallas import tpu as pltpu
from jax.sharding import Mesh, PartitionSpec as P

HEAD_DIM = 128
SPAN = 64
NBR = 2
NBR_LEN = 128
HEADS = 4
WIDTH = HEADS * HEAD_DIM
BLK_DEV = 8
NY, NZ, NX, NC = 4, 8, 4, 2
SEQ, STORE = ("y", "z"), ("x", "core")
ALL, EARLY = NX * NC, NX * NC - 2
SPANS_DEV = 12
CHUNKS = ((6, 12), (0, 6))
STAT_ROWS = 16
FAR = -1e30
SCALE = HEAD_DIM**-0.5 * 1.4426950408889634
LANES = 128


def ring(array, axis, size, by):
    return lax.ppermute(array, axis, [(i, (i + by) % size) for i in range(size)])


def lane_rows(rows):
    return -(-rows // LANES) * LANES


def load_state(state_ref, out_ref, stat_ref, first, rows):
    out_ref[pl.ds(first, rows), :] = state_ref[pl.ds(0, rows), :]
    wide = lane_rows(rows)
    packed = state_ref[pl.ds(rows, STAT_ROWS), pl.ds(0, wide)].astype(jnp.float32)
    parts = jnp.concatenate([packed, jnp.zeros((LANES - STAT_ROWS, wide), jnp.float32)], axis=0).T
    total = parts + pltpu.roll(parts, LANES - HEADS, 1) + pltpu.roll(parts, LANES - 2 * HEADS, 1)
    stat_ref[pl.ds(first, rows), :] = total[:rows]


def store_stats(stat_ref, out_ref, rows):
    wide = lane_rows(rows)
    lse = stat_ref[pl.ds(0, rows), :]
    if wide != rows:
        lse = jnp.concatenate([lse, jnp.zeros((wide - rows, LANES), jnp.float32)], axis=0)
    high = lse.astype(jnp.bfloat16).astype(jnp.float32)
    rest = lse - high
    middle = rest.astype(jnp.bfloat16).astype(jnp.float32)
    low = rest - middle
    lane = lax.broadcasted_iota(jnp.int32, lse.shape, 1)
    packed = jnp.where(
        lane < HEADS,
        high,
        jnp.where(lane < 2 * HEADS, pltpu.roll(middle, HEADS, 1), pltpu.roll(low, 2 * HEADS, 1)),
    )
    packed = jnp.where(lane < 3 * HEADS, packed, 0.0).T
    out_ref[pl.ds(rows, STAT_ROWS), pl.ds(0, wide)] = packed[:STAT_ROWS].astype(jnp.bfloat16)
    if wide < WIDTH:
        out_ref[pl.ds(rows, STAT_ROWS), pl.ds(wide, WIDTH - wide)] = jnp.zeros(
            (STAT_ROWS, WIDTH - wide), jnp.bfloat16
        )


def merge(old, new):
    best = jnp.maximum(old, new)
    old_part = jnp.exp2(old - best)
    new_part = jnp.exp2(new - best)
    both = old_part + new_part
    scale = 1.0 / both
    return old_part * scale, new_part * scale, best + jnp.log2(both)


def attend(q_ref, q_row, block, out_ref, stat_ref, row):
    at = pl.ds(row, SPAN)
    lane = lax.broadcasted_iota(jnp.int32, (SPAN, LANES), 1)
    queries = q_ref[pl.ds(q_row, SPAN), :]
    old = out_ref[at, :].astype(jnp.float32)
    old_lse = stat_ref[at, :]
    heads = [slice(head * HEAD_DIM, (head + 1) * HEAD_DIM) for head in range(HEADS)]
    scores = [
        lax.dot_general(
            queries[:, cols], block[:, cols], (((1,), (1,)), ((), ())),
            preferred_element_type=jnp.float32,
        )
        for cols in heads
    ]
    peaks = [jnp.max(score, axis=-1, keepdims=True) for score in scores]
    weights = [jnp.exp2((score - peak) * SCALE) for score, peak in zip(scores, peaks)]
    totals = [jnp.sum(weight, axis=-1, keepdims=True) for weight in weights]
    mixed = [
        jnp.dot(
            weight.astype(jnp.bfloat16),
            block[:, WIDTH + cols.start : WIDTH + cols.stop],
            preferred_element_type=jnp.float32,
        )
        for weight, cols in zip(weights, heads)
    ]
    peak_tile = jnp.zeros((SPAN, LANES), jnp.float32)
    total_tile = jnp.ones((SPAN, LANES), jnp.float32)
    for head in range(HEADS):
        peak_tile = jnp.where(lane == head, peaks[head], peak_tile)
        total_tile = jnp.where(lane == head, totals[head], total_tile)
    old_weight, new_weight, lse = merge(old_lse, peak_tile * SCALE + jnp.log2(total_tile))
    new_weight = new_weight / total_tile
    outs = [
        old[:, cols] * old_weight[:, head : head + 1] + mixed[head] * new_weight[:, head : head + 1]
        for head, cols in enumerate(heads)
    ]
    stat_ref[at, :] = lse
    for cols, out in zip(heads, outs):
        out_ref[at, cols] = out.astype(jnp.bfloat16)


def start_blocks(ids_ref, base, spans, kv_ref, buf_ref, sems, slot0):
    def one(i, carry):
        block = ids_ref[base + i]

        @pl.when(block >= 0)
        def _():
            pltpu.make_async_copy(
                kv_ref.at[block], buf_ref.at[slot0 + i], sems.at[slot0 + i]
            ).start()

        return carry

    lax.fori_loop(0, spans * NBR, one, 0)


def attend_blocks(ids_ref, base, spans, q_ref, kv_ref, buf_ref, sems, slot0, out_ref, stat_ref):
    def one(i, carry):
        block = ids_ref[base + i]

        @pl.when(block >= 0)
        def _():
            pltpu.make_async_copy(
                kv_ref.at[0], buf_ref.at[slot0 + i], sems.at[slot0 + i]
            ).wait()
            row = pl.multiple_of((i // NBR) * SPAN, SPAN)
            attend(q_ref, row, buf_ref.at[slot0 + i], out_ref, stat_ref, row)

        return carry

    lax.fori_loop(0, spans * NBR, one, 0)


def relay_kernel(ways, *refs):
    ids_ref, kv_ref = refs[:2]
    refs = refs[2:]
    plan = []
    for base, spans, begin, held in ways:
        q_ref, refs = refs[0], refs[1:]
        state_ref = None
        if held:
            state_ref, refs = refs[0], refs[1:]
        plan.append([base, spans, begin, held, q_ref, state_ref])
    outs, refs = refs[: len(ways)], refs[len(ways) :]
    buf_ref, sems = refs[:2]
    stats = refs[2:]
    slot0 = 0
    for base, spans, *_ in plan:
        start_blocks(ids_ref, base, spans, kv_ref, buf_ref, sems, slot0)
        slot0 += spans * NBR
    slot0 = 0
    for (base, spans, begin, held, q_ref, state_ref), out_ref, stat_ref in zip(plan, outs, stats):
        rows = spans * SPAN
        if held != spans:
            out_ref[pl.ds(0, rows), :] = jnp.zeros((rows, WIDTH), jnp.bfloat16)
            stat_ref[...] = jnp.full((rows, LANES), FAR, jnp.float32)
        if held:
            load_state(state_ref, out_ref, stat_ref, begin * SPAN, held * SPAN)
        attend_blocks(
            ids_ref, base, spans, q_ref, kv_ref, buf_ref, sems, slot0, out_ref, stat_ref
        )
        store_stats(stat_ref, out_ref, rows)
        slot0 += spans * NBR


def final_kernel(base, spans, mask_base, ids_ref, edge_ref, kv_ref, *refs):
    q_ref, fwd_ref, bwd_ref, out_ref, buf_ref, sems, stat_ref, other_ref, other_stat = refs
    rows = spans * SPAN
    start_blocks(ids_ref, base, spans, kv_ref, buf_ref, sems, 0)
    load_state(fwd_ref, out_ref, stat_ref, 0, rows)
    load_state(bwd_ref, other_ref, other_stat, 0, rows)
    weight, other_weight, lse = merge(stat_ref[...], other_stat[...])
    stat_ref[...] = lse
    for head in range(HEADS):
        cols = slice(head * HEAD_DIM, (head + 1) * HEAD_DIM)
        out_ref[:, cols] = (
            out_ref[:, cols].astype(jnp.float32) * weight[:, head : head + 1]
            + other_ref[:, cols].astype(jnp.float32) * other_weight[:, head : head + 1]
        ).astype(jnp.bfloat16)
    attend_blocks(ids_ref, base, spans, q_ref, kv_ref, buf_ref, sems, 0, out_ref, stat_ref)

    def cut(i, carry):
        @pl.when(edge_ref[mask_base + i] > 0)
        def _():
            at = pl.ds(pl.multiple_of(i * SPAN, SPAN), SPAN)
            kept = lax.broadcasted_iota(jnp.int32, (SPAN, WIDTH), 0) == 0
            out_ref[at, :] = jnp.where(kept, out_ref[at, :], jnp.zeros((SPAN, WIDTH), jnp.bfloat16))

        return carry

    lax.fori_loop(0, spans, cut, 0)


SMEM = pl.BlockSpec(memory_space=pltpu.SMEM)
VMEM = pl.BlockSpec(memory_space=pltpu.VMEM)
HBM = pl.BlockSpec(memory_space=pltpu.HBM)


def cost(pairs, rows):
    return pl.CostEstimate(
        flops=pairs * HEADS * 4 * SPAN * HEAD_DIM * NBR_LEN,
        bytes_accessed=pairs * NBR_LEN * 4 * WIDTH + rows * WIDTH * 8,
        transcendentals=pairs * HEADS * SPAN * NBR_LEN,
    )


def relay(ids, kv, ways):
    specs = [w[:4] for w in ways]
    operands = [ids, kv]
    for base, spans, begin, held, queries, state in ways:
        operands.append(queries)
        if held:
            operands.append(state)
    total = sum(spans for _, spans, _, _ in specs)
    return pl.pallas_call(
        functools.partial(relay_kernel, specs),
        out_shape=[
            jax.ShapeDtypeStruct((spans * SPAN + STAT_ROWS, WIDTH), jnp.bfloat16)
            for _, spans, _, _ in specs
        ],
        in_specs=[SMEM, HBM] + [VMEM] * (len(operands) - 2),
        out_specs=[VMEM] * len(specs),
        scratch_shapes=[
            pltpu.VMEM((total * NBR, NBR_LEN, 2 * WIDTH), jnp.bfloat16),
            pltpu.SemaphoreType.DMA((total * NBR,)),
        ]
        + [pltpu.VMEM((spans * SPAN, LANES), jnp.float32) for _, spans, _, _ in specs],
        compiler_params=pltpu.CompilerParams(vmem_limit_bytes=12 * 1024 * 1024),
        cost_estimate=cost(6, total * SPAN),
    )(*operands)


def finish(ids, edges, kv, base, spans, mask_base, queries, fwd, bwd):
    rows = spans * SPAN
    return pl.pallas_call(
        functools.partial(final_kernel, base, spans, mask_base),
        out_shape=jax.ShapeDtypeStruct((rows, WIDTH), jnp.bfloat16),
        in_specs=[SMEM, SMEM, HBM] + [VMEM] * 3,
        out_specs=VMEM,
        scratch_shapes=[
            pltpu.VMEM((spans * NBR, NBR_LEN, 2 * WIDTH), jnp.bfloat16),
            pltpu.SemaphoreType.DMA((spans * NBR,)),
            pltpu.VMEM((rows, LANES), jnp.float32),
            pltpu.VMEM((rows, WIDTH), jnp.bfloat16),
            pltpu.VMEM((rows, LANES), jnp.float32),
        ],
        compiler_params=pltpu.CompilerParams(vmem_limit_bytes=12 * 1024 * 1024),
        cost_estimate=cost(3, rows),
    )(ids, edges, kv, queries, fwd, bwd)


def add_pieces(place_ref, first, pieces, weight_ref, total):
    for i, piece_ref in enumerate(pieces):
        block = pl.ds(pl.multiple_of(place_ref[first + i] * WIDTH, WIDTH), WIDTH)
        term = jnp.dot(piece_ref[...], weight_ref[block, :], preferred_element_type=jnp.float32)
        total = term if total is None else total + term
    return total


def add_squares(pieces, squares):
    for piece_ref in pieces:
        for k in range(HEADS):
            wide = piece_ref[:, k * LANES : (k + 1) * LANES].astype(jnp.float32)
            squares = wide * wide if squares is None else squares + wide * wide
    return squares


def early_kernel(norm, place_ref, *refs):
    pieces, refs = refs[:EARLY], refs[EARLY:]
    weight_ref, refs = refs[0], refs[1:]
    if norm:
        total_ref, square_ref = refs
        square_ref[...] = add_squares(pieces, None)
        total_ref[...] = add_pieces(place_ref, 0, pieces, weight_ref, None)
    else:
        residual_ref, total_ref = refs
        total_ref[...] = add_pieces(
            place_ref, 0, pieces, weight_ref, residual_ref[...].astype(jnp.float32)
        )


def late_kernel(norm, place_ref, *refs):
    pieces, refs = refs[: ALL - EARLY], refs[ALL - EARLY :]
    weight_ref, total_ref = refs[:2]
    total = add_pieces(place_ref, EARLY, pieces, weight_ref, total_ref[...])
    if norm:
        squares = jnp.sum(add_squares(pieces, refs[2][...]), axis=-1, keepdims=True)
        total = total * lax.rsqrt(squares * (1.0 / (WIDTH * ALL)) + 1e-05)
    refs[-1][...] = total.astype(jnp.bfloat16)


def gathered_cost(rows, count):
    return pl.CostEstimate(
        flops=2 * rows * WIDTH * WIDTH * count,
        bytes_accessed=2 * WIDTH * (rows + WIDTH) * count + 4 * rows * WIDTH,
        transcendentals=0,
    )


def gathered_dot(place, pieces, weight, residual=None):
    rows = pieces[0].shape[0]
    norm = residual is None
    pieces = [pieces[r + other] for r in range(NX) for other in (0, NX)]
    params = pltpu.CompilerParams(vmem_limit_bytes=14 * 1024 * 1024)
    total = jax.ShapeDtypeStruct((rows, WIDTH), jnp.float32)
    squares = jax.ShapeDtypeStruct((rows, LANES), jnp.float32)
    partial = pl.pallas_call(
        functools.partial(early_kernel, norm),
        out_shape=[total, squares] if norm else [total],
        in_specs=[SMEM] + [VMEM] * (EARLY + 1 + (not norm)),
        out_specs=[VMEM] * (1 + norm),
        compiler_params=params,
        cost_estimate=gathered_cost(rows, EARLY),
    )(place, *pieces[:EARLY], weight, *([] if norm else [residual]))
    return pl.pallas_call(
        functools.partial(late_kernel, norm),
        out_shape=jax.ShapeDtypeStruct((rows, WIDTH), jnp.bfloat16),
        in_specs=[SMEM] + [VMEM] * (ALL - EARLY + 2 + norm),
        out_specs=VMEM,
        compiler_params=params,
        cost_estimate=gathered_cost(rows, ALL - EARLY),
    )(place, *pieces[EARLY:], weight, *partial)


def gather_pieces(own, before=((), (), ()), last=()):
    up = [(2 * x, 2 * ((x + 1) % NX)) for x in range(NX)]
    down = [(2 * x + 1, 2 * ((x - 1) % NX) + 1) for x in range(NX)]
    swap = [(i, i ^ 1) for i in range(NX * NC)]
    held = [own]
    for after in before:
        held.append(lax.ppermute(tie(held[-1], *after), STORE, up + down))
    others = [lax.ppermute(piece, STORE, swap) for piece in held[:-1]]
    return held + others + [lax.ppermute(tie(held[-1], *last), STORE, swap)]


def piece_places():
    x, core = lax.axis_index("x"), lax.axis_index("core")
    step = 1 - 2 * core
    away = jnp.arange(NX, dtype=jnp.int32) * step
    mine = ((x - away) % NX) * NC + core
    others = ((x + away) % NX) * NC + 1 - core
    return jnp.stack([mine, others], axis=1).reshape(-1).astype(jnp.int32)


def column_kernel(w_ref, out_ref):
    out_ref[...] = w_ref[...]


def column_blocks(weight):
    return pl.pallas_call(
        column_kernel,
        out_shape=jax.ShapeDtypeStruct((NX * NC * WIDTH, WIDTH), weight.dtype),
        grid=(NX * NC,),
        in_specs=[pl.BlockSpec((WIDTH, WIDTH), lambda k: (0, k))],
        out_specs=pl.BlockSpec((WIDTH, WIDTH), lambda k: (k, 0)),
        compiler_params=pltpu.CompilerParams(vmem_limit_bytes=4 * 1024 * 1024),
        cost_estimate=pl.CostEstimate(
            flops=0, bytes_accessed=4 * NX * NC * WIDTH * WIDTH, transcendentals=0
        ),
    )(weight)


def tie(array, *after):
    return lax.optimization_barrier((array, *after))[0]


def tie_all(arrays, *after):
    return list(lax.optimization_barrier((*arrays, *after))[: len(arrays)])


def on_device(hidden, nbr_shard, nbr_block, seq_lengths, kv_store, w_query, w_out):
    rows = hidden.shape[0]
    my_y, my_z = lax.axis_index("y"), lax.axis_index("z")
    seq_at = my_y * NZ + my_z
    order = [(i, i - 1) for i in range(1, NY * NZ)]
    edge = lax.ppermute(hidden[: SPAN - 1], SEQ, order)
    attending = jnp.concatenate([hidden[SPAN - 1 :], edge], axis=0)
    place = piece_places()

    wanted = (nbr_shard * BLK_DEV + nbr_block).reshape(-1)
    for by in (1, 2, 4):
        wanted = jnp.concatenate([wanted, ring(wanted, "z", NZ, -by)])
    shard, block = wanted // BLK_DEV, wanted % BLK_DEV
    local = jnp.where(shard % NZ == my_z, shard // NZ * BLK_DEV + block, -1).astype(jnp.int32)
    span_index = seq_at * SPANS_DEV + jnp.arange(SPANS_DEV, dtype=jnp.int32)
    upto = jnp.arange(seq_lengths.shape[0])
    seq_ends = jnp.sum(jnp.where(upto[None, :] <= upto[:, None], seq_lengths[None, :], 0), axis=1)
    boundary = jnp.any(seq_ends[None, :] == span_index[:, None] + 1, axis=1)
    boundary = boundary.astype(jnp.int32)

    parts = [attending[first * SPAN : last * SPAN] for first, last in CHUNKS]

    own = tie(kv_store, parts[1]).reshape(BLK_DEV, NBR_LEN, 2 * WIDTH)
    kv = lax.all_gather(own, "y", axis=0, tiled=True)
    kv = pltpu.with_memory_space_constraint(kv, pltpu.HBM)

    pieces = gather_pieces(parts[0], [(), (local, boundary), ()])
    queries = [gathered_dot(place, pieces, w_query)]
    pieces = gather_pieces(
        parts[1], [(), (pieces[1],), (pieces[2],)], (queries[0],)
    )
    queries.append(gathered_dot(place, pieces, w_query))

    count = len(CHUNKS)
    fwd, bwd = [[q] for q in queries], [[q] for q in queries]
    columns = column_blocks(tie(w_out, queries[1]))
    for step in range(3):
        for c in range(count):
            if step == 2 and c == 0:
                fwd[c][-1] = tie(fwd[c][-1], columns)
            fwd[c].append(ring(fwd[c][-1], "z", NZ, 1))
            bwd[c].append(ring(bwd[c][-1], "z", NZ, -1))
    w_cols = lax.all_to_all(columns, STORE, split_axis=0, concat_axis=0, tiled=True)
    cuts = [(last - first) // 2 for first, last in CHUNKS]
    far = [
        (ring(fwd[c][3][: cuts[c] * SPAN], "z", NZ, 1), ring(bwd[c][3][cuts[c] * SPAN :], "z", NZ, -1))
        for c in range(count)
    ]

    state = [None] * count
    sent = None
    for s in (4, 3, 2, 1, 0):
        for c, (first, last) in enumerate(CHUNKS):
            spans, split = last - first, cuts[c]

            def base(distance, start=0):
                return ((distance % NZ) * SPANS_DEV + first + start) * NBR

            if s == 4:
                top, low = far[c]
                if sent is not None:
                    top, low = tie_all([top, low], *sent)
                ways = [
                    (base(4), split, 0, 0, top, None),
                    (base(4, split), spans - split, 0, 0, low, None),
                ]
            else:
                if s == 2 and c == 0:
                    sent = [*sent, w_cols]
                top, low = tie_all(state[c], *sent)
                starts, helds = ((0, split), (split, spans - split)) if s == 3 else ((0, 0), (spans, spans))
                ways = [
                    (base(s), spans, starts[0], helds[0], bwd[c][s], top),
                    (base(-s), spans, starts[1], helds[1], fwd[c][s], low),
                ]
            if s:
                sent = relay(local, kv, ways)
                state[c] = [ring(sent[0], "z", NZ, 1), ring(sent[1], "z", NZ, -1)]
            else:
                state[c] = finish(
                    local, boundary, kv, base(0), spans, first, queries[c], top, low
                )
                sent = [state[c]]

    outs, done = {}, ()
    for c, (first, last) in enumerate(CHUNKS):
        pieces = gather_pieces(state[c], last=done)
        outs[first] = gathered_dot(place, pieces, w_cols, parts[c])
        done = (outs[first],)
    result = jnp.concatenate([outs[first] for first in sorted(outs)], axis=0)
    order = [(i, i + 1) for i in range(NY * NZ - 1)]
    head = lax.ppermute(result[rows - (SPAN - 1) :], SEQ, order)
    head = jnp.where(seq_at == 0, hidden[: SPAN - 1], head)
    return jnp.concatenate([head, result[: rows - (SPAN - 1)]], axis=0)


def solution(mesh):
    fine = Mesh(mesh.devices.reshape(NY, NZ, NX, NC), ("y", "z", "x", "core"))
    return jax.shard_map(
        on_device,
        mesh=fine,
        in_specs=(
            P(SEQ, STORE),
            P(SEQ, None),
            P(SEQ, None),
            P(),
            P(SEQ, None, None, STORE),
            P(None, STORE),
            P(STORE, None),
        ),
        out_specs=P(SEQ, STORE),
        check_vma=False,
    )
```

```python
import functools
import jax
import jax.numpy as jnp
from jax import lax
from jax.experimental import pallas as pl
from jax.experimental.pallas import tpu as pltpu
from jax.sharding import Mesh, PartitionSpec as P

HEAD_DIM = 128
SPAN = 64
NBR = 2
NBR_LEN = 128
HEADS = 4
WIDTH = HEADS * HEAD_DIM
BLK_DEV = 8
NY, NZ, NX, NC = 4, 8, 4, 2
SEQ, STORE = ("y", "z"), ("x", "core")
ALL, EARLY = NX * NC, NX * NC - 2
SPANS_DEV = 12
CHUNKS = ((6, 12), (0, 6))
ORDER = ((0, 4), (0, 3), (1, 4), (0, 2), (1, 3), (0, 1), (1, 2), (0, 0), (1, 1), (1, 0))
STAT_ROWS = 16
FAR = -1e30
SCALE = HEAD_DIM**-0.5 * 1.4426950408889634
LANES = 128


def ring(array, axis, size, by):
    return lax.ppermute(array, axis, [(i, (i + by) % size) for i in range(size)])


def lane_rows(rows):
    return -(-rows // LANES) * LANES


def load_state(state_ref, out_ref, stat_ref, first, rows):
    out_ref[pl.ds(first, rows), :] = state_ref[pl.ds(0, rows), :]
    wide = lane_rows(rows)
    packed = state_ref[pl.ds(rows, STAT_ROWS), pl.ds(0, wide)].astype(jnp.float32)
    parts = jnp.concatenate([packed, jnp.zeros((LANES - STAT_ROWS, wide), jnp.float32)], axis=0).T
    total = parts + pltpu.roll(parts, LANES - HEADS, 1) + pltpu.roll(parts, LANES - 2 * HEADS, 1)
    stat_ref[pl.ds(first, rows), :] = total[:rows]


def store_stats(stat_ref, out_ref, rows):
    wide = lane_rows(rows)
    lse = stat_ref[pl.ds(0, rows), :]
    if wide != rows:
        lse = jnp.concatenate([lse, jnp.zeros((wide - rows, LANES), jnp.float32)], axis=0)
    high = lse.astype(jnp.bfloat16).astype(jnp.float32)
    rest = lse - high
    middle = rest.astype(jnp.bfloat16).astype(jnp.float32)
    low = rest - middle
    lane = lax.broadcasted_iota(jnp.int32, lse.shape, 1)
    packed = jnp.where(
        lane < HEADS,
        high,
        jnp.where(lane < 2 * HEADS, pltpu.roll(middle, HEADS, 1), pltpu.roll(low, 2 * HEADS, 1)),
    )
    packed = jnp.where(lane < 3 * HEADS, packed, 0.0).T
    out_ref[pl.ds(rows, STAT_ROWS), pl.ds(0, wide)] = packed[:STAT_ROWS].astype(jnp.bfloat16)
    if wide < WIDTH:
        out_ref[pl.ds(rows, STAT_ROWS), pl.ds(wide, WIDTH - wide)] = jnp.zeros(
            (STAT_ROWS, WIDTH - wide), jnp.bfloat16
        )


def merge(old, new):
    best = jnp.maximum(old, new)
    old_part = jnp.exp2(old - best)
    new_part = jnp.exp2(new - best)
    both = old_part + new_part
    scale = 1.0 / both
    return old_part * scale, new_part * scale, best + jnp.log2(both)


def attend(q_ref, q_row, block, out_ref, stat_ref, row):
    at = pl.ds(row, SPAN)
    lane = lax.broadcasted_iota(jnp.int32, (SPAN, LANES), 1)
    queries = q_ref[pl.ds(q_row, SPAN), :]
    old = out_ref[at, :].astype(jnp.float32)
    old_lse = stat_ref[at, :]
    heads = [slice(head * HEAD_DIM, (head + 1) * HEAD_DIM) for head in range(HEADS)]
    scores = [
        lax.dot_general(
            queries[:, cols], block[:, cols], (((1,), (1,)), ((), ())),
            preferred_element_type=jnp.float32,
        )
        for cols in heads
    ]
    peaks = [jnp.max(score, axis=-1, keepdims=True) for score in scores]
    weights = [jnp.exp2((score - peak) * SCALE) for score, peak in zip(scores, peaks)]
    totals = [jnp.sum(weight, axis=-1, keepdims=True) for weight in weights]
    mixed = [
        jnp.dot(
            weight.astype(jnp.bfloat16),
            block[:, WIDTH + cols.start : WIDTH + cols.stop],
            preferred_element_type=jnp.float32,
        )
        for weight, cols in zip(weights, heads)
    ]
    peak_tile = jnp.zeros((SPAN, LANES), jnp.float32)
    total_tile = jnp.ones((SPAN, LANES), jnp.float32)
    for head in range(HEADS):
        peak_tile = jnp.where(lane == head, peaks[head], peak_tile)
        total_tile = jnp.where(lane == head, totals[head], total_tile)
    old_weight, new_weight, lse = merge(old_lse, peak_tile * SCALE + jnp.log2(total_tile))
    new_weight = new_weight / total_tile
    outs = [
        old[:, cols] * old_weight[:, head : head + 1] + mixed[head] * new_weight[:, head : head + 1]
        for head, cols in enumerate(heads)
    ]
    stat_ref[at, :] = lse
    for cols, out in zip(heads, outs):
        out_ref[at, cols] = out.astype(jnp.bfloat16)


def start_blocks(ids_ref, base, spans, kv_ref, buf_ref, sems, slot0):
    def one(i, carry):
        block = ids_ref[base + i]

        @pl.when(block >= 0)
        def _():
            pltpu.make_async_copy(
                kv_ref.at[block], buf_ref.at[slot0 + i], sems.at[slot0 + i]
            ).start()

        return carry

    lax.fori_loop(0, spans * NBR, one, 0)


def attend_blocks(ids_ref, base, spans, q_ref, kv_ref, buf_ref, sems, slot0, out_ref, stat_ref):
    def one(i, carry):
        block = ids_ref[base + i]

        @pl.when(block >= 0)
        def _():
            pltpu.make_async_copy(
                kv_ref.at[0], buf_ref.at[slot0 + i], sems.at[slot0 + i]
            ).wait()
            row = pl.multiple_of((i // NBR) * SPAN, SPAN)
            attend(q_ref, row, buf_ref.at[slot0 + i], out_ref, stat_ref, row)

        return carry

    lax.fori_loop(0, spans * NBR, one, 0)


def relay_kernel(ways, *refs):
    ids_ref, kv_ref = refs[:2]
    refs = refs[2:]
    plan = []
    for base, spans, begin, held in ways:
        q_ref, refs = refs[0], refs[1:]
        state_ref = None
        if held:
            state_ref, refs = refs[0], refs[1:]
        plan.append([base, spans, begin, held, q_ref, state_ref])
    outs, refs = refs[: len(ways)], refs[len(ways) :]
    buf_ref, sems = refs[:2]
    stats = refs[2:]
    slot0 = 0
    for base, spans, *_ in plan:
        start_blocks(ids_ref, base, spans, kv_ref, buf_ref, sems, slot0)
        slot0 += spans * NBR
    slot0 = 0
    for (base, spans, begin, held, q_ref, state_ref), out_ref, stat_ref in zip(plan, outs, stats):
        rows = spans * SPAN
        if held != spans:
            out_ref[pl.ds(0, rows), :] = jnp.zeros((rows, WIDTH), jnp.bfloat16)
            stat_ref[...] = jnp.full((rows, LANES), FAR, jnp.float32)
        if held:
            load_state(state_ref, out_ref, stat_ref, begin * SPAN, held * SPAN)
        attend_blocks(
            ids_ref, base, spans, q_ref, kv_ref, buf_ref, sems, slot0, out_ref, stat_ref
        )
        store_stats(stat_ref, out_ref, rows)
        slot0 += spans * NBR


def final_kernel(base, spans, mask_base, ids_ref, edge_ref, kv_ref, *refs):
    q_ref, fwd_ref, bwd_ref, out_ref, buf_ref, sems, stat_ref, other_ref, other_stat = refs
    rows = spans * SPAN
    start_blocks(ids_ref, base, spans, kv_ref, buf_ref, sems, 0)
    load_state(fwd_ref, out_ref, stat_ref, 0, rows)
    load_state(bwd_ref, other_ref, other_stat, 0, rows)
    weight, other_weight, lse = merge(stat_ref[...], other_stat[...])
    stat_ref[...] = lse
    for head in range(HEADS):
        cols = slice(head * HEAD_DIM, (head + 1) * HEAD_DIM)
        out_ref[:, cols] = (
            out_ref[:, cols].astype(jnp.float32) * weight[:, head : head + 1]
            + other_ref[:, cols].astype(jnp.float32) * other_weight[:, head : head + 1]
        ).astype(jnp.bfloat16)
    attend_blocks(ids_ref, base, spans, q_ref, kv_ref, buf_ref, sems, 0, out_ref, stat_ref)

    def cut(i, carry):
        @pl.when(edge_ref[mask_base + i] > 0)
        def _():
            at = pl.ds(pl.multiple_of(i * SPAN, SPAN), SPAN)
            kept = lax.broadcasted_iota(jnp.int32, (SPAN, WIDTH), 0) == 0
            out_ref[at, :] = jnp.where(kept, out_ref[at, :], jnp.zeros((SPAN, WIDTH), jnp.bfloat16))

        return carry

    lax.fori_loop(0, spans, cut, 0)


SMEM = pl.BlockSpec(memory_space=pltpu.SMEM)
VMEM = pl.BlockSpec(memory_space=pltpu.VMEM)
HBM = pl.BlockSpec(memory_space=pltpu.HBM)


def cost(pairs, rows):
    return pl.CostEstimate(
        flops=pairs * HEADS * 4 * SPAN * HEAD_DIM * NBR_LEN,
        bytes_accessed=pairs * NBR_LEN * 4 * WIDTH + rows * WIDTH * 8,
        transcendentals=pairs * HEADS * SPAN * NBR_LEN,
    )


def relay(ids, kv, ways):
    specs = [w[:4] for w in ways]
    operands = [ids, kv]
    for base, spans, begin, held, queries, state in ways:
        operands.append(queries)
        if held:
            operands.append(state)
    total = sum(spans for _, spans, _, _ in specs)
    return pl.pallas_call(
        functools.partial(relay_kernel, specs),
        out_shape=[
            jax.ShapeDtypeStruct((spans * SPAN + STAT_ROWS, WIDTH), jnp.bfloat16)
            for _, spans, _, _ in specs
        ],
        in_specs=[SMEM, HBM] + [VMEM] * (len(operands) - 2),
        out_specs=[VMEM] * len(specs),
        scratch_shapes=[
            pltpu.VMEM((total * NBR, NBR_LEN, 2 * WIDTH), jnp.bfloat16),
            pltpu.SemaphoreType.DMA((total * NBR,)),
        ]
        + [pltpu.VMEM((spans * SPAN, LANES), jnp.float32) for _, spans, _, _ in specs],
        compiler_params=pltpu.CompilerParams(vmem_limit_bytes=12 * 1024 * 1024),
        cost_estimate=cost(6, total * SPAN),
    )(*operands)


def finish(ids, edges, kv, base, spans, mask_base, queries, fwd, bwd):
    rows = spans * SPAN
    return pl.pallas_call(
        functools.partial(final_kernel, base, spans, mask_base),
        out_shape=jax.ShapeDtypeStruct((rows, WIDTH), jnp.bfloat16),
        in_specs=[SMEM, SMEM, HBM] + [VMEM] * 3,
        out_specs=VMEM,
        scratch_shapes=[
            pltpu.VMEM((spans * NBR, NBR_LEN, 2 * WIDTH), jnp.bfloat16),
            pltpu.SemaphoreType.DMA((spans * NBR,)),
            pltpu.VMEM((rows, LANES), jnp.float32),
            pltpu.VMEM((rows, WIDTH), jnp.bfloat16),
            pltpu.VMEM((rows, LANES), jnp.float32),
        ],
        compiler_params=pltpu.CompilerParams(vmem_limit_bytes=12 * 1024 * 1024),
        cost_estimate=cost(3, rows),
    )(ids, edges, kv, queries, fwd, bwd)


def block_copies(place_ref, first, count, weight_ref, buf_ref, sems):
    copies = []
    for i in range(count):
        block = pl.ds(pl.multiple_of(place_ref[first + i] * WIDTH, WIDTH), WIDTH)
        copies.append(pltpu.make_async_copy(weight_ref.at[block], buf_ref.at[i], sems.at[i]))
        copies[-1].start()
    return copies


def add_pieces(copies, pieces, buf_ref, total):
    for i, piece_ref in enumerate(pieces):
        copies[i].wait()
        term = jnp.dot(piece_ref[...], buf_ref[i], preferred_element_type=jnp.float32)
        total = term if total is None else total + term
    return total


def add_squares(pieces, squares):
    for piece_ref in pieces:
        for k in range(HEADS):
            wide = piece_ref[:, k * LANES : (k + 1) * LANES].astype(jnp.float32)
            squares = wide * wide if squares is None else squares + wide * wide
    return squares


def early_kernel(norm, place_ref, weight_ref, *refs):
    pieces, refs = refs[:EARLY], refs[EARLY:]
    buf_ref, sems = refs[-2:]
    copies = block_copies(place_ref, 0, EARLY, weight_ref, buf_ref, sems)
    if norm:
        total_ref, square_ref = refs[:2]
        square_ref[...] = add_squares(pieces, None)
        total_ref[...] = add_pieces(copies, pieces, buf_ref, None)
    else:
        residual_ref, total_ref = refs[:2]
        total_ref[...] = add_pieces(
            copies, pieces, buf_ref, residual_ref[...].astype(jnp.float32)
        )


def late_kernel(norm, place_ref, weight_ref, *refs):
    pieces, refs = refs[: ALL - EARLY], refs[ALL - EARLY :]
    out_ref, buf_ref, sems = refs[-3:]
    copies = block_copies(place_ref, EARLY, ALL - EARLY, weight_ref, buf_ref, sems)
    total = add_pieces(copies, pieces, buf_ref, refs[0][...])
    if norm:
        squares = jnp.sum(add_squares(pieces, refs[1][...]), axis=-1, keepdims=True)
        total = total * lax.rsqrt(squares * (1.0 / (WIDTH * ALL)) + 1e-05)
    out_ref[...] = total.astype(jnp.bfloat16)


def gathered_cost(rows, count):
    return pl.CostEstimate(
        flops=2 * rows * WIDTH * WIDTH * count,
        bytes_accessed=2 * WIDTH * (rows + WIDTH) * count + 4 * rows * WIDTH,
        transcendentals=0,
    )


def gathered_dot(place, pieces, weight, residual=None):
    rows = pieces[0].shape[0]
    norm = residual is None
    pieces = [pieces[r + other] for r in range(NX) for other in (0, NX)]
    params = pltpu.CompilerParams(vmem_limit_bytes=14 * 1024 * 1024)
    total = jax.ShapeDtypeStruct((rows, WIDTH), jnp.float32)
    squares = jax.ShapeDtypeStruct((rows, LANES), jnp.float32)
    weight = pltpu.with_memory_space_constraint(weight, pltpu.HBM)

    def scratch(count):
        return [
            pltpu.VMEM((count, WIDTH, WIDTH), jnp.bfloat16),
            pltpu.SemaphoreType.DMA((count,)),
        ]

    partial = pl.pallas_call(
        functools.partial(early_kernel, norm),
        out_shape=[total, squares] if norm else [total],
        in_specs=[SMEM, HBM] + [VMEM] * (EARLY + (not norm)),
        out_specs=[VMEM] * (1 + norm),
        scratch_shapes=scratch(EARLY),
        compiler_params=params,
        cost_estimate=gathered_cost(rows, EARLY),
    )(place, weight, *pieces[:EARLY], *([] if norm else [residual]))
    return pl.pallas_call(
        functools.partial(late_kernel, norm),
        out_shape=jax.ShapeDtypeStruct((rows, WIDTH), jnp.bfloat16),
        in_specs=[SMEM, HBM] + [VMEM] * (ALL - EARLY + 1 + norm),
        out_specs=VMEM,
        scratch_shapes=scratch(ALL - EARLY),
        compiler_params=params,
        cost_estimate=gathered_cost(rows, ALL - EARLY),
    )(place, weight, *pieces[EARLY:], *partial)


def gather_pieces(own, before=((), (), ()), last=()):
    up = [(2 * x, 2 * ((x + 1) % NX)) for x in range(NX)]
    down = [(2 * x + 1, 2 * ((x - 1) % NX) + 1) for x in range(NX)]
    swap = [(i, i ^ 1) for i in range(NX * NC)]
    held = [own]
    for after in before:
        held.append(lax.ppermute(tie(held[-1], *after), STORE, up + down))
    others = [lax.ppermute(piece, STORE, swap) for piece in held[:-1]]
    return held + others + [lax.ppermute(tie(held[-1], *last), STORE, swap)]


def piece_places():
    x, core = lax.axis_index("x"), lax.axis_index("core")
    step = 1 - 2 * core
    away = jnp.arange(NX, dtype=jnp.int32) * step
    mine = ((x - away) % NX) * NC + core
    others = ((x + away) % NX) * NC + 1 - core
    return jnp.stack([mine, others], axis=1).reshape(-1).astype(jnp.int32)


def column_kernel(w_ref, out_ref):
    out_ref[...] = w_ref[...]


def column_blocks(weight):
    return pl.pallas_call(
        column_kernel,
        out_shape=jax.ShapeDtypeStruct((NX * NC * WIDTH, WIDTH), weight.dtype),
        grid=(NX * NC,),
        in_specs=[pl.BlockSpec((WIDTH, WIDTH), lambda k: (0, k))],
        out_specs=pl.BlockSpec((WIDTH, WIDTH), lambda k: (k, 0)),
        compiler_params=pltpu.CompilerParams(vmem_limit_bytes=4 * 1024 * 1024),
        cost_estimate=pl.CostEstimate(
            flops=0, bytes_accessed=4 * NX * NC * WIDTH * WIDTH, transcendentals=0
        ),
    )(weight)


def tie(array, *after):
    return lax.optimization_barrier((array, *after))[0]


def tie_all(arrays, *after):
    return list(lax.optimization_barrier((*arrays, *after))[: len(arrays)])


def on_device(hidden, nbr_shard, nbr_block, seq_lengths, kv_store, w_query, w_out):
    rows = hidden.shape[0]
    my_y, my_z = lax.axis_index("y"), lax.axis_index("z")
    seq_at = my_y * NZ + my_z
    order = [(i, i - 1) for i in range(1, NY * NZ)]
    edge = lax.ppermute(hidden[: SPAN - 1], SEQ, order)
    attending = jnp.concatenate([hidden[SPAN - 1 :], edge], axis=0)
    place = piece_places()

    wanted = (nbr_shard * BLK_DEV + nbr_block).reshape(-1)
    for by in (1, 2, 4):
        wanted = jnp.concatenate([wanted, ring(wanted, "z", NZ, -by)])
    shard, block = wanted // BLK_DEV, wanted % BLK_DEV
    local = jnp.where(shard % NZ == my_z, shard // NZ * BLK_DEV + block, -1).astype(jnp.int32)
    span_index = seq_at * SPANS_DEV + jnp.arange(SPANS_DEV, dtype=jnp.int32)
    upto = jnp.arange(seq_lengths.shape[0])
    seq_ends = jnp.sum(jnp.where(upto[None, :] <= upto[:, None], seq_lengths[None, :], 0), axis=1)
    boundary = jnp.any(seq_ends[None, :] == span_index[:, None] + 1, axis=1)
    boundary = boundary.astype(jnp.int32)

    parts = [attending[first * SPAN : last * SPAN] for first, last in CHUNKS]

    own = tie(kv_store, parts[1]).reshape(BLK_DEV, NBR_LEN, 2 * WIDTH)
    kv = lax.all_gather(own, "y", axis=0, tiled=True)
    kv = pltpu.with_memory_space_constraint(kv, pltpu.HBM)

    columns = column_blocks(w_out)
    pieces = gather_pieces(parts[0], [(), (), (local, boundary)], (columns,))
    queries = [gathered_dot(place, pieces, w_query)]
    fwd, bwd = [[queries[0]]], [[queries[0]]]
    fwd[0].append(ring(fwd[0][-1], "z", NZ, 1))
    bwd[0].append(ring(bwd[0][-1], "z", NZ, -1))
    pieces = gather_pieces(parts[1], last=(queries[0],))
    pieces[-1] = tie(pieces[-1], fwd[0][1], bwd[0][1])
    queries.append(gathered_dot(place, pieces, w_query))
    fwd.append([queries[1]])
    bwd.append([queries[1]])
    count = len(CHUNKS)
    for c in range(count):
        while len(fwd[c]) < 4:
            fwd[c].append(ring(fwd[c][-1], "z", NZ, 1))
            bwd[c].append(ring(bwd[c][-1], "z", NZ, -1))
    columns = tie(columns, queries[1])
    w_cols = lax.all_to_all(columns, STORE, split_axis=0, concat_axis=0, tiled=True)
    cuts = [(last - first) // 2 for first, last in CHUNKS]
    far = [
        (ring(fwd[c][3][: cuts[c] * SPAN], "z", NZ, 1), ring(bwd[c][3][cuts[c] * SPAN :], "z", NZ, -1))
        for c in range(count)
    ]

    state, sent, gathered = [None] * count, (), [None] * count
    for c, s in ORDER:
        first, last = CHUNKS[c]
        spans, split = last - first, cuts[c]

        def base(distance, start=0):
            return ((distance % NZ) * SPANS_DEV + first + start) * NBR

        after = [*sent]
        if (c, s) == (0, 2):
            after.extend(state[1])
        if (c, s) == (0, 0):
            after.append(w_cols)
        if (c, s) == (1, 0):
            after.append(gathered[0][2])
        top, low = tie_all(far[c] if s == 4 else state[c], *after)
        if s == 0:
            sent = [finish(local, boundary, kv, base(0), spans, first, queries[c], top, low)]
            gathered[c] = gather_pieces(sent[0])
            continue
        if s == 4:
            ways = [
                (base(4), split, 0, 0, top, None),
                (base(4, split), spans - split, 0, 0, low, None),
            ]
        else:
            starts, helds = ((0, split), (split, spans - split)) if s == 3 else ((0, 0), (spans, spans))
            ways = [
                (base(s), spans, starts[0], helds[0], bwd[c][s], top),
                (base(-s), spans, starts[1], helds[1], fwd[c][s], low),
            ]
        sent = relay(local, kv, ways)
        state[c] = [ring(sent[0], "z", NZ, 1), ring(sent[1], "z", NZ, -1)]

    outs = {}
    for c, (first, last) in enumerate(CHUNKS):
        outs[first] = gathered_dot(place, gathered[c], w_cols, parts[c])
    result = jnp.concatenate([outs[first] for first in sorted(outs)], axis=0)
    order = [(i, i + 1) for i in range(NY * NZ - 1)]
    head = lax.ppermute(result[rows - (SPAN - 1) :], SEQ, order)
    head = jnp.where(seq_at == 0, hidden[: SPAN - 1], head)
    return jnp.concatenate([head, result[: rows - (SPAN - 1)]], axis=0)


def solution(mesh):
    fine = Mesh(mesh.devices.reshape(NY, NZ, NX, NC), ("y", "z", "x", "core"))
    return jax.shard_map(
        on_device,
        mesh=fine,
        in_specs=(
            P(SEQ, STORE),
            P(SEQ, None),
            P(SEQ, None),
            P(),
            P(SEQ, None, None, STORE),
            P(None, STORE),
            P(STORE, None),
        ),
        out_specs=P(SEQ, STORE),
        check_vma=False,
    )
```

```python
import functools
import jax
import jax.numpy as jnp
from jax import lax
from jax.experimental import pallas as pl
from jax.experimental.pallas import tpu as pltpu
from jax.sharding import Mesh, PartitionSpec as P

HEAD_DIM = 128
SPAN = 64
NBR = 2
NBR_LEN = 128
HEADS = 4
WIDTH = HEADS * HEAD_DIM
BLK_DEV = 8
NY, NZ, NX, NC = 4, 8, 4, 2
SEQ, STORE = ("y", "z"), ("x", "core")
ALL, EARLY = NX * NC, NX * NC - 2
SPANS_DEV = 12
CHUNKS = ((6, 12), (0, 6))
ORDER = tuple((c, s) for s in (4, 3, 2, 1, 0) for c in (0, 1))
STAT_ROWS = 16
FAR = -1e30
SCALE = HEAD_DIM**-0.5 * 1.4426950408889634
LANES = 128


def ring(array, axis, size, by):
    return lax.ppermute(array, axis, [(i, (i + by) % size) for i in range(size)])


def lane_rows(rows):
    return -(-rows // LANES) * LANES


def load_state(state_ref, out_ref, stat_ref, first, rows):
    out_ref[pl.ds(first, rows), :] = state_ref[pl.ds(0, rows), :]
    wide = lane_rows(rows)
    packed = state_ref[pl.ds(rows, STAT_ROWS), pl.ds(0, wide)].astype(jnp.float32)
    parts = jnp.concatenate([packed, jnp.zeros((LANES - STAT_ROWS, wide), jnp.float32)], axis=0).T
    total = parts + pltpu.roll(parts, LANES - HEADS, 1) + pltpu.roll(parts, LANES - 2 * HEADS, 1)
    stat_ref[pl.ds(first, rows), :] = total[:rows]


def store_stats(stat_ref, out_ref, rows):
    wide = lane_rows(rows)
    lse = stat_ref[pl.ds(0, rows), :]
    if wide != rows:
        lse = jnp.concatenate([lse, jnp.zeros((wide - rows, LANES), jnp.float32)], axis=0)
    high = lse.astype(jnp.bfloat16).astype(jnp.float32)
    rest = lse - high
    middle = rest.astype(jnp.bfloat16).astype(jnp.float32)
    low = rest - middle
    lane = lax.broadcasted_iota(jnp.int32, lse.shape, 1)
    packed = jnp.where(
        lane < HEADS,
        high,
        jnp.where(lane < 2 * HEADS, pltpu.roll(middle, HEADS, 1), pltpu.roll(low, 2 * HEADS, 1)),
    )
    packed = jnp.where(lane < 3 * HEADS, packed, 0.0).T
    out_ref[pl.ds(rows, STAT_ROWS), pl.ds(0, wide)] = packed[:STAT_ROWS].astype(jnp.bfloat16)
    if wide < WIDTH:
        out_ref[pl.ds(rows, STAT_ROWS), pl.ds(wide, WIDTH - wide)] = jnp.zeros(
            (STAT_ROWS, WIDTH - wide), jnp.bfloat16
        )


def merge(old, new):
    best = jnp.maximum(old, new)
    old_part = jnp.exp2(old - best)
    new_part = jnp.exp2(new - best)
    both = old_part + new_part
    scale = 1.0 / both
    return old_part * scale, new_part * scale, best + jnp.log2(both)


def attend(q_ref, q_row, block, out_ref, stat_ref, row):
    at = pl.ds(row, SPAN)
    lane = lax.broadcasted_iota(jnp.int32, (SPAN, LANES), 1)
    queries = q_ref[pl.ds(q_row, SPAN), :]
    old = out_ref[at, :].astype(jnp.float32)
    old_lse = stat_ref[at, :]
    heads = [slice(head * HEAD_DIM, (head + 1) * HEAD_DIM) for head in range(HEADS)]
    scores = [
        lax.dot_general(
            queries[:, cols], block[:, cols], (((1,), (1,)), ((), ())),
            preferred_element_type=jnp.float32,
        )
        for cols in heads
    ]
    peaks = [jnp.max(score, axis=-1, keepdims=True) for score in scores]
    weights = [jnp.exp2((score - peak) * SCALE) for score, peak in zip(scores, peaks)]
    totals = [jnp.sum(weight, axis=-1, keepdims=True) for weight in weights]
    mixed = [
        jnp.dot(
            weight.astype(jnp.bfloat16),
            block[:, WIDTH + cols.start : WIDTH + cols.stop],
            preferred_element_type=jnp.float32,
        )
        for weight, cols in zip(weights, heads)
    ]
    peak_tile = jnp.zeros((SPAN, LANES), jnp.float32)
    total_tile = jnp.ones((SPAN, LANES), jnp.float32)
    for head in range(HEADS):
        peak_tile = jnp.where(lane == head, peaks[head], peak_tile)
        total_tile = jnp.where(lane == head, totals[head], total_tile)
    old_weight, new_weight, lse = merge(old_lse, peak_tile * SCALE + jnp.log2(total_tile))
    new_weight = new_weight / total_tile
    outs = [
        old[:, cols] * old_weight[:, head : head + 1] + mixed[head] * new_weight[:, head : head + 1]
        for head, cols in enumerate(heads)
    ]
    stat_ref[at, :] = lse
    for cols, out in zip(heads, outs):
        out_ref[at, cols] = out.astype(jnp.bfloat16)


def start_blocks(ids_ref, base, spans, kv_ref, buf_ref, sems, slot0):
    def one(i, carry):
        block = ids_ref[base + i]

        @pl.when(block >= 0)
        def _():
            pltpu.make_async_copy(
                kv_ref.at[block], buf_ref.at[slot0 + i], sems.at[slot0 + i]
            ).start()

        return carry

    lax.fori_loop(0, spans * NBR, one, 0)


def attend_blocks(ids_ref, base, spans, q_ref, kv_ref, buf_ref, sems, slot0, out_ref, stat_ref):
    def one(i, carry):
        block = ids_ref[base + i]

        @pl.when(block >= 0)
        def _():
            pltpu.make_async_copy(
                kv_ref.at[0], buf_ref.at[slot0 + i], sems.at[slot0 + i]
            ).wait()
            row = pl.multiple_of((i // NBR) * SPAN, SPAN)
            attend(q_ref, row, buf_ref.at[slot0 + i], out_ref, stat_ref, row)

        return carry

    lax.fori_loop(0, spans * NBR, one, 0)


def relay_kernel(ways, *refs):
    ids_ref, kv_ref = refs[:2]
    refs = refs[2:]
    plan = []
    for base, spans, begin, held in ways:
        q_ref, refs = refs[0], refs[1:]
        state_ref = None
        if held:
            state_ref, refs = refs[0], refs[1:]
        plan.append([base, spans, begin, held, q_ref, state_ref])
    outs, refs = refs[: len(ways)], refs[len(ways) :]
    buf_ref, sems = refs[:2]
    stats = refs[2:]
    slot0 = 0
    for base, spans, *_ in plan:
        start_blocks(ids_ref, base, spans, kv_ref, buf_ref, sems, slot0)
        slot0 += spans * NBR
    slot0 = 0
    for (base, spans, begin, held, q_ref, state_ref), out_ref, stat_ref in zip(plan, outs, stats):
        rows = spans * SPAN
        if held != spans:
            out_ref[pl.ds(0, rows), :] = jnp.zeros((rows, WIDTH), jnp.bfloat16)
            stat_ref[...] = jnp.full((rows, LANES), FAR, jnp.float32)
        if held:
            load_state(state_ref, out_ref, stat_ref, begin * SPAN, held * SPAN)
        attend_blocks(
            ids_ref, base, spans, q_ref, kv_ref, buf_ref, sems, slot0, out_ref, stat_ref
        )
        store_stats(stat_ref, out_ref, rows)
        slot0 += spans * NBR


def final_kernel(base, spans, mask_base, ids_ref, edge_ref, kv_ref, *refs):
    q_ref, fwd_ref, bwd_ref, out_ref, buf_ref, sems, stat_ref, other_ref, other_stat = refs
    rows = spans * SPAN
    start_blocks(ids_ref, base, spans, kv_ref, buf_ref, sems, 0)
    load_state(fwd_ref, out_ref, stat_ref, 0, rows)
    load_state(bwd_ref, other_ref, other_stat, 0, rows)
    weight, other_weight, lse = merge(stat_ref[...], other_stat[...])
    stat_ref[...] = lse
    for head in range(HEADS):
        cols = slice(head * HEAD_DIM, (head + 1) * HEAD_DIM)
        out_ref[:, cols] = (
            out_ref[:, cols].astype(jnp.float32) * weight[:, head : head + 1]
            + other_ref[:, cols].astype(jnp.float32) * other_weight[:, head : head + 1]
        ).astype(jnp.bfloat16)
    attend_blocks(ids_ref, base, spans, q_ref, kv_ref, buf_ref, sems, 0, out_ref, stat_ref)

    def cut(i, carry):
        @pl.when(edge_ref[mask_base + i] > 0)
        def _():
            at = pl.ds(pl.multiple_of(i * SPAN, SPAN), SPAN)
            kept = lax.broadcasted_iota(jnp.int32, (SPAN, WIDTH), 0) == 0
            out_ref[at, :] = jnp.where(kept, out_ref[at, :], jnp.zeros((SPAN, WIDTH), jnp.bfloat16))

        return carry

    lax.fori_loop(0, spans, cut, 0)


SMEM = pl.BlockSpec(memory_space=pltpu.SMEM)
VMEM = pl.BlockSpec(memory_space=pltpu.VMEM)
HBM = pl.BlockSpec(memory_space=pltpu.HBM)


def cost(pairs, rows):
    return pl.CostEstimate(
        flops=pairs * HEADS * 4 * SPAN * HEAD_DIM * NBR_LEN,
        bytes_accessed=pairs * NBR_LEN * 4 * WIDTH + rows * WIDTH * 8,
        transcendentals=pairs * HEADS * SPAN * NBR_LEN,
    )


def relay(ids, kv, ways):
    specs = [w[:4] for w in ways]
    operands = [ids, kv]
    for base, spans, begin, held, queries, state in ways:
        operands.append(queries)
        if held:
            operands.append(state)
    total = sum(spans for _, spans, _, _ in specs)
    return pl.pallas_call(
        functools.partial(relay_kernel, specs),
        out_shape=[
            jax.ShapeDtypeStruct((spans * SPAN + STAT_ROWS, WIDTH), jnp.bfloat16)
            for _, spans, _, _ in specs
        ],
        in_specs=[SMEM, HBM] + [VMEM] * (len(operands) - 2),
        out_specs=[VMEM] * len(specs),
        scratch_shapes=[
            pltpu.VMEM((total * NBR, NBR_LEN, 2 * WIDTH), jnp.bfloat16),
            pltpu.SemaphoreType.DMA((total * NBR,)),
        ]
        + [pltpu.VMEM((spans * SPAN, LANES), jnp.float32) for _, spans, _, _ in specs],
        compiler_params=pltpu.CompilerParams(vmem_limit_bytes=12 * 1024 * 1024),
        cost_estimate=cost(6, total * SPAN),
    )(*operands)


def finish(ids, edges, kv, base, spans, mask_base, queries, fwd, bwd):
    rows = spans * SPAN
    return pl.pallas_call(
        functools.partial(final_kernel, base, spans, mask_base),
        out_shape=jax.ShapeDtypeStruct((rows, WIDTH), jnp.bfloat16),
        in_specs=[SMEM, SMEM, HBM] + [VMEM] * 3,
        out_specs=VMEM,
        scratch_shapes=[
            pltpu.VMEM((spans * NBR, NBR_LEN, 2 * WIDTH), jnp.bfloat16),
            pltpu.SemaphoreType.DMA((spans * NBR,)),
            pltpu.VMEM((rows, LANES), jnp.float32),
            pltpu.VMEM((rows, WIDTH), jnp.bfloat16),
            pltpu.VMEM((rows, LANES), jnp.float32),
        ],
        compiler_params=pltpu.CompilerParams(vmem_limit_bytes=12 * 1024 * 1024),
        cost_estimate=cost(3, rows),
    )(ids, edges, kv, queries, fwd, bwd)


def block_copies(place_ref, first, count, weight_ref, buf_ref, sems):
    copies = []
    for i in range(first, first + count):
        block = pl.ds(pl.multiple_of(place_ref[i] * WIDTH, WIDTH), WIDTH)
        copy = pltpu.make_async_copy(weight_ref.at[block], buf_ref.at[i - first], sems.at[i])
        copy.start()
        copies.append(copy)
    return copies


def add_pieces(pieces, buf_ref, total, copies=()):
    for i, piece_ref in enumerate(pieces):
        if copies:
            copies[i].wait()
        term = jnp.dot(piece_ref[...], buf_ref[i], preferred_element_type=jnp.float32)
        total = term if total is None else total + term
    return total


def add_squares(pieces, squares):
    for piece_ref in pieces:
        for k in range(HEADS):
            wide = piece_ref[:, k * LANES : (k + 1) * LANES].astype(jnp.float32)
            squares = wide * wide if squares is None else squares + wide * wide
    return squares


def early_kernel(norm, place_ref, weight_ref, *refs):
    pieces, refs = refs[:EARLY], refs[EARLY:]
    buf_ref, sems = refs[-2:]
    late_ref, total_ref = refs[-4:-2]
    copies = block_copies(place_ref, 0, EARLY, weight_ref, buf_ref, sems)
    late_copies = block_copies(place_ref, EARLY, ALL - EARLY, weight_ref, late_ref, sems)
    if norm:
        refs[0][...] = add_squares(pieces, None)
        total_ref[...] = add_pieces(pieces, buf_ref, None, copies)
    else:
        total_ref[...] = add_pieces(pieces, buf_ref, refs[0][...].astype(jnp.float32), copies)
    for copy in late_copies:
        copy.wait()


def late_kernel(norm, late_ref, *refs):
    pieces, refs = refs[: ALL - EARLY], refs[ALL - EARLY :]
    total_ref, out_ref = refs[-2:]
    total = add_pieces(pieces, late_ref, total_ref[...])
    if norm:
        squares = jnp.sum(add_squares(pieces, refs[0][...]), axis=-1, keepdims=True)
        total = total * lax.rsqrt(squares * (1.0 / (WIDTH * ALL)) + 1e-05)
    out_ref[...] = total.astype(jnp.bfloat16)


def gathered_cost(rows, count):
    return pl.CostEstimate(
        flops=2 * rows * WIDTH * WIDTH * count,
        bytes_accessed=2 * WIDTH * (rows + WIDTH) * count + 4 * rows * WIDTH,
        transcendentals=0,
    )


def gathered_dot(place, pieces, weight, residual=None):
    rows = pieces[0].shape[0]
    norm = residual is None
    pieces = [pieces[r + other] for r in range(NX) for other in (0, NX)]
    params = pltpu.CompilerParams(vmem_limit_bytes=14 * 1024 * 1024)
    total = jax.ShapeDtypeStruct((rows, WIDTH), jnp.float32)
    squares = jax.ShapeDtypeStruct((rows, LANES), jnp.float32)
    weight = pltpu.with_memory_space_constraint(weight, pltpu.HBM)
    late = jax.ShapeDtypeStruct((ALL - EARLY, WIDTH, WIDTH), jnp.bfloat16)
    outs = pl.pallas_call(
        functools.partial(early_kernel, norm),
        out_shape=([squares] if norm else []) + [late, total],
        in_specs=[SMEM, HBM] + [VMEM] * (EARLY + (not norm)),
        out_specs=[VMEM] * (2 + norm),
        scratch_shapes=[
            pltpu.VMEM((EARLY, WIDTH, WIDTH), jnp.bfloat16),
            pltpu.SemaphoreType.DMA((ALL,)),
        ],
        compiler_params=params,
        cost_estimate=gathered_cost(rows, EARLY),
    )(place, weight, *pieces[:EARLY], *([] if norm else [residual]))
    return pl.pallas_call(
        functools.partial(late_kernel, norm),
        out_shape=jax.ShapeDtypeStruct((rows, WIDTH), jnp.bfloat16),
        in_specs=[VMEM] * (ALL - EARLY + 2 + norm),
        out_specs=VMEM,
        compiler_params=params,
        cost_estimate=gathered_cost(rows, ALL - EARLY),
    )(outs[-2], *pieces[EARLY:], *outs[:-2], outs[-1])


def gather_pieces(own, before=((), (), ()), last=()):
    up = [(2 * x, 2 * ((x + 1) % NX)) for x in range(NX)]
    down = [(2 * x + 1, 2 * ((x - 1) % NX) + 1) for x in range(NX)]
    swap = [(i, i ^ 1) for i in range(NX * NC)]
    held = [own]
    for after in before:
        held.append(lax.ppermute(tie(held[-1], *after), STORE, up + down))
    others = [lax.ppermute(piece, STORE, swap) for piece in held[:-1]]
    return held + others + [lax.ppermute(tie(held[-1], *last), STORE, swap)]


def piece_places():
    x, core = lax.axis_index("x"), lax.axis_index("core")
    step = 1 - 2 * core
    away = jnp.arange(NX, dtype=jnp.int32) * step
    mine = ((x - away) % NX) * NC + core
    others = ((x + away) % NX) * NC + 1 - core
    return jnp.stack([mine, others], axis=1).reshape(-1).astype(jnp.int32)


def column_kernel(w_ref, out_ref):
    out_ref[...] = w_ref[...]


def column_blocks(weight):
    return pl.pallas_call(
        column_kernel,
        out_shape=jax.ShapeDtypeStruct((NX * NC * WIDTH, WIDTH), weight.dtype),
        grid=(NX * NC,),
        in_specs=[pl.BlockSpec((WIDTH, WIDTH), lambda k: (0, k))],
        out_specs=pl.BlockSpec((WIDTH, WIDTH), lambda k: (k, 0)),
        compiler_params=pltpu.CompilerParams(vmem_limit_bytes=4 * 1024 * 1024),
        cost_estimate=pl.CostEstimate(
            flops=0, bytes_accessed=4 * NX * NC * WIDTH * WIDTH, transcendentals=0
        ),
    )(weight)


def tie(array, *after):
    return lax.optimization_barrier((array, *after))[0]


def tie_all(arrays, *after):
    return list(lax.optimization_barrier((*arrays, *after))[: len(arrays)])


def on_device(hidden, nbr_shard, nbr_block, seq_lengths, kv_store, w_query, w_out):
    rows = hidden.shape[0]
    my_y, my_z = lax.axis_index("y"), lax.axis_index("z")
    seq_at = my_y * NZ + my_z
    order = [(i, i - 1) for i in range(1, NY * NZ)]
    edge = lax.ppermute(hidden[: SPAN - 1], SEQ, order)
    attending = jnp.concatenate([hidden[SPAN - 1 :], edge], axis=0)
    place = piece_places()

    wanted = (nbr_shard * BLK_DEV + nbr_block).reshape(-1)
    for by in (1, 2, 4):
        wanted = jnp.concatenate([wanted, ring(wanted, "z", NZ, -by)])
    shard, block = wanted // BLK_DEV, wanted % BLK_DEV
    local = jnp.where(shard % NZ == my_z, shard // NZ * BLK_DEV + block, -1).astype(jnp.int32)
    span_index = seq_at * SPANS_DEV + jnp.arange(SPANS_DEV, dtype=jnp.int32)
    upto = jnp.arange(seq_lengths.shape[0])
    seq_ends = jnp.sum(jnp.where(upto[None, :] <= upto[:, None], seq_lengths[None, :], 0), axis=1)
    boundary = jnp.any(seq_ends[None, :] == span_index[:, None] + 1, axis=1)
    boundary = boundary.astype(jnp.int32)

    parts = [attending[first * SPAN : last * SPAN] for first, last in CHUNKS]

    own = tie(kv_store, parts[1]).reshape(BLK_DEV, NBR_LEN, 2 * WIDTH)
    kv = lax.all_gather(own, "y", axis=0, tiled=True)
    kv = pltpu.with_memory_space_constraint(kv, pltpu.HBM)

    columns = column_blocks(w_out)
    before = [[(), (), (local, boundary, columns)], ((), (), ())]
    queries = [
        gathered_dot(place, gather_pieces(part, when), w_query)
        for part, when in zip(parts, before)
    ]
    columns = tie(columns, *queries)
    w_cols = lax.all_to_all(columns, STORE, split_axis=0, concat_axis=0, tiled=True)
    fwd, bwd = [[q] for q in queries], [[q] for q in queries]
    count = len(CHUNKS)
    for _ in range(3):
        for c in range(count):
            fwd[c].append(ring(fwd[c][-1], "z", NZ, 1))
            bwd[c].append(ring(bwd[c][-1], "z", NZ, -1))
    cuts = [(last - first) // 2 for first, last in CHUNKS]
    far = [
        (ring(fwd[c][3][: cuts[c] * SPAN], "z", NZ, 1), ring(bwd[c][3][cuts[c] * SPAN :], "z", NZ, -1))
        for c in range(count)
    ]

    state, sent, gathered = [None] * count, (), [None] * count
    for c, s in ORDER:
        first, last = CHUNKS[c]
        spans, split = last - first, cuts[c]

        def base(distance, start=0):
            return ((distance % NZ) * SPANS_DEV + first + start) * NBR

        after = [*sent]
        if (c, s) == (0, 0):
            after.append(w_cols)
        top, low = tie_all(far[c] if s == 4 else state[c], *after)
        if s == 0:
            sent = [finish(local, boundary, kv, base(0), spans, first, queries[c], top, low)]
            gathered[c] = gather_pieces(sent[0])
            continue
        if s == 4:
            ways = [
                (base(4), split, 0, 0, top, None),
                (base(4, split), spans - split, 0, 0, low, None),
            ]
        else:
            starts, helds = ((0, split), (split, spans - split)) if s == 3 else ((0, 0), (spans, spans))
            ways = [
                (base(s), spans, starts[0], helds[0], bwd[c][s], top),
                (base(-s), spans, starts[1], helds[1], fwd[c][s], low),
            ]
        sent = relay(local, kv, ways)
        state[c] = [ring(sent[0], "z", NZ, 1), ring(sent[1], "z", NZ, -1)]

    outs = {}
    for c, (first, last) in enumerate(CHUNKS):
        outs[first] = gathered_dot(place, gathered[c], w_cols, parts[c])
    result = jnp.concatenate([outs[first] for first in sorted(outs)], axis=0)
    order = [(i, i + 1) for i in range(NY * NZ - 1)]
    head = lax.ppermute(result[rows - (SPAN - 1) :], SEQ, order)
    head = jnp.where(seq_at == 0, hidden[: SPAN - 1], head)
    return jnp.concatenate([head, result[: rows - (SPAN - 1)]], axis=0)


def solution(mesh):
    fine = Mesh(mesh.devices.reshape(NY, NZ, NX, NC), ("y", "z", "x", "core"))
    return jax.shard_map(
        on_device,
        mesh=fine,
        in_specs=(
            P(SEQ, STORE),
            P(SEQ, None),
            P(SEQ, None),
            P(),
            P(SEQ, None, None, STORE),
            P(None, STORE),
            P(STORE, None),
        ),
        out_specs=P(SEQ, STORE),
        check_vma=False,
    )
```

```python
import functools
import jax
import jax.numpy as jnp
from jax import lax
from jax.experimental import pallas as pl
from jax.experimental.pallas import tpu as pltpu
from jax.sharding import Mesh, PartitionSpec as P

HEAD_DIM = 128
SPAN = 64
NBR = 2
NBR_LEN = 128
HEADS = 4
WIDTH = HEADS * HEAD_DIM
BLK_DEV = 8
NY, NZ, NX, NC = 4, 8, 4, 2
SEQ, STORE = ("y", "z"), ("x", "core")
ALL, EARLY = NX * NC, NX * NC - 2
SPANS_DEV = 12
CHUNKS = ((6, 12), (0, 6))
ORDER = tuple((c, s) for s in (4, 3, 2, 1, 0) for c in (0, 1))
STAT_ROWS = 16
FAR = -1e30
SCALE = HEAD_DIM**-0.5 * 1.4426950408889634
LANES = 128


def ring(array, axis, size, by):
    return lax.ppermute(array, axis, [(i, (i + by) % size) for i in range(size)])


def lane_rows(rows):
    return -(-rows // LANES) * LANES


def load_state(state_ref, out_ref, stat_ref, first, rows):
    out_ref[pl.ds(first, rows), :] = state_ref[pl.ds(0, rows), :]
    wide = lane_rows(rows)
    packed = state_ref[pl.ds(rows, STAT_ROWS), pl.ds(0, wide)].astype(jnp.float32)
    parts = jnp.concatenate([packed, jnp.zeros((LANES - STAT_ROWS, wide), jnp.float32)], axis=0).T
    total = parts + pltpu.roll(parts, LANES - HEADS, 1) + pltpu.roll(parts, LANES - 2 * HEADS, 1)
    stat_ref[pl.ds(first, rows), :] = total[:rows]


def store_stats(stat_ref, out_ref, rows):
    wide = lane_rows(rows)
    lse = stat_ref[pl.ds(0, rows), :]
    if wide != rows:
        lse = jnp.concatenate([lse, jnp.zeros((wide - rows, LANES), jnp.float32)], axis=0)
    high = lse.astype(jnp.bfloat16).astype(jnp.float32)
    rest = lse - high
    middle = rest.astype(jnp.bfloat16).astype(jnp.float32)
    low = rest - middle
    lane = lax.broadcasted_iota(jnp.int32, lse.shape, 1)
    packed = jnp.where(
        lane < HEADS,
        high,
        jnp.where(lane < 2 * HEADS, pltpu.roll(middle, HEADS, 1), pltpu.roll(low, 2 * HEADS, 1)),
    )
    packed = jnp.where(lane < 3 * HEADS, packed, 0.0).T
    out_ref[pl.ds(rows, STAT_ROWS), pl.ds(0, wide)] = packed[:STAT_ROWS].astype(jnp.bfloat16)
    if wide < WIDTH:
        out_ref[pl.ds(rows, STAT_ROWS), pl.ds(wide, WIDTH - wide)] = jnp.zeros(
            (STAT_ROWS, WIDTH - wide), jnp.bfloat16
        )


def merge(old, new):
    best = jnp.maximum(old, new)
    old_part = jnp.exp2(old - best)
    new_part = jnp.exp2(new - best)
    both = old_part + new_part
    scale = 1.0 / both
    return old_part * scale, new_part * scale, best + jnp.log2(both)


def attend(q_ref, q_row, block, out_ref, stat_ref, row):
    at = pl.ds(row, SPAN)
    lane = lax.broadcasted_iota(jnp.int32, (SPAN, LANES), 1)
    queries = q_ref[pl.ds(q_row, SPAN), :]
    old = out_ref[at, :].astype(jnp.float32)
    old_lse = stat_ref[at, :]
    heads = [slice(head * HEAD_DIM, (head + 1) * HEAD_DIM) for head in range(HEADS)]
    scores = [
        lax.dot_general(
            queries[:, cols], block[:, cols], (((1,), (1,)), ((), ())),
            preferred_element_type=jnp.float32,
        )
        for cols in heads
    ]
    peaks = [jnp.max(score, axis=-1, keepdims=True) for score in scores]
    weights = [jnp.exp2((score - peak) * SCALE) for score, peak in zip(scores, peaks)]
    totals = [jnp.sum(weight, axis=-1, keepdims=True) for weight in weights]
    mixed = [
        jnp.dot(
            weight.astype(jnp.bfloat16),
            block[:, WIDTH + cols.start : WIDTH + cols.stop],
            preferred_element_type=jnp.float32,
        )
        for weight, cols in zip(weights, heads)
    ]
    peak_tile = jnp.zeros((SPAN, LANES), jnp.float32)
    total_tile = jnp.ones((SPAN, LANES), jnp.float32)
    for head in range(HEADS):
        peak_tile = jnp.where(lane == head, peaks[head], peak_tile)
        total_tile = jnp.where(lane == head, totals[head], total_tile)
    old_weight, new_weight, lse = merge(old_lse, peak_tile * SCALE + jnp.log2(total_tile))
    new_weight = new_weight / total_tile
    outs = [
        old[:, cols] * old_weight[:, head : head + 1] + mixed[head] * new_weight[:, head : head + 1]
        for head, cols in enumerate(heads)
    ]
    stat_ref[at, :] = lse
    for cols, out in zip(heads, outs):
        out_ref[at, cols] = out.astype(jnp.bfloat16)


def start_blocks(ids_ref, base, spans, kv_ref, buf_ref, sems, slot0):
    def one(i, carry):
        block = ids_ref[base + i]

        @pl.when(block >= 0)
        def _():
            pltpu.make_async_copy(
                kv_ref.at[block], buf_ref.at[slot0 + i], sems.at[slot0 + i]
            ).start()

        return carry

    lax.fori_loop(0, spans * NBR, one, 0)


def attend_blocks(ids_ref, base, spans, q_ref, kv_ref, buf_ref, sems, slot0, out_ref, stat_ref):
    def one(i, carry):
        block = ids_ref[base + i]

        @pl.when(block >= 0)
        def _():
            pltpu.make_async_copy(
                kv_ref.at[0], buf_ref.at[slot0 + i], sems.at[slot0 + i]
            ).wait()
            row = pl.multiple_of((i // NBR) * SPAN, SPAN)
            attend(q_ref, row, buf_ref.at[slot0 + i], out_ref, stat_ref, row)

        return carry

    lax.fori_loop(0, spans * NBR, one, 0)


def relay_kernel(ways, *refs):
    ids_ref, kv_ref = refs[:2]
    refs = refs[2:]
    plan = []
    for base, spans, begin, held in ways:
        q_ref, refs = refs[0], refs[1:]
        state_ref = None
        if held:
            state_ref, refs = refs[0], refs[1:]
        plan.append([base, spans, begin, held, q_ref, state_ref])
    outs, refs = refs[: len(ways)], refs[len(ways) :]
    buf_ref, sems = refs[:2]
    stats = refs[2:]
    slot0 = 0
    for base, spans, *_ in plan:
        start_blocks(ids_ref, base, spans, kv_ref, buf_ref, sems, slot0)
        slot0 += spans * NBR
    slot0 = 0
    for (base, spans, begin, held, q_ref, state_ref), out_ref, stat_ref in zip(plan, outs, stats):
        rows = spans * SPAN
        if held != spans:
            out_ref[pl.ds(0, rows), :] = jnp.zeros((rows, WIDTH), jnp.bfloat16)
            stat_ref[...] = jnp.full((rows, LANES), FAR, jnp.float32)
        if held:
            load_state(state_ref, out_ref, stat_ref, begin * SPAN, held * SPAN)
        attend_blocks(
            ids_ref, base, spans, q_ref, kv_ref, buf_ref, sems, slot0, out_ref, stat_ref
        )
        store_stats(stat_ref, out_ref, rows)
        slot0 += spans * NBR


def final_kernel(base, spans, mask_base, ids_ref, edge_ref, kv_ref, *refs):
    q_ref, fwd_ref, bwd_ref, out_ref, buf_ref, sems, stat_ref, other_ref, other_stat = refs
    rows = spans * SPAN
    start_blocks(ids_ref, base, spans, kv_ref, buf_ref, sems, 0)
    load_state(fwd_ref, out_ref, stat_ref, 0, rows)
    load_state(bwd_ref, other_ref, other_stat, 0, rows)
    weight, other_weight, lse = merge(stat_ref[...], other_stat[...])
    stat_ref[...] = lse
    for head in range(HEADS):
        cols = slice(head * HEAD_DIM, (head + 1) * HEAD_DIM)
        out_ref[:, cols] = (
            out_ref[:, cols].astype(jnp.float32) * weight[:, head : head + 1]
            + other_ref[:, cols].astype(jnp.float32) * other_weight[:, head : head + 1]
        ).astype(jnp.bfloat16)
    attend_blocks(ids_ref, base, spans, q_ref, kv_ref, buf_ref, sems, 0, out_ref, stat_ref)

    def cut(i, carry):
        @pl.when(edge_ref[mask_base + i] > 0)
        def _():
            at = pl.ds(pl.multiple_of(i * SPAN, SPAN), SPAN)
            kept = lax.broadcasted_iota(jnp.int32, (SPAN, WIDTH), 0) == 0
            out_ref[at, :] = jnp.where(kept, out_ref[at, :], jnp.zeros((SPAN, WIDTH), jnp.bfloat16))

        return carry

    lax.fori_loop(0, spans, cut, 0)


SMEM = pl.BlockSpec(memory_space=pltpu.SMEM)
VMEM = pl.BlockSpec(memory_space=pltpu.VMEM)
HBM = pl.BlockSpec(memory_space=pltpu.HBM)


def cost(pairs, rows):
    return pl.CostEstimate(
        flops=pairs * HEADS * 4 * SPAN * HEAD_DIM * NBR_LEN,
        bytes_accessed=pairs * NBR_LEN * 4 * WIDTH + rows * WIDTH * 8,
        transcendentals=pairs * HEADS * SPAN * NBR_LEN,
    )


def relay(ids, kv, ways):
    specs = [w[:4] for w in ways]
    operands = [ids, kv]
    for base, spans, begin, held, queries, state in ways:
        operands.append(queries)
        if held:
            operands.append(state)
    total = sum(spans for _, spans, _, _ in specs)
    return pl.pallas_call(
        functools.partial(relay_kernel, specs),
        out_shape=[
            jax.ShapeDtypeStruct((spans * SPAN + STAT_ROWS, WIDTH), jnp.bfloat16)
            for _, spans, _, _ in specs
        ],
        in_specs=[SMEM, HBM] + [VMEM] * (len(operands) - 2),
        out_specs=[VMEM] * len(specs),
        scratch_shapes=[
            pltpu.VMEM((total * NBR, NBR_LEN, 2 * WIDTH), jnp.bfloat16),
            pltpu.SemaphoreType.DMA((total * NBR,)),
        ]
        + [pltpu.VMEM((spans * SPAN, LANES), jnp.float32) for _, spans, _, _ in specs],
        compiler_params=pltpu.CompilerParams(vmem_limit_bytes=12 * 1024 * 1024),
        cost_estimate=cost(6, total * SPAN),
    )(*operands)


def finish(ids, edges, kv, base, spans, mask_base, queries, fwd, bwd):
    rows = spans * SPAN
    return pl.pallas_call(
        functools.partial(final_kernel, base, spans, mask_base),
        out_shape=jax.ShapeDtypeStruct((rows, WIDTH), jnp.bfloat16),
        in_specs=[SMEM, SMEM, HBM] + [VMEM] * 3,
        out_specs=VMEM,
        scratch_shapes=[
            pltpu.VMEM((spans * NBR, NBR_LEN, 2 * WIDTH), jnp.bfloat16),
            pltpu.SemaphoreType.DMA((spans * NBR,)),
            pltpu.VMEM((rows, LANES), jnp.float32),
            pltpu.VMEM((rows, WIDTH), jnp.bfloat16),
            pltpu.VMEM((rows, LANES), jnp.float32),
        ],
        compiler_params=pltpu.CompilerParams(vmem_limit_bytes=12 * 1024 * 1024),
        cost_estimate=cost(3, rows),
    )(ids, edges, kv, queries, fwd, bwd)


def block_copies(place_ref, first, count, weight_ref, buf_ref, sems):
    copies = []
    for i in range(first, first + count):
        block = pl.ds(pl.multiple_of(place_ref[i] * WIDTH, WIDTH), WIDTH)
        copy = pltpu.make_async_copy(weight_ref.at[block], buf_ref.at[i - first], sems.at[i])
        copy.start()
        copies.append(copy)
    return copies


def add_pieces(pieces, buf_ref, total, copies=()):
    for i, piece_ref in enumerate(pieces):
        if copies:
            copies[i].wait()
        term = jnp.dot(piece_ref[...], buf_ref[i], preferred_element_type=jnp.float32)
        total = term if total is None else total + term
    return total


def add_squares(pieces):
    squares = None
    for piece_ref in pieces:
        for k in range(HEADS):
            wide = piece_ref[:, k * LANES : (k + 1) * LANES].astype(jnp.float32)
            squares = wide * wide if squares is None else squares + wide * wide
    return squares


def query_kernel(place_ref, weight_ref, *refs):
    pieces, (out_ref, buf_ref, sems) = refs[:ALL], refs[ALL:]
    copies = block_copies(place_ref, 0, ALL, weight_ref, buf_ref, sems)
    squares = jnp.sum(add_squares(pieces), axis=-1, keepdims=True)
    total = add_pieces(pieces, buf_ref, None, copies)
    total = total * lax.rsqrt(squares * (1.0 / (WIDTH * ALL)) + 1e-05)
    out_ref[...] = total.astype(jnp.bfloat16)


def early_kernel(place_ref, weight_ref, *refs):
    pieces, refs = refs[:EARLY], refs[EARLY:]
    residual_ref, late_ref, total_ref, buf_ref, sems = refs
    copies = block_copies(place_ref, 0, EARLY, weight_ref, buf_ref, sems)
    late_copies = block_copies(place_ref, EARLY, ALL - EARLY, weight_ref, late_ref, sems)
    total_ref[...] = add_pieces(pieces, buf_ref, residual_ref[...].astype(jnp.float32), copies)
    for copy in late_copies:
        copy.wait()


def late_kernel(late_ref, *refs):
    pieces, (total_ref, out_ref) = refs[: ALL - EARLY], refs[ALL - EARLY :]
    out_ref[...] = add_pieces(pieces, late_ref, total_ref[...]).astype(jnp.bfloat16)


def gathered_cost(rows, count):
    return pl.CostEstimate(
        flops=2 * rows * WIDTH * WIDTH * count,
        bytes_accessed=2 * WIDTH * (rows + WIDTH) * count + 4 * rows * WIDTH,
        transcendentals=0,
    )


def in_order(pieces):
    return [pieces[r + other] for r in range(NX) for other in (0, NX)]


PARAMS = pltpu.CompilerParams(vmem_limit_bytes=14 * 1024 * 1024)


def project_queries(place, pieces, weight):
    rows = pieces[0].shape[0]
    return pl.pallas_call(
        query_kernel,
        out_shape=jax.ShapeDtypeStruct((rows, WIDTH), jnp.bfloat16),
        in_specs=[SMEM, HBM] + [VMEM] * ALL,
        out_specs=VMEM,
        scratch_shapes=[
            pltpu.VMEM((ALL, WIDTH, WIDTH), jnp.bfloat16),
            pltpu.SemaphoreType.DMA((ALL,)),
        ],
        compiler_params=PARAMS,
        cost_estimate=gathered_cost(rows, ALL),
    )(place, pltpu.with_memory_space_constraint(weight, pltpu.HBM), *in_order(pieces))


def project_out(place, pieces, weight, residual):
    rows = residual.shape[0]
    pieces = in_order(pieces)
    late, total = pl.pallas_call(
        early_kernel,
        out_shape=[
            jax.ShapeDtypeStruct((ALL - EARLY, WIDTH, WIDTH), jnp.bfloat16),
            jax.ShapeDtypeStruct((rows, WIDTH), jnp.float32),
        ],
        in_specs=[SMEM, HBM] + [VMEM] * (EARLY + 1),
        out_specs=[VMEM] * 2,
        scratch_shapes=[
            pltpu.VMEM((EARLY, WIDTH, WIDTH), jnp.bfloat16),
            pltpu.SemaphoreType.DMA((ALL,)),
        ],
        compiler_params=PARAMS,
        cost_estimate=gathered_cost(rows, EARLY),
    )(place, pltpu.with_memory_space_constraint(weight, pltpu.HBM), *pieces[:EARLY], residual)
    return pl.pallas_call(
        late_kernel,
        out_shape=jax.ShapeDtypeStruct((rows, WIDTH), jnp.bfloat16),
        in_specs=[VMEM] * (ALL - EARLY + 2),
        out_specs=VMEM,
        compiler_params=PARAMS,
        cost_estimate=gathered_cost(rows, ALL - EARLY),
    )(late, *pieces[EARLY:], total)


def gather_pieces(own, before=((), (), ()), last=()):
    up = [(2 * x, 2 * ((x + 1) % NX)) for x in range(NX)]
    down = [(2 * x + 1, 2 * ((x - 1) % NX) + 1) for x in range(NX)]
    swap = [(i, i ^ 1) for i in range(NX * NC)]
    held = [own]
    for after in before:
        held.append(lax.ppermute(tie(held[-1], *after), STORE, up + down))
    others = [lax.ppermute(piece, STORE, swap) for piece in held[:-1]]
    return held + others + [lax.ppermute(tie(held[-1], *last), STORE, swap)]


def piece_places():
    x, core = lax.axis_index("x"), lax.axis_index("core")
    step = 1 - 2 * core
    away = jnp.arange(NX, dtype=jnp.int32) * step
    mine = ((x - away) % NX) * NC + core
    others = ((x + away) % NX) * NC + 1 - core
    return jnp.stack([mine, others], axis=1).reshape(-1).astype(jnp.int32)


def column_kernel(w_ref, out_ref):
    out_ref[...] = w_ref[...]


def column_blocks(weight):
    return pl.pallas_call(
        column_kernel,
        out_shape=jax.ShapeDtypeStruct((NX * NC * WIDTH, WIDTH), weight.dtype),
        grid=(NX * NC,),
        in_specs=[pl.BlockSpec((WIDTH, WIDTH), lambda k: (0, k))],
        out_specs=pl.BlockSpec((WIDTH, WIDTH), lambda k: (k, 0)),
        compiler_params=pltpu.CompilerParams(vmem_limit_bytes=4 * 1024 * 1024),
        cost_estimate=pl.CostEstimate(
            flops=0, bytes_accessed=4 * NX * NC * WIDTH * WIDTH, transcendentals=0
        ),
    )(weight)


def tie(array, *after):
    return lax.optimization_barrier((array, *after))[0]


def tie_all(arrays, *after):
    return list(lax.optimization_barrier((*arrays, *after))[: len(arrays)])


def on_device(hidden, nbr_shard, nbr_block, seq_lengths, kv_store, w_query, w_out):
    rows = hidden.shape[0]
    my_y, my_z = lax.axis_index("y"), lax.axis_index("z")
    seq_at = my_y * NZ + my_z
    order = [(i, i - 1) for i in range(1, NY * NZ)]
    edge = lax.ppermute(hidden[: SPAN - 1], SEQ, order)
    attending = jnp.concatenate([hidden[SPAN - 1 :], edge], axis=0)
    place = piece_places()

    wanted = (nbr_shard * BLK_DEV + nbr_block).reshape(-1)
    for by in (1, 2, 4):
        wanted = jnp.concatenate([wanted, ring(wanted, "z", NZ, -by)])
    shard, block = wanted // BLK_DEV, wanted % BLK_DEV
    local = jnp.where(shard % NZ == my_z, shard // NZ * BLK_DEV + block, -1).astype(jnp.int32)
    span_index = seq_at * SPANS_DEV + jnp.arange(SPANS_DEV, dtype=jnp.int32)
    upto = jnp.arange(seq_lengths.shape[0])
    seq_ends = jnp.sum(jnp.where(upto[None, :] <= upto[:, None], seq_lengths[None, :], 0), axis=1)
    boundary = jnp.any(seq_ends[None, :] == span_index[:, None] + 1, axis=1)
    boundary = boundary.astype(jnp.int32)

    parts = [attending[first * SPAN : last * SPAN] for first, last in CHUNKS]

    columns = column_blocks(w_out)
    before = [[(), (), (local, boundary, columns)], ((), (), ())]
    pieces = [gather_pieces(part, when) for part, when in zip(parts, before)]

    own = tie(kv_store, parts[1]).reshape(BLK_DEV, NBR_LEN, 2 * WIDTH)
    kv = lax.all_gather(own, "y", axis=0, tiled=True)
    kv = pltpu.with_memory_space_constraint(kv, pltpu.HBM)

    queries = [project_queries(place, piece, w_query) for piece in pieces]
    columns = tie(columns, *queries)
    w_cols = lax.all_to_all(columns, STORE, split_axis=0, concat_axis=0, tiled=True)
    fwd, bwd = [[q] for q in queries], [[q] for q in queries]
    count = len(CHUNKS)
    for _ in range(3):
        for c in range(count):
            fwd[c].append(ring(fwd[c][-1], "z", NZ, 1))
            bwd[c].append(ring(bwd[c][-1], "z", NZ, -1))
    cuts = [(last - first) // 2 for first, last in CHUNKS]
    far = [
        (ring(fwd[c][3][: cuts[c] * SPAN], "z", NZ, 1), ring(bwd[c][3][cuts[c] * SPAN :], "z", NZ, -1))
        for c in range(count)
    ]

    state, sent, attended = [None] * count, (), [None] * count
    for c, s in ORDER:
        first, last = CHUNKS[c]
        spans, split = last - first, cuts[c]

        def base(distance, start=0):
            return ((distance % NZ) * SPANS_DEV + first + start) * NBR

        after = [*sent]
        if (c, s) == (0, 0):
            after.append(w_cols)
        top, low = tie_all(far[c] if s == 4 else state[c], *after)
        if s == 0:
            sent = [finish(local, boundary, kv, base(0), spans, first, queries[c], top, low)]
            attended[c] = sent[0]
            continue
        if s == 4:
            ways = [
                (base(4), split, 0, 0, top, None),
                (base(4, split), spans - split, 0, 0, low, None),
            ]
        else:
            starts, helds = ((0, split), (split, spans - split)) if s == 3 else ((0, 0), (spans, spans))
            ways = [
                (base(s), spans, starts[0], helds[0], bwd[c][s], top),
                (base(-s), spans, starts[1], helds[1], fwd[c][s], low),
            ]
        sent = relay(local, kv, ways)
        state[c] = [ring(sent[0], "z", NZ, 1), ring(sent[1], "z", NZ, -1)]

    tail = rows - (CHUNKS[0][0] * SPAN + SPAN - 1)
    order = [(i, i + 1) for i in range(NY * NZ - 1)]
    head = tie(lax.ppermute(attended[0][tail:], SEQ, order), attended[1])
    attended[0] = jnp.concatenate([head, attended[0][:tail]], axis=0)
    residual = jnp.concatenate([hidden[: SPAN - 1], hidden[rows - tail :]], axis=0)
    middle = project_out(place, gather_pieces(attended[1]), w_cols, parts[1])
    ends = project_out(place, gather_pieces(attended[0], last=(middle,)), w_cols, residual)
    return jnp.concatenate([ends[: SPAN - 1], middle, ends[SPAN - 1 :]], axis=0)


def solution(mesh):
    fine = Mesh(mesh.devices.reshape(NY, NZ, NX, NC), ("y", "z", "x", "core"))
    return jax.shard_map(
        on_device,
        mesh=fine,
        in_specs=(
            P(SEQ, STORE),
            P(SEQ, None),
            P(SEQ, None),
            P(),
            P(SEQ, None, None, STORE),
            P(None, STORE),
            P(STORE, None),
        ),
        out_specs=P(SEQ, STORE),
        check_vma=False,
    )
```

```python
import functools
import jax
import jax.numpy as jnp
from jax import lax
from jax.experimental import pallas as pl
from jax.experimental.pallas import tpu as pltpu
from jax.sharding import Mesh, PartitionSpec as P

HEAD_DIM = 128
SPAN = 64
NBR = 2
NBR_LEN = 128
HEADS = 4
WIDTH = HEADS * HEAD_DIM
BLK_DEV = 8
NY, NZ, NX, NC = 4, 8, 4, 2
SEQ, STORE = ("y", "z"), ("x", "core")
ALL, EARLY = NX * NC, NX * NC - 2
SPANS_DEV = 12
CHUNKS = ((6, 12), (0, 6))
ORDER = tuple((c, s) for s in (1, 2, 3, 4, 5, 6, 7, 0) for c in (0, 1))
AHEAD = 3
STAT_ROWS = 16
FAR = -1e30
SCALE = HEAD_DIM**-0.5 * 1.4426950408889634
LANES = 128


def ring(array, axis, size, by):
    return lax.ppermute(array, axis, [(i, (i + by) % size) for i in range(size)])


def turn(array):
    up = [(NC * z, NC * ((z + 1) % NZ)) for z in range(NZ)]
    down = [(NC * z + 1, NC * ((z - 1) % NZ) + 1) for z in range(NZ)]
    return lax.ppermute(array, ("z", "core"), up + down)


def lane_rows(rows):
    return -(-rows // LANES) * LANES


def load_state(state_ref, out_ref, stat_ref, first, rows):
    out_ref[pl.ds(first, rows), :] = state_ref[pl.ds(0, rows), :]
    wide = lane_rows(rows)
    packed = state_ref[pl.ds(rows, STAT_ROWS), pl.ds(0, wide)].astype(jnp.float32)
    parts = jnp.concatenate([packed, jnp.zeros((LANES - STAT_ROWS, wide), jnp.float32)], axis=0).T
    total = parts + pltpu.roll(parts, LANES - HEADS, 1) + pltpu.roll(parts, LANES - 2 * HEADS, 1)
    stat_ref[pl.ds(first, rows), :] = total[:rows]


def store_stats(stat_ref, out_ref, rows):
    wide = lane_rows(rows)
    lse = stat_ref[pl.ds(0, rows), :]
    if wide != rows:
        lse = jnp.concatenate([lse, jnp.zeros((wide - rows, LANES), jnp.float32)], axis=0)
    high = lse.astype(jnp.bfloat16).astype(jnp.float32)
    rest = lse - high
    middle = rest.astype(jnp.bfloat16).astype(jnp.float32)
    low = rest - middle
    lane = lax.broadcasted_iota(jnp.int32, lse.shape, 1)
    packed = jnp.where(
        lane < HEADS,
        high,
        jnp.where(lane < 2 * HEADS, pltpu.roll(middle, HEADS, 1), pltpu.roll(low, 2 * HEADS, 1)),
    )
    packed = jnp.where(lane < 3 * HEADS, packed, 0.0).T
    out_ref[pl.ds(rows, STAT_ROWS), pl.ds(0, wide)] = packed[:STAT_ROWS].astype(jnp.bfloat16)
    if wide < WIDTH:
        out_ref[pl.ds(rows, STAT_ROWS), pl.ds(wide, WIDTH - wide)] = jnp.zeros(
            (STAT_ROWS, WIDTH - wide), jnp.bfloat16
        )


def merge(old, new):
    best = jnp.maximum(old, new)
    old_part = jnp.exp2(old - best)
    new_part = jnp.exp2(new - best)
    both = old_part + new_part
    scale = 1.0 / both
    return old_part * scale, new_part * scale, best + jnp.log2(both)


def attend(q_ref, q_row, block, out_ref, stat_ref, row):
    at = pl.ds(row, SPAN)
    lane = lax.broadcasted_iota(jnp.int32, (SPAN, LANES), 1)
    queries = q_ref[pl.ds(q_row, SPAN), :]
    old = out_ref[at, :].astype(jnp.float32)
    old_lse = stat_ref[at, :]
    heads = [slice(head * HEAD_DIM, (head + 1) * HEAD_DIM) for head in range(HEADS)]
    scores = [
        lax.dot_general(
            queries[:, cols], block[:, cols], (((1,), (1,)), ((), ())),
            preferred_element_type=jnp.float32,
        )
        for cols in heads
    ]
    peaks = [jnp.max(score, axis=-1, keepdims=True) for score in scores]
    weights = [jnp.exp2((score - peak) * SCALE) for score, peak in zip(scores, peaks)]
    totals = [jnp.sum(weight, axis=-1, keepdims=True) for weight in weights]
    mixed = [
        jnp.dot(
            weight.astype(jnp.bfloat16),
            block[:, WIDTH + cols.start : WIDTH + cols.stop],
            preferred_element_type=jnp.float32,
        )
        for weight, cols in zip(weights, heads)
    ]
    peak_tile = jnp.zeros((SPAN, LANES), jnp.float32)
    total_tile = jnp.ones((SPAN, LANES), jnp.float32)
    for head in range(HEADS):
        peak_tile = jnp.where(lane == head, peaks[head], peak_tile)
        total_tile = jnp.where(lane == head, totals[head], total_tile)
    old_weight, new_weight, lse = merge(old_lse, peak_tile * SCALE + jnp.log2(total_tile))
    new_weight = new_weight / total_tile
    outs = [
        old[:, cols] * old_weight[:, head : head + 1] + mixed[head] * new_weight[:, head : head + 1]
        for head, cols in enumerate(heads)
    ]
    stat_ref[at, :] = lse
    for cols, out in zip(heads, outs):
        out_ref[at, cols] = out.astype(jnp.bfloat16)


def start_blocks(ids_ref, base, spans, kv_ref, buf_ref, sems, slot0):
    def one(i, carry):
        block = ids_ref[base + i]

        @pl.when(block >= 0)
        def _():
            pltpu.make_async_copy(
                kv_ref.at[block], buf_ref.at[slot0 + i], sems.at[slot0 + i]
            ).start()

        return carry

    lax.fori_loop(0, spans * NBR, one, 0)


def attend_blocks(ids_ref, base, spans, q_ref, kv_ref, buf_ref, sems, slot0, out_ref, stat_ref):
    def one(i, carry):
        block = ids_ref[base + i]

        @pl.when(block >= 0)
        def _():
            pltpu.make_async_copy(
                kv_ref.at[0], buf_ref.at[slot0 + i], sems.at[slot0 + i]
            ).wait()
            row = pl.multiple_of((i // NBR) * SPAN, SPAN)
            attend(q_ref, row, buf_ref.at[slot0 + i], out_ref, stat_ref, row)

        return carry

    lax.fori_loop(0, spans * NBR, one, 0)


def relay_kernel(ways, *refs):
    ids_ref, kv_ref = refs[:2]
    refs = refs[2:]
    plan = []
    for base, spans, begin, held in ways:
        q_ref, refs = refs[0], refs[1:]
        state_ref = None
        if held:
            state_ref, refs = refs[0], refs[1:]
        plan.append([base, spans, begin, held, q_ref, state_ref])
    outs, refs = refs[: len(ways)], refs[len(ways) :]
    buf_ref, sems = refs[:2]
    stats = refs[2:]
    slot0 = 0
    for base, spans, *_ in plan:
        start_blocks(ids_ref, base, spans, kv_ref, buf_ref, sems, slot0)
        slot0 += spans * NBR
    slot0 = 0
    for (base, spans, begin, held, q_ref, state_ref), out_ref, stat_ref in zip(plan, outs, stats):
        rows = spans * SPAN
        if held != spans:
            out_ref[pl.ds(0, rows), :] = jnp.zeros((rows, WIDTH), jnp.bfloat16)
            stat_ref[...] = jnp.full((rows, LANES), FAR, jnp.float32)
        if held:
            load_state(state_ref, out_ref, stat_ref, begin * SPAN, held * SPAN)
        attend_blocks(
            ids_ref, base, spans, q_ref, kv_ref, buf_ref, sems, slot0, out_ref, stat_ref
        )
        store_stats(stat_ref, out_ref, rows)
        slot0 += spans * NBR


def final_kernel(base, spans, mask_base, ids_ref, edge_ref, kv_ref, *refs):
    q_ref, state_ref, out_ref, buf_ref, sems, stat_ref = refs
    rows = spans * SPAN
    start_blocks(ids_ref, base, spans, kv_ref, buf_ref, sems, 0)
    load_state(state_ref, out_ref, stat_ref, 0, rows)
    attend_blocks(ids_ref, base, spans, q_ref, kv_ref, buf_ref, sems, 0, out_ref, stat_ref)

    def cut(i, carry):
        @pl.when(edge_ref[mask_base + i] > 0)
        def _():
            at = pl.ds(pl.multiple_of(i * SPAN, SPAN), SPAN)
            kept = lax.broadcasted_iota(jnp.int32, (SPAN, WIDTH), 0) == 0
            out_ref[at, :] = jnp.where(kept, out_ref[at, :], jnp.zeros((SPAN, WIDTH), jnp.bfloat16))

        return carry

    lax.fori_loop(0, spans, cut, 0)


SMEM = pl.BlockSpec(memory_space=pltpu.SMEM)
VMEM = pl.BlockSpec(memory_space=pltpu.VMEM)
HBM = pl.BlockSpec(memory_space=pltpu.HBM)


def cost(pairs, rows):
    return pl.CostEstimate(
        flops=pairs * HEADS * 4 * SPAN * HEAD_DIM * NBR_LEN,
        bytes_accessed=pairs * NBR_LEN * 4 * WIDTH + rows * WIDTH * 8,
        transcendentals=pairs * HEADS * SPAN * NBR_LEN,
    )


def relay(ids, kv, ways):
    specs = [w[:4] for w in ways]
    operands = [ids, kv]
    for base, spans, begin, held, queries, state in ways:
        operands.append(queries)
        if held:
            operands.append(state)
    total = sum(spans for _, spans, _, _ in specs)
    return pl.pallas_call(
        functools.partial(relay_kernel, specs),
        out_shape=[
            jax.ShapeDtypeStruct((spans * SPAN + STAT_ROWS, WIDTH), jnp.bfloat16)
            for _, spans, _, _ in specs
        ],
        in_specs=[SMEM, HBM] + [VMEM] * (len(operands) - 2),
        out_specs=[VMEM] * len(specs),
        scratch_shapes=[
            pltpu.VMEM((total * NBR, NBR_LEN, 2 * WIDTH), jnp.bfloat16),
            pltpu.SemaphoreType.DMA((total * NBR,)),
        ]
        + [pltpu.VMEM((spans * SPAN, LANES), jnp.float32) for _, spans, _, _ in specs],
        compiler_params=pltpu.CompilerParams(vmem_limit_bytes=12 * 1024 * 1024),
        cost_estimate=cost(3, total * SPAN),
    )(*operands)


def finish(ids, edges, kv, base, spans, mask_base, queries, state):
    rows = spans * SPAN
    return pl.pallas_call(
        functools.partial(final_kernel, base, spans, mask_base),
        out_shape=jax.ShapeDtypeStruct((rows, WIDTH), jnp.bfloat16),
        in_specs=[SMEM, SMEM, HBM] + [VMEM] * 2,
        out_specs=VMEM,
        scratch_shapes=[
            pltpu.VMEM((spans * NBR, NBR_LEN, 2 * WIDTH), jnp.bfloat16),
            pltpu.SemaphoreType.DMA((spans * NBR,)),
            pltpu.VMEM((rows, LANES), jnp.float32),
        ],
        compiler_params=pltpu.CompilerParams(vmem_limit_bytes=12 * 1024 * 1024),
        cost_estimate=cost(3, rows),
    )(ids, edges, kv, queries, state)


def block_copies(place_ref, first, count, weight_ref, buf_ref, sems):
    copies = []
    for i in range(first, first + count):
        block = pl.ds(pl.multiple_of(place_ref[i] * WIDTH, WIDTH), WIDTH)
        copy = pltpu.make_async_copy(weight_ref.at[block], buf_ref.at[i - first], sems.at[i])
        copy.start()
        copies.append(copy)
    return copies


def add_pieces(pieces, buf_ref, total, copies=()):
    for i, piece_ref in enumerate(pieces):
        if copies:
            copies[i].wait()
        term = jnp.dot(piece_ref[...], buf_ref[i], preferred_element_type=jnp.float32)
        total = term if total is None else total + term
    return total


def add_squares(pieces):
    squares = None
    for piece_ref in pieces:
        for k in range(HEADS):
            wide = piece_ref[:, k * LANES : (k + 1) * LANES].astype(jnp.float32)
            squares = wide * wide if squares is None else squares + wide * wide
    return squares


def query_kernel(place_ref, weight_ref, *refs):
    pieces, (out_ref, buf_ref, sems) = refs[:ALL], refs[ALL:]
    copies = block_copies(place_ref, 0, ALL, weight_ref, buf_ref, sems)
    squares = jnp.sum(add_squares(pieces), axis=-1, keepdims=True)
    total = add_pieces(pieces, buf_ref, None, copies)
    total = total * lax.rsqrt(squares * (1.0 / (WIDTH * ALL)) + 1e-05)
    out_ref[...] = total.astype(jnp.bfloat16)


def early_kernel(place_ref, weight_ref, *refs):
    pieces, refs = refs[:EARLY], refs[EARLY:]
    residual_ref, late_ref, total_ref, buf_ref, sems = refs
    copies = block_copies(place_ref, 0, EARLY, weight_ref, buf_ref, sems)
    late_copies = block_copies(place_ref, EARLY, ALL - EARLY, weight_ref, late_ref, sems)
    total_ref[...] = add_pieces(pieces, buf_ref, residual_ref[...].astype(jnp.float32), copies)
    for copy in late_copies:
        copy.wait()


def late_kernel(late_ref, *refs):
    pieces, (total_ref, out_ref) = refs[: ALL - EARLY], refs[ALL - EARLY :]
    out_ref[...] = add_pieces(pieces, late_ref, total_ref[...]).astype(jnp.bfloat16)


def gathered_cost(rows, count):
    return pl.CostEstimate(
        flops=2 * rows * WIDTH * WIDTH * count,
        bytes_accessed=2 * WIDTH * (rows + WIDTH) * count + 4 * rows * WIDTH,
        transcendentals=0,
    )


def in_order(pieces):
    return [pieces[r + other] for r in range(NX) for other in (0, NX)]


PARAMS = pltpu.CompilerParams(vmem_limit_bytes=14 * 1024 * 1024)


def project_queries(place, pieces, weight):
    rows = pieces[0].shape[0]
    return pl.pallas_call(
        query_kernel,
        out_shape=jax.ShapeDtypeStruct((rows, WIDTH), jnp.bfloat16),
        in_specs=[SMEM, HBM] + [VMEM] * ALL,
        out_specs=VMEM,
        scratch_shapes=[
            pltpu.VMEM((ALL, WIDTH, WIDTH), jnp.bfloat16),
            pltpu.SemaphoreType.DMA((ALL,)),
        ],
        compiler_params=PARAMS,
        cost_estimate=gathered_cost(rows, ALL),
    )(place, pltpu.with_memory_space_constraint(weight, pltpu.HBM), *in_order(pieces))


def project_out(place, pieces, weight, residual):
    rows = residual.shape[0]
    pieces = in_order(pieces)
    late, total = pl.pallas_call(
        early_kernel,
        out_shape=[
            jax.ShapeDtypeStruct((ALL - EARLY, WIDTH, WIDTH), jnp.bfloat16),
            jax.ShapeDtypeStruct((rows, WIDTH), jnp.float32),
        ],
        in_specs=[SMEM, HBM] + [VMEM] * (EARLY + 1),
        out_specs=[VMEM] * 2,
        scratch_shapes=[
            pltpu.VMEM((EARLY, WIDTH, WIDTH), jnp.bfloat16),
            pltpu.SemaphoreType.DMA((ALL,)),
        ],
        compiler_params=PARAMS,
        cost_estimate=gathered_cost(rows, EARLY),
    )(place, pltpu.with_memory_space_constraint(weight, pltpu.HBM), *pieces[:EARLY], residual)
    return pl.pallas_call(
        late_kernel,
        out_shape=jax.ShapeDtypeStruct((rows, WIDTH), jnp.bfloat16),
        in_specs=[VMEM] * (ALL - EARLY + 2),
        out_specs=VMEM,
        compiler_params=PARAMS,
        cost_estimate=gathered_cost(rows, ALL - EARLY),
    )(late, *pieces[EARLY:], total)


def gather_pieces(own, before=((), (), ()), last=()):
    up = [(2 * x, 2 * ((x + 1) % NX)) for x in range(NX)]
    down = [(2 * x + 1, 2 * ((x - 1) % NX) + 1) for x in range(NX)]
    swap = [(i, i ^ 1) for i in range(NX * NC)]
    held = [own]
    for after in before:
        held.append(lax.ppermute(tie(held[-1], *after), STORE, up + down))
    others = [lax.ppermute(piece, STORE, swap) for piece in held[:-1]]
    return held + others + [lax.ppermute(tie(held[-1], *last), STORE, swap)]


def piece_places():
    x, core = lax.axis_index("x"), lax.axis_index("core")
    step = 1 - 2 * core
    away = jnp.arange(NX, dtype=jnp.int32) * step
    mine = ((x - away) % NX) * NC + core
    others = ((x + away) % NX) * NC + 1 - core
    return jnp.stack([mine, others], axis=1).reshape(-1).astype(jnp.int32)


def column_kernel(w_ref, out_ref):
    out_ref[...] = w_ref[...]


def column_blocks(weight):
    return pl.pallas_call(
        column_kernel,
        out_shape=jax.ShapeDtypeStruct((NX * NC * WIDTH, WIDTH), weight.dtype),
        grid=(NX * NC,),
        in_specs=[pl.BlockSpec((WIDTH, WIDTH), lambda k: (0, k))],
        out_specs=pl.BlockSpec((WIDTH, WIDTH), lambda k: (k, 0)),
        compiler_params=pltpu.CompilerParams(vmem_limit_bytes=4 * 1024 * 1024),
        cost_estimate=pl.CostEstimate(
            flops=0, bytes_accessed=4 * NX * NC * WIDTH * WIDTH, transcendentals=0
        ),
    )(weight)


def tie(array, *after):
    return lax.optimization_barrier((array, *after))[0]


def tie_all(arrays, *after):
    return list(lax.optimization_barrier((*arrays, *after))[: len(arrays)])


def on_device(hidden, nbr_shard, nbr_block, seq_lengths, kv_store, w_query, w_out):
    rows = hidden.shape[0]
    my_y, my_z = lax.axis_index("y"), lax.axis_index("z")
    seq_at = my_y * NZ + my_z
    order = [(i, i - 1) for i in range(1, NY * NZ)]
    edge = lax.ppermute(hidden[: SPAN - 1], SEQ, order)
    attending = jnp.concatenate([hidden[SPAN - 1 :], edge], axis=0)
    place = piece_places()

    wanted = (nbr_shard * BLK_DEV + nbr_block).reshape(-1)
    for by in (1, 2, 4):
        wanted = jnp.concatenate([wanted, ring(wanted, "z", NZ, -by)])
    shard, block = wanted // BLK_DEV, wanted % BLK_DEV
    local = jnp.where(shard % NZ == my_z, shard // NZ * BLK_DEV + block, -1).astype(jnp.int32)
    local = local.reshape(NZ, SPANS_DEV * NBR)
    turned = jnp.concatenate([local[:1], local[:0:-1]], axis=0)
    local = jnp.where(lax.axis_index("core") == 0, turned, local).reshape(-1)
    span_index = seq_at * SPANS_DEV + jnp.arange(SPANS_DEV, dtype=jnp.int32)
    upto = jnp.arange(seq_lengths.shape[0])
    seq_ends = jnp.sum(jnp.where(upto[None, :] <= upto[:, None], seq_lengths[None, :], 0), axis=1)
    boundary = jnp.any(seq_ends[None, :] == span_index[:, None] + 1, axis=1)
    boundary = boundary.astype(jnp.int32)

    parts = [attending[first * SPAN : last * SPAN] for first, last in CHUNKS]

    columns = column_blocks(w_out)
    before = [[(), (), (local, boundary, columns)], ((), (), ())]
    pieces = [gather_pieces(part, when) for part, when in zip(parts, before)]

    own = tie(kv_store, parts[1]).reshape(BLK_DEV, NBR_LEN, 2 * WIDTH)
    kv = lax.all_gather(own, "y", axis=0, tiled=True)
    kv = pltpu.with_memory_space_constraint(kv, pltpu.HBM)

    queries = [project_queries(place, piece, w_query) for piece in pieces]
    columns = tie(columns, *queries)
    w_cols = lax.all_to_all(columns, STORE, split_axis=0, concat_axis=0, tiled=True)
    held = [[q] for q in queries]
    count = len(CHUNKS)
    for _ in range(NZ - 1):
        for c in range(count):
            held[c].append(turn(held[c][-1]))

    state, sent, attended = [None] * count, (), [None] * count
    for c, s in ORDER:
        first, last = CHUNKS[c]
        spans = last - first
        base = (s * SPANS_DEV + first) * NBR
        queries_of, after = held[c][s], [*sent]
        if (c, s) == (0, 0):
            after.append(w_cols)
        if s == 1:
            queries_of = tie(queries_of, held[c][AHEAD], *after)
        else:
            state[c] = tie(state[c], *after)
        if s == 0:
            sent = [finish(local, boundary, kv, base, spans, first, queries_of, state[c])]
            attended[c] = sent[0]
            continue
        sent = relay(local, kv, [(base, spans, 0, 0 if s == 1 else spans, queries_of, state[c])])
        state[c] = turn(sent[0])

    tail = rows - (CHUNKS[0][0] * SPAN + SPAN - 1)
    order = [(i, i + 1) for i in range(NY * NZ - 1)]
    head = tie(lax.ppermute(attended[0][tail:], SEQ, order), attended[1])
    attended[0] = jnp.concatenate([head, attended[0][:tail]], axis=0)
    residual = jnp.concatenate([hidden[: SPAN - 1], hidden[rows - tail :]], axis=0)
    middle = project_out(place, gather_pieces(attended[1]), w_cols, parts[1])
    ends = project_out(place, gather_pieces(attended[0], last=(middle,)), w_cols, residual)
    return jnp.concatenate([ends[: SPAN - 1], middle, ends[SPAN - 1 :]], axis=0)


def solution(mesh):
    fine = Mesh(mesh.devices.reshape(NY, NZ, NX, NC), ("y", "z", "x", "core"))
    return jax.shard_map(
        on_device,
        mesh=fine,
        in_specs=(
            P(SEQ, STORE),
            P(SEQ, None),
            P(SEQ, None),
            P(),
            P(SEQ, None, None, STORE),
            P(None, STORE),
            P(STORE, None),
        ),
        out_specs=P(SEQ, STORE),
        check_vma=False,
    )
```

```python
import functools
import jax
import jax.numpy as jnp
from jax import lax
from jax.experimental import pallas as pl
from jax.experimental.pallas import tpu as pltpu
from jax.sharding import Mesh, PartitionSpec as P

HEAD_DIM = 128
SPAN = 64
NBR = 2
NBR_LEN = 128
HEADS = 4
WIDTH = HEADS * HEAD_DIM
BLK_DEV = 8
NY, NZ, NX, NC = 4, 8, 4, 2
SEQ, STORE = ("y", "z"), ("x", "core")
ALL, EARLY = NX * NC, NX * NC - 2
SPANS_DEV = 12
CHUNKS = ((6, 12), (0, 6))
ORDER = tuple((c, s) for s in (4, 3, 2, 1, 0) for c in (0, 1))
STAT_ROWS = 16
FAR = -1e30
SCALE = HEAD_DIM**-0.5 * 1.4426950408889634
LANES = 128


def ring(array, axis, size, by):
    return lax.ppermute(array, axis, [(i, (i + by) % size) for i in range(size)])


def lane_rows(rows):
    return -(-rows // LANES) * LANES


def load_state(state_ref, out_ref, stat_ref, first, rows):
    out_ref[pl.ds(first, rows), :] = state_ref[pl.ds(0, rows), :]
    wide = lane_rows(rows)
    packed = state_ref[pl.ds(rows, STAT_ROWS), pl.ds(0, wide)].astype(jnp.float32)
    parts = jnp.concatenate([packed, jnp.zeros((LANES - STAT_ROWS, wide), jnp.float32)], axis=0).T
    total = parts + pltpu.roll(parts, LANES - HEADS, 1) + pltpu.roll(parts, LANES - 2 * HEADS, 1)
    stat_ref[pl.ds(first, rows), :] = total[:rows]


def store_stats(stat_ref, out_ref, rows):
    wide = lane_rows(rows)
    lse = stat_ref[pl.ds(0, rows), :]
    if wide != rows:
        lse = jnp.concatenate([lse, jnp.zeros((wide - rows, LANES), jnp.float32)], axis=0)
    high = lse.astype(jnp.bfloat16).astype(jnp.float32)
    rest = lse - high
    middle = rest.astype(jnp.bfloat16).astype(jnp.float32)
    low = rest - middle
    lane = lax.broadcasted_iota(jnp.int32, lse.shape, 1)
    packed = jnp.where(
        lane < HEADS,
        high,
        jnp.where(lane < 2 * HEADS, pltpu.roll(middle, HEADS, 1), pltpu.roll(low, 2 * HEADS, 1)),
    )
    packed = jnp.where(lane < 3 * HEADS, packed, 0.0).T
    out_ref[pl.ds(rows, STAT_ROWS), pl.ds(0, wide)] = packed[:STAT_ROWS].astype(jnp.bfloat16)
    if wide < WIDTH:
        out_ref[pl.ds(rows, STAT_ROWS), pl.ds(wide, WIDTH - wide)] = jnp.zeros(
            (STAT_ROWS, WIDTH - wide), jnp.bfloat16
        )


def merge(old, new):
    best = jnp.maximum(old, new)
    old_part = jnp.exp2(old - best)
    new_part = jnp.exp2(new - best)
    both = old_part + new_part
    scale = 1.0 / both
    return old_part * scale, new_part * scale, best + jnp.log2(both)


def attend(q_ref, q_row, block, out_ref, stat_ref, row):
    at = pl.ds(row, SPAN)
    lane = lax.broadcasted_iota(jnp.int32, (SPAN, LANES), 1)
    queries = q_ref[pl.ds(q_row, SPAN), :]
    old = out_ref[at, :].astype(jnp.float32)
    old_lse = stat_ref[at, :]
    heads = [slice(head * HEAD_DIM, (head + 1) * HEAD_DIM) for head in range(HEADS)]
    scores = [
        lax.dot_general(
            queries[:, cols], block[:, cols], (((1,), (1,)), ((), ())),
            preferred_element_type=jnp.float32,
        )
        for cols in heads
    ]
    peaks = [jnp.max(score, axis=-1, keepdims=True) for score in scores]
    weights = [jnp.exp2((score - peak) * SCALE) for score, peak in zip(scores, peaks)]
    totals = [jnp.sum(weight, axis=-1, keepdims=True) for weight in weights]
    mixed = [
        jnp.dot(
            weight.astype(jnp.bfloat16),
            block[:, WIDTH + cols.start : WIDTH + cols.stop],
            preferred_element_type=jnp.float32,
        )
        for weight, cols in zip(weights, heads)
    ]
    peak_tile = jnp.zeros((SPAN, LANES), jnp.float32)
    total_tile = jnp.ones((SPAN, LANES), jnp.float32)
    for head in range(HEADS):
        peak_tile = jnp.where(lane == head, peaks[head], peak_tile)
        total_tile = jnp.where(lane == head, totals[head], total_tile)
    old_weight, new_weight, lse = merge(old_lse, peak_tile * SCALE + jnp.log2(total_tile))
    new_weight = new_weight / total_tile
    outs = [
        old[:, cols] * old_weight[:, head : head + 1] + mixed[head] * new_weight[:, head : head + 1]
        for head, cols in enumerate(heads)
    ]
    stat_ref[at, :] = lse
    for cols, out in zip(heads, outs):
        out_ref[at, cols] = out.astype(jnp.bfloat16)


def start_blocks(ids_ref, base, spans, kv_ref, buf_ref, sems, slot0):
    def one(i, carry):
        block = ids_ref[base + i]

        @pl.when(block >= 0)
        def _():
            pltpu.make_async_copy(
                kv_ref.at[block], buf_ref.at[slot0 + i], sems.at[slot0 + i]
            ).start()

        return carry

    lax.fori_loop(0, spans * NBR, one, 0)


def attend_blocks(ids_ref, base, spans, q_ref, kv_ref, buf_ref, sems, slot0, out_ref, stat_ref):
    def one(i, carry):
        block = ids_ref[base + i]

        @pl.when(block >= 0)
        def _():
            pltpu.make_async_copy(
                kv_ref.at[0], buf_ref.at[slot0 + i], sems.at[slot0 + i]
            ).wait()
            row = pl.multiple_of((i // NBR) * SPAN, SPAN)
            attend(q_ref, row, buf_ref.at[slot0 + i], out_ref, stat_ref, row)

        return carry

    lax.fori_loop(0, spans * NBR, one, 0)


def relay_kernel(ways, *refs):
    ids_ref, kv_ref = refs[:2]
    refs = refs[2:]
    plan = []
    for base, spans, begin, held in ways:
        q_ref, refs = refs[0], refs[1:]
        state_ref = None
        if held:
            state_ref, refs = refs[0], refs[1:]
        plan.append([base, spans, begin, held, q_ref, state_ref])
    outs, refs = refs[: len(ways)], refs[len(ways) :]
    buf_ref, sems = refs[:2]
    stats = refs[2:]
    slot0 = 0
    for base, spans, *_ in plan:
        start_blocks(ids_ref, base, spans, kv_ref, buf_ref, sems, slot0)
        slot0 += spans * NBR
    slot0 = 0
    for (base, spans, begin, held, q_ref, state_ref), out_ref, stat_ref in zip(plan, outs, stats):
        rows = spans * SPAN
        if held != spans:
            out_ref[pl.ds(0, rows), :] = jnp.zeros((rows, WIDTH), jnp.bfloat16)
            stat_ref[...] = jnp.full((rows, LANES), FAR, jnp.float32)
        if held:
            load_state(state_ref, out_ref, stat_ref, begin * SPAN, held * SPAN)
        attend_blocks(
            ids_ref, base, spans, q_ref, kv_ref, buf_ref, sems, slot0, out_ref, stat_ref
        )
        store_stats(stat_ref, out_ref, rows)
        slot0 += spans * NBR


def final_kernel(base, spans, mask_base, ids_ref, edge_ref, kv_ref, *refs):
    q_ref, fwd_ref, bwd_ref, out_ref, buf_ref, sems, stat_ref, other_ref, other_stat = refs
    rows = spans * SPAN
    start_blocks(ids_ref, base, spans, kv_ref, buf_ref, sems, 0)
    load_state(fwd_ref, out_ref, stat_ref, 0, rows)
    load_state(bwd_ref, other_ref, other_stat, 0, rows)
    weight, other_weight, lse = merge(stat_ref[...], other_stat[...])
    stat_ref[...] = lse
    for head in range(HEADS):
        cols = slice(head * HEAD_DIM, (head + 1) * HEAD_DIM)
        out_ref[:, cols] = (
            out_ref[:, cols].astype(jnp.float32) * weight[:, head : head + 1]
            + other_ref[:, cols].astype(jnp.float32) * other_weight[:, head : head + 1]
        ).astype(jnp.bfloat16)
    attend_blocks(ids_ref, base, spans, q_ref, kv_ref, buf_ref, sems, 0, out_ref, stat_ref)

    def cut(i, carry):
        @pl.when(edge_ref[mask_base + i] > 0)
        def _():
            at = pl.ds(pl.multiple_of(i * SPAN, SPAN), SPAN)
            kept = lax.broadcasted_iota(jnp.int32, (SPAN, WIDTH), 0) == 0
            out_ref[at, :] = jnp.where(kept, out_ref[at, :], jnp.zeros((SPAN, WIDTH), jnp.bfloat16))

        return carry

    lax.fori_loop(0, spans, cut, 0)


SMEM = pl.BlockSpec(memory_space=pltpu.SMEM)
VMEM = pl.BlockSpec(memory_space=pltpu.VMEM)
HBM = pl.BlockSpec(memory_space=pltpu.HBM)


def cost(pairs, rows):
    return pl.CostEstimate(
        flops=pairs * HEADS * 4 * SPAN * HEAD_DIM * NBR_LEN,
        bytes_accessed=pairs * NBR_LEN * 4 * WIDTH + rows * WIDTH * 8,
        transcendentals=pairs * HEADS * SPAN * NBR_LEN,
    )


def relay(ids, kv, ways):
    specs = [w[:4] for w in ways]
    operands = [ids, kv]
    for base, spans, begin, held, queries, state in ways:
        operands.append(queries)
        if held:
            operands.append(state)
    total = sum(spans for _, spans, _, _ in specs)
    return pl.pallas_call(
        functools.partial(relay_kernel, specs),
        out_shape=[
            jax.ShapeDtypeStruct((spans * SPAN + STAT_ROWS, WIDTH), jnp.bfloat16)
            for _, spans, _, _ in specs
        ],
        in_specs=[SMEM, HBM] + [VMEM] * (len(operands) - 2),
        out_specs=[VMEM] * len(specs),
        scratch_shapes=[
            pltpu.VMEM((total * NBR, NBR_LEN, 2 * WIDTH), jnp.bfloat16),
            pltpu.SemaphoreType.DMA((total * NBR,)),
        ]
        + [pltpu.VMEM((spans * SPAN, LANES), jnp.float32) for _, spans, _, _ in specs],
        compiler_params=pltpu.CompilerParams(vmem_limit_bytes=12 * 1024 * 1024),
        cost_estimate=cost(6, total * SPAN),
    )(*operands)


def finish(ids, edges, kv, base, spans, mask_base, queries, fwd, bwd):
    rows = spans * SPAN
    return pl.pallas_call(
        functools.partial(final_kernel, base, spans, mask_base),
        out_shape=jax.ShapeDtypeStruct((rows, WIDTH), jnp.bfloat16),
        in_specs=[SMEM, SMEM, HBM] + [VMEM] * 3,
        out_specs=VMEM,
        scratch_shapes=[
            pltpu.VMEM((spans * NBR, NBR_LEN, 2 * WIDTH), jnp.bfloat16),
            pltpu.SemaphoreType.DMA((spans * NBR,)),
            pltpu.VMEM((rows, LANES), jnp.float32),
            pltpu.VMEM((rows, WIDTH), jnp.bfloat16),
            pltpu.VMEM((rows, LANES), jnp.float32),
        ],
        compiler_params=pltpu.CompilerParams(vmem_limit_bytes=12 * 1024 * 1024),
        cost_estimate=cost(3, rows),
    )(ids, edges, kv, queries, fwd, bwd)


def block_copies(place_ref, first, count, weight_ref, buf_ref, sems):
    copies = []
    for i in range(first, first + count):
        block = pl.ds(pl.multiple_of(place_ref[i] * WIDTH, WIDTH), WIDTH)
        copy = pltpu.make_async_copy(weight_ref.at[block], buf_ref.at[i - first], sems.at[i])
        copy.start()
        copies.append(copy)
    return copies


def add_pieces(pieces, buf_ref, total, copies=()):
    for i, piece_ref in enumerate(pieces):
        if copies:
            copies[i].wait()
        term = jnp.dot(piece_ref[...], buf_ref[i], preferred_element_type=jnp.float32)
        total = term if total is None else total + term
    return total


def add_squares(pieces):
    squares = None
    for piece_ref in pieces:
        for k in range(HEADS):
            wide = piece_ref[:, k * LANES : (k + 1) * LANES].astype(jnp.float32)
            squares = wide * wide if squares is None else squares + wide * wide
    return squares


def query_kernel(place_ref, weight_ref, *refs):
    pieces, (out_ref, buf_ref, sems) = refs[:ALL], refs[ALL:]
    copies = block_copies(place_ref, 0, ALL, weight_ref, buf_ref, sems)
    squares = jnp.sum(add_squares(pieces), axis=-1, keepdims=True)
    total = add_pieces(pieces, buf_ref, None, copies)
    total = total * lax.rsqrt(squares * (1.0 / (WIDTH * ALL)) + 1e-05)
    out_ref[...] = total.astype(jnp.bfloat16)


def early_kernel(place_ref, weight_ref, *refs):
    pieces, refs = refs[:EARLY], refs[EARLY:]
    residual_ref, late_ref, total_ref, buf_ref, sems = refs
    copies = block_copies(place_ref, 0, EARLY, weight_ref, buf_ref, sems)
    late_copies = block_copies(place_ref, EARLY, ALL - EARLY, weight_ref, late_ref, sems)
    total_ref[...] = add_pieces(pieces, buf_ref, residual_ref[...].astype(jnp.float32), copies)
    for copy in late_copies:
        copy.wait()


def late_kernel(late_ref, *refs):
    pieces, (total_ref, out_ref) = refs[: ALL - EARLY], refs[ALL - EARLY :]
    out_ref[...] = add_pieces(pieces, late_ref, total_ref[...]).astype(jnp.bfloat16)


def gathered_cost(rows, count):
    return pl.CostEstimate(
        flops=2 * rows * WIDTH * WIDTH * count,
        bytes_accessed=2 * WIDTH * (rows + WIDTH) * count + 4 * rows * WIDTH,
        transcendentals=0,
    )


def in_order(pieces):
    return [pieces[r + other] for r in range(NX) for other in (0, NX)]


PARAMS = pltpu.CompilerParams(vmem_limit_bytes=14 * 1024 * 1024)


def project_queries(place, pieces, weight):
    rows = pieces[0].shape[0]
    return pl.pallas_call(
        query_kernel,
        out_shape=jax.ShapeDtypeStruct((rows, WIDTH), jnp.bfloat16),
        in_specs=[SMEM, HBM] + [VMEM] * ALL,
        out_specs=VMEM,
        scratch_shapes=[
            pltpu.VMEM((ALL, WIDTH, WIDTH), jnp.bfloat16),
            pltpu.SemaphoreType.DMA((ALL,)),
        ],
        compiler_params=PARAMS,
        cost_estimate=gathered_cost(rows, ALL),
    )(place, pltpu.with_memory_space_constraint(weight, pltpu.HBM), *in_order(pieces))


def project_out(place, pieces, weight, residual):
    rows = residual.shape[0]
    pieces = in_order(pieces)
    late, total = pl.pallas_call(
        early_kernel,
        out_shape=[
            jax.ShapeDtypeStruct((ALL - EARLY, WIDTH, WIDTH), jnp.bfloat16),
            jax.ShapeDtypeStruct((rows, WIDTH), jnp.float32),
        ],
        in_specs=[SMEM, HBM] + [VMEM] * (EARLY + 1),
        out_specs=[VMEM] * 2,
        scratch_shapes=[
            pltpu.VMEM((EARLY, WIDTH, WIDTH), jnp.bfloat16),
            pltpu.SemaphoreType.DMA((ALL,)),
        ],
        compiler_params=PARAMS,
        cost_estimate=gathered_cost(rows, EARLY),
    )(place, pltpu.with_memory_space_constraint(weight, pltpu.HBM), *pieces[:EARLY], residual)
    return pl.pallas_call(
        late_kernel,
        out_shape=jax.ShapeDtypeStruct((rows, WIDTH), jnp.bfloat16),
        in_specs=[VMEM] * (ALL - EARLY + 2),
        out_specs=VMEM,
        compiler_params=PARAMS,
        cost_estimate=gathered_cost(rows, ALL - EARLY),
    )(late, *pieces[EARLY:], total)


def swap(array):
    return lax.ppermute(array, STORE, [(i, i ^ 1) for i in range(NX * NC)])


def gather_pieces(own, before=((), (), ()), last=()):
    up = [(2 * x, 2 * ((x + 1) % NX)) for x in range(NX)]
    down = [(2 * x + 1, 2 * ((x - 1) % NX) + 1) for x in range(NX)]
    held = [own]
    for after in before:
        held.append(lax.ppermute(tie(held[-1], *after), STORE, up + down))
    return held + [swap(piece) for piece in held[:-1]] + [swap(tie(held[-1], *last))]


def piece_places():
    x, core = lax.axis_index("x"), lax.axis_index("core")
    step = 1 - 2 * core
    away = jnp.arange(NX, dtype=jnp.int32) * step
    mine = ((x - away) % NX) * NC + core
    others = ((x + away) % NX) * NC + 1 - core
    return jnp.stack([mine, others], axis=1).reshape(-1).astype(jnp.int32)


def column_kernel(w_ref, out_ref):
    out_ref[...] = w_ref[...]


def column_blocks(weight):
    return pl.pallas_call(
        column_kernel,
        out_shape=jax.ShapeDtypeStruct((NX * NC * WIDTH, WIDTH), weight.dtype),
        grid=(NX * NC,),
        in_specs=[pl.BlockSpec((WIDTH, WIDTH), lambda k: (0, k))],
        out_specs=pl.BlockSpec((WIDTH, WIDTH), lambda k: (k, 0)),
        compiler_params=pltpu.CompilerParams(vmem_limit_bytes=4 * 1024 * 1024),
        cost_estimate=pl.CostEstimate(
            flops=0, bytes_accessed=4 * NX * NC * WIDTH * WIDTH, transcendentals=0
        ),
    )(weight)


def tie(array, *after):
    return lax.optimization_barrier((array, *after))[0]


def tie_all(arrays, *after):
    return list(lax.optimization_barrier((*arrays, *after))[: len(arrays)])


def on_device(hidden, nbr_shard, nbr_block, seq_lengths, kv_store, w_query, w_out):
    rows = hidden.shape[0]
    my_y, my_z = lax.axis_index("y"), lax.axis_index("z")
    seq_at = my_y * NZ + my_z
    order = [(i, i - 1) for i in range(1, NY * NZ)]
    edge = lax.ppermute(hidden[: SPAN - 1], SEQ, order)
    attending = jnp.concatenate([hidden[SPAN - 1 :], edge], axis=0)
    place = piece_places()

    wanted = (nbr_shard * BLK_DEV + nbr_block).reshape(-1)
    for by in (1, 2, 4):
        wanted = jnp.concatenate([wanted, ring(wanted, "z", NZ, -by)])
    shard, block = wanted // BLK_DEV, wanted % BLK_DEV
    local = jnp.where(shard % NZ == my_z, shard // NZ * BLK_DEV + block, -1).astype(jnp.int32)
    span_index = seq_at * SPANS_DEV + jnp.arange(SPANS_DEV, dtype=jnp.int32)
    upto = jnp.arange(seq_lengths.shape[0])
    seq_ends = jnp.sum(jnp.where(upto[None, :] <= upto[:, None], seq_lengths[None, :], 0), axis=1)
    boundary = jnp.any(seq_ends[None, :] == span_index[:, None] + 1, axis=1)
    boundary = boundary.astype(jnp.int32)

    parts = [attending[first * SPAN : last * SPAN] for first, last in CHUNKS]

    columns = column_blocks(w_out)
    before = [[(), (), (local, boundary, columns)], ((), (), ())]
    pieces = [gather_pieces(part, when) for part, when in zip(parts, before)]

    own = tie(kv_store, parts[1]).reshape(BLK_DEV, NBR_LEN, 2 * WIDTH)
    kv = lax.all_gather(own, "y", axis=0, tiled=True)
    kv = pltpu.with_memory_space_constraint(kv, pltpu.HBM)

    queries = [project_queries(place, piece, w_query) for piece in pieces]
    columns = tie(columns, *queries)
    w_cols = lax.all_to_all(columns, STORE, split_axis=0, concat_axis=0, tiled=True)
    fwd, bwd = [[q] for q in queries], [[q] for q in queries]
    count = len(CHUNKS)
    for _ in range(3):
        for c in range(count):
            fwd[c].append(ring(fwd[c][-1], "z", NZ, 1))
            bwd[c].append(ring(bwd[c][-1], "z", NZ, -1))
    cuts = [(last - first) // 2 for first, last in CHUNKS]
    far = [
        (ring(fwd[c][3][: cuts[c] * SPAN], "z", NZ, 1), ring(bwd[c][3][cuts[c] * SPAN :], "z", NZ, -1))
        for c in range(count)
    ]

    state, sent, attended = [None] * count, (), [None] * count
    tail = rows - (CHUNKS[0][0] * SPAN + SPAN - 1)
    order = [(i, i + 1) for i in range(NY * NZ - 1)]
    for c, s in ORDER:
        first, last = CHUNKS[c]
        spans, split = last - first, cuts[c]

        def base(distance, start=0):
            return ((distance % NZ) * SPANS_DEV + first + start) * NBR

        after = [*sent]
        if (c, s) == (0, 0):
            after.append(w_cols)
        if (c, s) == (1, 0):
            head = lax.ppermute(attended[0][tail:], SEQ, order)
            after.append(head)
        top, low = tie_all(far[c] if s == 4 else state[c], *after)
        if s == 0:
            sent = [finish(local, boundary, kv, base(0), spans, first, queries[c], top, low)]
            attended[c] = sent[0]
            continue
        if s == 4:
            ways = [
                (base(4), split, 0, 0, top, None),
                (base(4, split), spans - split, 0, 0, low, None),
            ]
        else:
            starts, helds = ((0, split), (split, spans - split)) if s == 3 else ((0, 0), (spans, spans))
            ways = [
                (base(s), spans, starts[0], helds[0], bwd[c][s], top),
                (base(-s), spans, starts[1], helds[1], fwd[c][s], low),
            ]
        sent = relay(local, kv, ways)
        state[c] = [ring(sent[0], "z", NZ, 1), ring(sent[1], "z", NZ, -1)]

    attended[0] = jnp.concatenate([head, attended[0][:tail]], axis=0)
    residual = jnp.concatenate([hidden[: SPAN - 1], hidden[rows - tail :]], axis=0)
    pieces = gather_pieces(attended[0])
    others = gather_pieces(attended[1], [(), (pieces[1],), (pieces[2],)])
    middle = project_out(place, others, w_cols, parts[1])
    pieces[-1] = swap(tie(pieces[NX - 1], middle))
    ends = project_out(place, pieces, w_cols, residual)
    return jnp.concatenate([ends[: SPAN - 1], middle, ends[SPAN - 1 :]], axis=0)


def solution(mesh):
    fine = Mesh(mesh.devices.reshape(NY, NZ, NX, NC), ("y", "z", "x", "core"))
    return jax.shard_map(
        on_device,
        mesh=fine,
        in_specs=(
            P(SEQ, STORE),
            P(SEQ, None),
            P(SEQ, None),
            P(),
            P(SEQ, None, None, STORE),
            P(None, STORE),
            P(STORE, None),
        ),
        out_specs=P(SEQ, STORE),
        check_vma=False,
    )
```
